128 devices in a mesh: dp: 16 (over z, y), seq: 8 (over x, core).
Axes of the slice: x: 4, y: 4, z: 4, core: 2. Of those that a mesh axis runs over, the one named last changes fastest.
Arguments:
- inputs: bfloat16 [16, 1024, 1024], P('dp', 'seq'), may hold values from -6 to 6
- cotangent: bfloat16 [16, 1024, 1024], P('dp', 'seq'), may hold values from -6 to 6
- ln1_gain: bfloat16 [1024], P(('dp', 'seq')), may hold values from 0.25 to 1.75
- ln1_bias: bfloat16 [1024], P(('dp', 'seq')), may hold values from -3 to 3
- w_query: bfloat16 [1024, 1024], P(('dp', 'seq')), may hold values from -0.1875 to 0.1875
- w_key: bfloat16 [1024, 1024], P(('dp', 'seq')), may hold values from -0.1875 to 0.1875
- w_value: bfloat16 [1024, 1728], P(('dp', 'seq')), may hold values from -0.1875 to 0.1875
- w_gate: bfloat16 [1024, 1728], P(('dp', 'seq')), may hold values from -0.1875 to 0.1875
- w_out: bfloat16 [1728, 1024], P(None, ('dp', 'seq')), may hold values from -0.3125 to 0.3125
- ln2_gain: bfloat16 [1024], P(('dp', 'seq')), may hold values from 0.25 to 1.75
- ln2_bias: bfloat16 [1024], P(('dp', 'seq')), may hold values from -3 to 3
- w_mlp_gate: bfloat16 [1024, 1728], P(('dp', 'seq')), may hold values from -0.1875 to 0.1875
- w_mlp_up: bfloat16 [1024, 1728], P(('dp', 'seq')), may hold values from -0.1875 to 0.1875
- w_mlp_down: bfloat16 [1728, 1024], P(None, ('dp', 'seq')), may hold values from -0.3125 to 0.3125
Outputs:
- outputs: bfloat16 [16, 1024, 1024], P('dp', 'seq')
- grad_inputs: bfloat16 [16, 1024, 1024], P('dp', 'seq')
- grad_ln1_gain: float32 [1024], P(('dp', 'seq'))
- grad_ln1_bias: float32 [1024], P(('dp', 'seq'))
- grad_w_query: float32 [1024, 1024], P(('dp', 'seq'))
- grad_w_key: float32 [1024, 1024], P(('dp', 'seq'))
- grad_w_value: float32 [1024, 1728], P(('dp', 'seq'))
- grad_w_gate: float32 [1024, 1728], P(('dp', 'seq'))
- grad_w_out: float32 [1728, 1024], P(None, ('dp', 'seq'))
- grad_ln2_gain: float32 [1024], P(('dp', 'seq'))
- grad_ln2_bias: float32 [1024], P(('dp', 'seq'))
- grad_w_mlp_gate: float32 [1024, 1728], P(('dp', 'seq'))
- grad_w_mlp_up: float32 [1024, 1728], P(('dp', 'seq'))
- grad_w_mlp_down: float32 [1728, 1024], P(None, ('dp', 'seq'))
The draws below stay inside these ranges and needn't reach their ends.
All inputs are finite; a program needn't handle non-finite values.
Results may differ from the reference program's by a relative error of at most 0.019.
Values may be sent and summed in bfloat16 or wider, within the bound.
A program may use at most 192 MiB of HBM per device.

```python
import jax
import jax.numpy as jnp
from jax import lax

D = 1024
HEADS = 4
KHEAD = 256
VHEAD = 432
FF = 1728
LENGTH = 1024
KDIM = 1024
VDIM = 1728
SEQUENCES = 16
N_SEQ = 8


def shard_levels(stream_key, extent, split, smallest, largest):
    def one(position, parts):
        steps = jax.random.uniform(jax.random.fold_in(jax.random.fold_in(stream_key, 6), position), (parts,), jnp.float32, smallest / len(split), largest / len(split))
        return jnp.repeat(jnp.exp(steps), extent[position] // parts).reshape((-1,) + (1,) * (len(extent) - position - 1))

    level = one(*split[0])
    for cut in split[1:]:
        level = level * one(*cut)
    return level


def gaussian(key, shape, scale, bound, pieces=(), kind=jnp.bfloat16):
    loudness = shard_levels(key, shape, pieces, -0.22, 0.18) if pieces else 1.0
    array = jax.random.normal(key, shape, jnp.float32) * scale * loudness
    return jnp.minimum(jnp.maximum(array, -bound), bound).astype(kind)


def setup_inputs(seed: int = 0) -> dict:
    streams_of = jax.random.split(jax.random.key(seed), 15)
    inputs = gaussian(streams_of[0], (SEQUENCES, LENGTH, D), 1.0, 6.0, ((0, 16), (1, 8)))
    cotangent = gaussian(streams_of[1], (SEQUENCES, LENGTH, D), 1.0, 6.0, ((0, 16), (1, 8)))
    ln1_gain = jnp.clip(1.0 + 0.15 * jax.random.normal(streams_of[2], (D,), jnp.float32), 0.25, 1.75).astype(jnp.bfloat16)
    ln1_bias = gaussian(streams_of[3], (D,), 0.3, 3.0, ((0, 128),))
    w_query = gaussian(streams_of[4], (D, KDIM), D ** -0.5, 0.1875, ((0, 128),))
    w_key = gaussian(streams_of[5], (D, KDIM), D ** -0.5, 0.1875, ((0, 128),))
    w_value = gaussian(streams_of[6], (D, VDIM), D ** -0.5, 0.1875, ((0, 128),))
    w_gate = gaussian(streams_of[7], (D, VDIM), D ** -0.5, 0.1875, ((0, 128),))
    w_out = gaussian(streams_of[8], (VDIM, D), (VDIM // 4) ** -0.5, 0.3125, ((1, 128),))
    ln2_gain = jnp.clip(1.0 + 0.15 * jax.random.normal(streams_of[9], (D,), jnp.float32), 0.25, 1.75).astype(jnp.bfloat16)
    ln2_bias = gaussian(streams_of[10], (D,), 0.3, 3.0, ((0, 128),))
    w_mlp_gate = gaussian(streams_of[11], (D, FF), D ** -0.5, 0.1875, ((0, 128),))
    w_mlp_up = gaussian(streams_of[12], (D, FF), D ** -0.5, 0.1875, ((0, 128),))
    w_mlp_down = gaussian(streams_of[13], (FF, D), (FF // 4) ** -0.5, 0.3125, ((1, 128),))
    return dict(inputs=inputs, cotangent=cotangent, ln1_gain=ln1_gain, ln1_bias=ln1_bias, w_query=w_query, w_key=w_key, w_value=w_value, w_gate=w_gate, w_out=w_out, ln2_gain=ln2_gain, ln2_bias=ln2_bias, w_mlp_gate=w_mlp_gate, w_mlp_up=w_mlp_up, w_mlp_down=w_mlp_down)


highest_precision_mode = lax.Precision.HIGHEST
epsilon = 1e-05

@jax.custom_vjp
def low(v):
    return lax.optimization_barrier(v.astype(jnp.bfloat16)).astype(jnp.float32)

@jax.custom_vjp
def low_back(v):
    return v

def low_keep(v):
    return (low(v), None)

def low_pass(kept, grad):
    return (grad,)

def back_keep(v):
    return (v, None)

def back_low(kept, grad):
    return (low(grad),)
low.defvjp(low_keep, low_pass)
low_back.defvjp(back_keep, back_low)

def norm_rows(rows, gain, bias):
    center = rows - lax.optimization_barrier(jnp.mean(rows, axis=-1, keepdims=True))
    spread = lax.optimization_barrier(jnp.mean(center * center, axis=-1, keepdims=True))
    return center * lax.rsqrt(spread + epsilon) * gain + bias

def group_norm(mixed):
    center = mixed - lax.optimization_barrier(jnp.mean(mixed, axis=-1, keepdims=True))
    spread = lax.optimization_barrier(jnp.mean(center * center, axis=-1, keepdims=True))
    return center * lax.rsqrt(spread + epsilon)

def angle_table(positions):
    half = KHEAD // 2
    inverse = 10000.0 ** (-jnp.arange(half, dtype=jnp.float32) / half)
    angles = positions.astype(jnp.float32)[:, None] * inverse[None, :]
    return (jnp.cos(angles)[:, None, :], jnp.sin(angles)[:, None, :])

def rotate(field, cosine, sine):
    half = field.shape[-1] // 2
    first = field[..., :half]
    second = field[..., half:]
    return jnp.concatenate([first * cosine - second * sine, first * sine + second * cosine], axis=-1)

def decay_tables(width):
    log_decay = jnp.log(1.0 - 2.0 ** (-5.0 - jnp.arange(HEADS, dtype=jnp.float32)))
    spots = jnp.arange(width, dtype=jnp.float32)
    offset = spots[:, None] - spots[None, :]
    causal = offset >= 0
    safe = jnp.where(causal, offset, 0.0)
    mask = jnp.where(causal[None], jnp.exp(safe[None] * log_decay[:, None, None]), 0.0)
    query_scaling_factor = jnp.exp((spots[:, None] + 1.0) * log_decay[None, :])
    key_scaling_factor = jnp.exp((width - 1.0 - spots[:, None]) * log_decay[None, :])
    carry_scale = jnp.exp(width * log_decay)
    return (mask, query_scaling_factor, key_scaling_factor, carry_scale)

def retention(query_rot, key_rot, value_low):
    width = LENGTH // N_SEQ
    mask, query_scaling_factor, key_scaling_factor, carry_scale = decay_tables(width)
    blocks = (query_rot.reshape(N_SEQ, width, HEADS, KHEAD), key_rot.reshape(N_SEQ, width, HEADS, KHEAD), value_low.reshape(N_SEQ, width, HEADS, VHEAD))

    @jax.checkpoint
    def span_step(retention_state, block):
        query_rows, key_portion, value_rows = block
        raw = jnp.einsum('ihk,jhk->hij', query_rows, key_portion, precision=highest_precision_mode)
        weights = low(low_back(raw) * mask)
        inner = jnp.einsum('hij,jhv->ihv', weights, value_rows, precision=highest_precision_mode)
        outer_product = jnp.einsum('tfx,fxz->tfz', query_rows, retention_state, precision=highest_precision_mode) * query_scaling_factor[:, :, None]
        state_update = jnp.einsum('lua,lus->uas', key_portion * key_scaling_factor[:, :, None], value_rows, precision=highest_precision_mode)
        return (carry_scale[:, None, None] * retention_state + state_update, inner + outer_product)
    start = jnp.zeros((HEADS, KHEAD, VHEAD), jnp.float32)
    final, outputs = lax.scan(span_step, start, blocks)
    return outputs.reshape(LENGTH, HEADS, VHEAD)

def block(rows, ln1_gain, ln1_bias, w_query, w_key, w_value, w_gate, w_out, ln2_gain, ln2_bias, w_mlp_gate, w_mlp_up, w_mlp_down):
    length = rows.shape[0]
    normed = low(norm_rows(rows, ln1_gain, ln1_bias))
    cosine, sine = angle_table(jnp.arange(length))
    query_proj = low_back(jnp.dot(normed, w_query, precision=highest_precision_mode)).reshape(length, HEADS, KHEAD)
    key_proj = low_back(jnp.dot(normed, w_key, precision=highest_precision_mode)).reshape(length, HEADS, KHEAD)
    query_rot = low(rotate(query_proj, cosine, sine))
    key_rot = low(rotate(key_proj, cosine, sine) * KHEAD ** (-0.5))
    value_low = low(low_back(jnp.dot(normed, w_value, precision=highest_precision_mode))).reshape(length, HEADS, VHEAD)
    gate_proj = low_back(jnp.dot(normed, w_gate, precision=highest_precision_mode))
    mixed = low_back(retention(query_rot, key_rot, value_low))
    grouped = group_norm(mixed).reshape(length, HEADS * VHEAD)
    gated = low(jax.nn.silu(gate_proj) * grouped)
    middle = rows + low_back(jnp.dot(gated, w_out, precision=highest_precision_mode))
    second = low(norm_rows(middle, ln2_gain, ln2_bias))
    gate_two = low_back(jnp.dot(second, w_mlp_gate, precision=highest_precision_mode))
    up_two = low_back(jnp.dot(second, w_mlp_up, precision=highest_precision_mode))
    hidden = low(jax.nn.gelu(gate_two, approximate=False) * up_two)
    return middle + low_back(jnp.dot(hidden, w_mlp_down, precision=highest_precision_mode))

def reference(inputs, cotangent, ln1_gain, ln1_bias, w_query, w_key, w_value, w_gate, w_out, ln2_gain, ln2_bias, w_mlp_gate, w_mlp_up, w_mlp_down):
    params = tuple((item.astype(jnp.float32) for item in (ln1_gain, ln1_bias, w_query, w_key, w_value, w_gate, w_out, ln2_gain, ln2_bias, w_mlp_gate, w_mlp_up, w_mlp_down)))

    def one_sequence(totals, pair):
        rows, grads_out = pair
        result, pull = jax.vjp(block, rows.astype(jnp.float32), *params)
        grads = pull(grads_out.astype(jnp.float32))
        totals = tuple((total + grad for total, grad in zip(totals, grads[1:])))
        return (totals, (result.astype(jnp.bfloat16), grads[0].astype(jnp.bfloat16)))
    zeros = tuple((jnp.zeros_like(item) for item in params))
    sums, (outputs, grad_inputs) = lax.scan(one_sequence, zeros, (inputs, cotangent))
    return (outputs, grad_inputs) + sums
```

```python
import functools

import jax
import jax.numpy as jnp
import numpy as np
from jax import lax
from jax.experimental import pallas as pl
from jax.experimental.pallas import tpu as pltpu
from jax.sharding import PartitionSpec as P

MESH = pl.DeviceIdType.MESH
F32 = jnp.float32
BF16 = jnp.bfloat16
EPS = 1e-05
VH = 432

CQ, CK, CV, CG, CO, CMG, CMU, CMD, TOTAL = 0, 512, 1024, 1920, 2816, 3712, 4608, 5504, 6400
WIDE = 896
REAL = 864
VTILE = CV + 768

GROUPS = (
    ((0, 640), (640, 640), (1280, 640)),
    ((1920, 640), (2560, 640), (3200, 512)),
    ((3712, 640), (4352, 512), (4864, 640)),
    ((5504, 256), (5760, 384), (6144, 256)),
)
ORDERS = (("x", "y", "z"), ("y", "z", "x"), ("z", "x", "y"))
ZYX = ("z", "y", "x")


def tables():
    half = 128
    inverse = np.power(10000.0, -np.arange(half, dtype=np.float64) / half)
    angles = np.arange(1024, dtype=np.float64)[:, None] * inverse[None, :]
    return (
        np.cos(angles).astype(np.float32).reshape(4, 256, half),
        np.sin(angles).astype(np.float32).reshape(4, 256, half),
    )


def mm(a, b):
    return lax.dot_general(a, b, (((1,), (0,)), ((), ())), preferred_element_type=F32)


def mm_nt(a, b):
    return lax.dot_general(a, b, (((1,), (1,)), ((), ())), preferred_element_type=F32)


def loop(n, body):
    def step(i, carry):
        body(i)
        return carry

    lax.fori_loop(0, n, step, 0)


def kernel(
    x_in, g_in, vec_in, wq_in, wk_in, wv_in, wg_in, wo_in, wmg_in, wmu_in, wmd_in, cos_in, sin_in,
    out_ref, gin_ref, gvec_ref, gq_ref, gk_ref, gv_ref, gg_ref, go_ref, gmg_ref, gmu_ref, gmd_ref,
    *scratch,
):
    (
        W, Gd, R1, R2, R3, FIN, X, G, WS, PSEND, PRECV, VEC, VA, COS, SIN,
        NORM, NORMT, TT, Q, QS, K, KW, V, GATE, WT, MASK, MIX, GRP,
        UT, STATES, CT, GUT, GATED, MID, SB, RB, SB1, RB1, OWN1, RB2, RB3, OWN2,
        SEC, ACT, BCT, HID, GGL, GUL, GM, GMX, GQ, GK, GV, FSEND, FRECV,
        ag_s, ag_r, rs_s, rs_r, st_s, st_r, ex_s, ex_r, loc,
    ) = scratch
    S1, S2, VT, RSTD, GML, GGP = R1.at[0], R2.at[0], TT.at[0:WIDE], MIX, SEC, HID
    dp = lax.axis_index("dp")
    sq = lax.axis_index("seq")
    me = {"z": dp // 4, "y": dp % 4, "x": sq // 2}
    c = sq % 2
    c0 = (c == 0).astype(F32)
    c1 = (c == 1).astype(F32)

    def shifted(axis, k):
        p = dict(me)
        p[axis] = (me[axis] + k) % 4
        return p

    def device(p, core):
        return (p["z"] * 4 + p["y"], p["x"] * 2 + core)

    sibling = device(me, 1 - c)

    def remote(src, dst, ss, rs, dev):
        return pltpu.make_async_remote_copy(
            src_ref=src, dst_ref=dst, send_sem=ss, recv_sem=rs, device_id=dev, device_id_type=MESH
        )

    cos_copy = pltpu.make_async_copy(cos_in.at[me["x"]], COS, loc.at[0])
    sin_copy = pltpu.make_async_copy(sin_in.at[me["x"]], SIN, loc.at[1])
    cos_copy.start()
    sin_copy.start()
    barrier = pltpu.get_barrier_semaphore()
    pl.semaphore_signal(barrier, inc=1, device_id=sibling, device_id_type=MESH)
    for axis in ZYX:
        for k in (1, 2, 3):
            pl.semaphore_signal(
                barrier, inc=1, device_id=device(shifted(axis, k), c), device_id_type=MESH
            )

    def put(ref, col, own):
        both = jnp.concatenate([own * c0, own * c1], axis=0)
        ref[:, col : col + own.shape[1]] = both.astype(BF16)

    def pack(col, h0, h1):
        put(PRECV.at[0], col, h0 * c0 + h1 * c1)
        put(PSEND, col, h0 * c1 + h1 * c0)

    for ref, col in ((wq_in, CQ), (wk_in, CK)):
        w = ref[...].astype(F32)
        pack(col, w[:, :512], w[:, 512:])
    lane = lax.broadcasted_iota(jnp.int32, (8, WIDE), 1)
    for ref, col in (
        (wv_in, CV), (wg_in, CG), (wo_in, CO), (wmg_in, CMG), (wmu_in, CMU), (wmd_in, CMD),
    ):
        WS[:, 1664:1792] = jnp.zeros((8, 128), F32)
        WS[:, :1728] = ref[...].astype(F32)
        h0 = jnp.where(lane < REAL, WS[:, :WIDE], 0.0)
        h1 = pltpu.roll(WS[:, 768:1792], 1024 - 96, 1)[:, :WIDE]
        h1 = jnp.where(lane < REAL, h1, 0.0)
        if col == CV:
            v = jnp.concatenate([jnp.zeros((8, 768), F32), vec_in[...].astype(F32)], axis=1)
            h0 = h0 + v
            h1 = h1 + v
        pack(col, h0, h1)

    pl.semaphore_wait(barrier, 10)

    rows_own = pl.ds(pl.multiple_of(c * 128, 128), 128)
    rows_sib = pl.ds(pl.multiple_of((1 - c) * 128, 128), 128)
    e_pack = remote(PSEND, PRECV.at[1], ex_s.at[0], ex_r.at[0], sibling)
    e_x = remote(x_in, X.at[rows_own, :], ex_s.at[1], ex_r.at[1], sibling)
    e_g = remote(g_in, G.at[rows_own, :], ex_s.at[2], ex_r.at[2], sibling)
    e_pack.start()
    e_x.start()
    e_g.start()
    e_pack.wait_recv()
    for col in range(0, TOTAL, 1280):
        s = pl.ds(col, 1280)
        W[me["z"], me["y"], me["x"], :, s] = (
            PRECV[0, :, s].astype(F32) + PRECV[1, :, s].astype(F32)
        ).astype(BF16)

    def ag(group, phase):
        copies = []
        for part in range(3):
            order = ORDERS[part]
            col, n = GROUPS[group][part]
            idx = tuple(slice(None) if a in order[:phase] else me[a] for a in ZYX)
            src = W.at[idx + (slice(None), pl.ds(col, n))]
            for k in (1, 2, 3):
                s = ((group * 3 + part) * 3 + phase) * 3 + k - 1
                copies.append(
                    remote(src, src, ag_s.at[s], ag_r.at[s], device(shifted(order[phase], k), c))
                )
        for copy in copies:
            copy.start()
        return copies

    pending = []

    def ag_wait(copies):
        for copy in copies:
            copy.wait_recv()
        pending.extend(copies)

    first = [ag(g, 0) for g in range(4)]
    ag_wait(first[0])
    second = ag(0, 1)
    third = []
    for g in range(4):
        if g < 3:
            ag_wait(first[g + 1])
        ag_wait(second)
        third.append(ag(g, 2))
        if g < 3:
            second = ag(g + 1, 1)

    X[rows_own, :] = x_in[...]
    G[rows_own, :] = g_in[...]
    e_x.wait_recv()
    e_g.wait_recv()
    cos_copy.wait()
    sin_copy.wait()

    def wcols(col, n):
        return W[:, :, :, :, col : col + n].reshape(1024, n)

    def wrows(i, col, n):
        return W[i, :, :, :, col : col + n].reshape(256, n)

    def fwd(a, col, n, emit):
        for at in range(0, n, 256):
            w = min(256, n - at)
            emit(at, w, mm(a[...], wcols(col + at, w)))

    def grad(at, b, col):
        n = b.shape[1]

        def body(i):
            r = mm(at[pl.ds(pl.multiple_of(i * 256, 256), 256), :], b[...])
            Gd[i, :, :, :, col : col + n] = r.astype(BF16).reshape(4, 4, 16, n)

        loop(4, body)

    def rows(i, n=32):
        return pl.ds(pl.multiple_of(i * n, n), n)

    lanes = lax.broadcasted_iota(jnp.int32, (32, WIDE), 1)
    in0 = lanes < VH
    in1 = (lanes >= VH) & (lanes < REAL)
    real = lanes < REAL

    def log_gamma(hh):
        g0 = float(np.log(1.0 - 2.0 ** (-5.0 - hh)))
        g1 = float(np.log(1.0 - 2.0 ** (-7.0 - hh)))
        return jnp.where(c == 0, jnp.float32(g0), jnp.float32(g1))

    lg = [log_gamma(0), log_gamma(1)]

    def mask_body(i):
        ii = lax.broadcasted_iota(jnp.int32, (32, 256), 0) + i * 32
        jj = lax.broadcasted_iota(jnp.int32, (32, 256), 1)
        d = (ii - jj).astype(F32)
        for hh in range(2):
            MASK[hh, rows(i), :] = jnp.where(d >= 0, jnp.exp(jnp.maximum(d, 0.0) * lg[hh]), 0.0)

    loop(8, mask_body)
    VA[...] = jnp.zeros_like(VA)

    ag_wait(third[0])
    VEC[...] = wcols(VTILE, 128).astype(F32).T[96:104, :]
    gain1, bias1 = VEC[0:1, :], VEC[1:2, :]
    gain2, bias2 = VEC[2:3, :], VEC[3:4, :]

    def norm(v):
        center = v - jnp.mean(v, axis=-1, keepdims=True)
        spread = jnp.mean(center * center, axis=-1, keepdims=True)
        rstd = lax.rsqrt(spread + EPS)
        return center * rstd, rstd

    def ln1(i):
        xh, _ = norm(X[rows(i), :].astype(F32))
        NORM[rows(i), :] = (xh * gain1 + bias1).astype(BF16)

    loop(8, ln1)

    def transpose(src, dst):
        dst[...] = src[...].T

    def rotated(dst, dst2, offset, sign, scale):
        def emit(at, w, r):
            hh = at // 256
            u, z = r[:, :128], r[:, 128:]
            co, si = COS[...], SIN[...]
            a0 = ((u * co - z * si) * scale).astype(BF16)
            a1 = ((u * si + z * co) * scale).astype(BF16)
            spot = lax.broadcasted_iota(jnp.int32, (256, 128), 0).astype(F32)
            sc = jnp.exp((spot * sign + offset) * lg[hh])
            dst[:, at : at + 128] = a0
            dst[:, at + 128 : at + 256] = a1
            dst2[:, at : at + 128] = (a0.astype(F32) * sc).astype(BF16)
            dst2[:, at + 128 : at + 256] = (a1.astype(F32) * sc).astype(BF16)

        return emit

    fwd(NORM, CK, 512, rotated(K, KW, 255.0, -1.0, 0.0625))

    def emit_v(at, w, r):
        col = lax.broadcasted_iota(jnp.int32, (256, w), 1) + at
        V[:, at : at + w] = jnp.where(col < REAL, r, 0.0).astype(BF16)

    fwd(NORM, CV, WIDE, emit_v)
    transpose(V, VT)
    for hh in range(2):
        r = mm(VT[VH * hh : VH * (hh + 1), :], KW[:, 256 * hh : 256 * (hh + 1)])
        UT[VH * hh : VH * (hh + 1), :] = r.astype(BF16)

    def state_send(src, base, sign):
        copies = []
        for k in (1, 2, 3):
            ok = (me["x"] + sign * k >= 0) & (me["x"] + sign * k <= 3)
            got = (me["x"] - sign * k >= 0) & (me["x"] - sign * k <= 3)
            to, slot = (k - 1, k - 1) if sign > 0 else (me["x"] - 1, me["x"] + k - 1)
            dev = device(shifted("x", sign * k), c)
            t = base + k - 1
            out = remote(src, STATES.at[jnp.clip(to, 0, 2)], st_s.at[t], st_r.at[t], dev)
            pl.when(ok)(out.start)
            slot = jnp.clip(slot, 0, 2)
            copies.append((out, remote(src, STATES.at[slot], st_s.at[t], st_r.at[t], dev), slot, ok, got))
        return copies

    def state_sum(copies, dst):
        dst[...] = jnp.zeros_like(dst)
        for k, (out, come, slot, ok, got) in enumerate(copies):

            def add(k=k, come=come, slot=slot):
                come.wait_recv()
                for hh in range(2):
                    s = slice(VH * hh, VH * (hh + 1))
                    coef = jnp.exp(256.0 * k * lg[hh])
                    dst[s, :] = (
                        dst[s, :].astype(F32) + coef * STATES[slot, s, :].astype(F32)
                    ).astype(BF16)

            pl.when(got)(add)
        for out, come, slot, ok, got in copies:
            pl.when(ok)(out.wait_send)

    u_copies = state_send(UT, 0, 1)
    fwd(NORM, CQ, 512, rotated(Q, QS, 1.0, 1.0, 1.0))

    for hh in range(2):
        raw = mm_nt(Q[:, 256 * hh : 256 * (hh + 1)], K[:, 256 * hh : 256 * (hh + 1)])
        WT[hh] = (raw * MASK[hh]).astype(BF16)

    def join(dst, h0, h1):
        pick = lax.broadcasted_iota(jnp.int32, (256, 128), 1) < VH - 384
        dst[:, 0:384] = h0[:, :384]
        dst[:, 384:512] = jnp.where(pick, h0[:, 384:512], h1[:, :128])
        dst[:, 512:896] = h1[:, 128:512]

    join(MIX, mm(WT[0], V[:, 0:512]), mm(WT[1], V[:, 384:896]))
    ag_wait(third[1])

    def emit_gate(at, w, r):
        GATE[:, at : at + w] = r

    fwd(NORM, CG, WIDE, emit_gate)
    transpose(NORM, NORMT)
    state_sum(u_copies, CT)
    join(GRP, mm_nt(QS[:, 0:256], CT[0:512, :]), mm_nt(QS[:, 256:512], CT[384:896, :]))

    def heads_mean(v):
        m0 = jnp.sum(jnp.where(in0, v, 0.0), axis=-1, keepdims=True) * (1.0 / VH)
        m1 = jnp.sum(jnp.where(in1, v, 0.0), axis=-1, keepdims=True) * (1.0 / VH)
        return jnp.where(in0, m0, m1)

    def group_norm(i):
        m = MIX[rows(i), :] + GRP[rows(i), :]
        center = m - heads_mean(m)
        rstd = lax.rsqrt(heads_mean(center * center) + EPS)
        grouped = jnp.where(real, center * rstd, 0.0)
        GRP[rows(i), :] = grouped
        RSTD[rows(i), :] = rstd
        gate = GATE[rows(i), :]
        GATED[rows(i), :] = (gate * jax.nn.sigmoid(gate) * grouped).astype(BF16)

    loop(8, group_norm)

    def out_body(i):
        r = mm_nt(GATED[...], wrows(i, CO, WIDE))
        s = pl.ds(pl.multiple_of(i * 256, 256), 256)
        MID[:, s] = r
        SB[:, s] = r.astype(BF16)

    loop(4, out_body)
    e_mid = remote(SB, RB, ex_s.at[3], ex_r.at[3], sibling)
    e_mid.start()
    ag_wait(third[2])
    e_mid.wait_recv()

    def ln2(i):
        m = X[rows(i), :].astype(F32) + MID[rows(i), :] + RB[rows(i), :].astype(F32)
        MID[rows(i), :] = m
        xh, _ = norm(m)
        SEC[rows(i), :] = (xh * gain2 + bias2).astype(BF16)

    loop(8, ln2)

    def emit_act(at, w, r):
        ACT[:, at : at + w] = r

    def emit_bct(at, w, r):
        BCT[:, at : at + w] = r

    fwd(SEC, CMG, WIDE, emit_act)
    fwd(SEC, CMU, WIDE, emit_bct)

    def gelu(i):
        g = ACT[rows(i), :]
        u = BCT[rows(i), :]
        cdf = 0.5 * (1.0 + lax.erf(g * 0.7071067811865476))
        ge = g * cdf
        HID[rows(i), :] = (ge * u).astype(BF16)
        BCT[rows(i), :] = ge
        ACT[rows(i), :] = (cdf + g * jnp.exp(-0.5 * g * g) * 0.3989422804014327) * u

    loop(8, gelu)
    ag_wait(third[3])

    def down_body(i):
        r = mm_nt(HID[...], wrows(i, CMD, WIDE))
        s = pl.ds(pl.multiple_of(i * 256, 256), 256)
        OWN1[:, s] = r[0:128] * c0 + r[128:256] * c1
        SB1[:, s] = (r[0:128] * c1 + r[128:256] * c0).astype(BF16)

    loop(4, down_body)
    e_out = remote(SB1, RB1, ex_s.at[4], ex_r.at[4], sibling)
    e_out.start()

    def back(group, phase, parts=(0, 1, 2)):
        copies = []
        for part in parts:
            order = ORDERS[part][::-1]
            col, n = GROUPS[group][part]
            s = pl.ds(col, n)
            left = [a for a in ZYX if a not in order[:phase]]
            axis = order[phase]
            for k in (1, 2, 3):
                to = shifted(axis, k)
                idx = tuple(to[a] if a == axis else slice(None) for a in left)
                src = (Gd, S1, S2)[phase].at[idx + (slice(None), s)]
                if phase == 0:
                    dst = R1.at[k - 1, :, :, :, s]
                elif phase == 1:
                    dst = R2.at[k - 1, :, :, s]
                else:
                    dst = R3.at[k - 1, :, s]
                t = ((group * 3 + part) * 3 + phase) * 3 + k - 1
                copies.append(remote(src, dst, rs_s.at[t], rs_r.at[t], device(to, c)))
        for copy in copies:
            copy.start()
        return copies

    def back_wait(copies):
        for copy in copies:
            copy.wait_recv()
        pending.extend(copies)

    def back_sum(group, phase, parts=(0, 1, 2)):
        for part in parts:
            order = ORDERS[part][::-1]
            col, n = GROUPS[group][part]
            s = pl.ds(col, n)
            left = [a for a in ZYX if a not in order[:phase]]
            axis = order[phase]
            at = left.index(axis)
            if phase == 0:

                def body(i):
                    if at == 0:
                        own = Gd[me[axis], i, :, :, s]
                    elif at == 1:
                        own = Gd[i, me[axis], :, :, s]
                    else:
                        own = Gd[i, :, me[axis], :, s]
                    t = own.astype(F32)
                    for k in range(3):
                        t = t + R1[k, i, :, :, s].astype(F32)
                    S1[i, :, :, s] = t.astype(BF16)

                loop(4, body)
            elif phase == 1:
                own = S1[me[axis], :, :, s] if at == 0 else S1[:, me[axis], :, s]
                t = own.astype(F32)
                for k in range(3):
                    t = t + R2[k, :, :, s].astype(F32)
                S2[:, :, s] = t.astype(BF16)
            else:
                t = S2[me[axis], :, s].astype(F32)
                for k in range(3):
                    t = t + R3[k, :, s].astype(F32)
                FIN[:, s] = t


    def step(copies, group, phase):
        back_wait(copies)
        back_sum(group, phase)
        return back(group, phase + 1) if phase < 2 else None

    transpose(G, TT)
    grad(TT, HID, CMD)
    r3 = back(3, 0)

    def emit_hidden(at, w, r):
        GGL[:, at : at + w] = (r * ACT[:, at : at + w]).astype(BF16)
        GUL[:, at : at + w] = (r * BCT[:, at : at + w]).astype(BF16)

    fwd(G, CMD, WIDE, emit_hidden)

    e_mid.wait_send()

    def second_body(i):
        r = mm_nt(GGL[...], wrows(i, CMG, WIDE)) + mm_nt(GUL[...], wrows(i, CMU, WIDE))
        s = pl.ds(pl.multiple_of(i * 256, 256), 256)
        GM[:, s] = r
        SB[:, s] = r.astype(BF16)

    loop(4, second_body)
    e_sec = remote(SB, RB2, ex_s.at[5], ex_r.at[5], sibling)
    e_sec.start()
    transpose(SEC, TT)
    grad(TT, GGL, CMG)
    grad(TT, GUL, CMU)
    r2 = back(2, 0)
    e_out.wait_recv()
    out_ref[...] = (MID[rows_own, :] + OWN1[...] + RB1[...].astype(F32)).astype(BF16)
    e_sec.wait_recv()

    def norm_back(gs, v, gain):
        xh, rstd = norm(v)
        gx = gs * gain
        m0 = jnp.mean(gx, axis=-1, keepdims=True)
        m1 = jnp.mean(gx * xh, axis=-1, keepdims=True)
        return rstd * (gx - m0 - xh * m1), jnp.sum(gs * xh, axis=0, keepdims=True), jnp.sum(gs, axis=0, keepdims=True)

    def ln2_back(i):
        gs = GM[rows(i), :] + RB2[rows(i), :].astype(F32)
        part, ggain, gbias = norm_back(gs, MID[rows(i), :], gain2)
        gm = G[rows(i), :].astype(F32) + part
        GM[rows(i), :] = gm
        GML[rows(i), :] = gm.astype(BF16)
        mine = (i // 4 == c).astype(F32)
        VA[2:3, :] += ggain * mine
        VA[3:4, :] += gbias * mine

    loop(8, ln2_back)
    r3 = step(r3, 3, 0)

    def emit_gated(at, w, r):
        ACT[:, at : at + w] = r

    fwd(GML, CO, WIDE, emit_gated)

    def group_back(i):
        gr = ACT[rows(i), :]
        z = GATE[rows(i), :]
        sg = jax.nn.sigmoid(z)
        grp = GRP[rows(i), :]
        GGP[rows(i), :] = (gr * (sg * (1.0 + z * (1.0 - sg))) * grp).astype(BF16)
        gg = gr * (z * sg)
        gmx = RSTD[rows(i), :] * (gg - heads_mean(gg) - grp * heads_mean(gg * grp))
        GMX[rows(i), :] = jnp.where(real, gmx, 0.0).astype(BF16)

    loop(8, group_back)
    transpose(GMX, VT)
    for hh in range(2):
        r = mm(VT[VH * hh : VH * (hh + 1), :], QS[:, 256 * hh : 256 * (hh + 1)])
        UT[VH * hh : VH * (hh + 1), :] = r.astype(BF16)
    c_copies = state_send(UT, 3, -1)
    r2 = step(r2, 2, 0)
    r3 = step(r3, 3, 1)
    transpose(GML, TT)
    grad(TT, GATED, CO)
    grad(NORMT, GGP, CG)
    r1 = back(1, 0)

    wide = lax.broadcasted_iota(jnp.int32, (256, 512), 1)
    windows = (slice(0, 512), slice(384, 896))

    def window(ref, hh):
        a = ref[:, windows[hh]]
        keep = wide < VH if hh == 0 else wide >= VH - 384
        return jnp.where(keep, a, jnp.zeros_like(a))

    gvi = []
    for hh in range(2):
        h = slice(256 * hh, 256 * (hh + 1))
        gm = window(GMX, hh)
        vw = V[:, windows[hh]]
        graw = (mm_nt(gm, vw) * MASK[hh]).astype(BF16)
        grawt = graw.T
        wt = WT[hh].T
        ACT[:, h] = mm(graw, K[:, h])
        BCT[:, h] = mm(grawt, Q[:, h])
        gvi.append(mm(wt, gm))
    join(MIX, gvi[0], gvi[1])
    state_sum(c_copies, GUT)

    def spots(hh, offset, sign):
        spot = lax.broadcasted_iota(jnp.int32, (256, 128), 0).astype(F32)
        return jnp.exp((spot * sign + offset) * lg[hh])

    gvs = []
    for hh in range(2):
        h = slice(256 * hh, 256 * (hh + 1))
        co, si = COS[...], SIN[...]
        cross = mm(window(GMX, hh), CT[windows[hh], :])
        sc = spots(hh, 1.0, 1.0)
        u = ACT[:, 256 * hh : 256 * hh + 128] + cross[:, :128] * sc
        z = ACT[:, 256 * hh + 128 : 256 * hh + 256] + cross[:, 128:] * sc
        GQ[:, 256 * hh : 256 * hh + 128] = (u * co + z * si).astype(BF16)
        GQ[:, 256 * hh + 128 : 256 * hh + 256] = (z * co - u * si).astype(BF16)
        cross = mm(window(V, hh), GUT[windows[hh], :])
        sc = spots(hh, 255.0, -1.0)
        u = (BCT[:, 256 * hh : 256 * hh + 128] + cross[:, :128] * sc) * 0.0625
        z = (BCT[:, 256 * hh + 128 : 256 * hh + 256] + cross[:, 128:] * sc) * 0.0625
        GK[:, 256 * hh : 256 * hh + 128] = (u * co + z * si).astype(BF16)
        GK[:, 256 * hh + 128 : 256 * hh + 256] = (z * co - u * si).astype(BF16)
        gvs.append(mm_nt(KW[:, h], GUT[windows[hh], :]))
    join(ACT, gvs[0], gvs[1])
    GV[...] = (MIX[...] + ACT[...]).astype(BF16)

    e_out.wait_send()

    def normed_body(i):
        r = mm_nt(GQ[...], wrows(i, CQ, 512)) + mm_nt(GK[...], wrows(i, CK, 512))
        r = r + mm_nt(GV[...], wrows(i, CV, WIDE)) + mm_nt(GGP[...], wrows(i, CG, WIDE))
        s = pl.ds(pl.multiple_of(i * 256, 256), 256)
        OWN2[:, s] = r[0:128] * c0 + r[128:256] * c1
        SB1[:, s] = (r[0:128] * c1 + r[128:256] * c0).astype(BF16)

    loop(4, normed_body)
    e_norm = remote(SB1, RB3, ex_s.at[6], ex_r.at[6], sibling)
    e_norm.start()
    r2 = step(r2, 2, 1)
    r3 = step(r3, 3, 2)
    grad(NORMT, GQ, CQ)
    grad(NORMT, GK, CK)
    grad(NORMT, GV, CV)
    r0 = back(0, 0, (0, 1))
    r1 = step(r1, 1, 0)
    e_norm.wait_recv()

    def ln1_back(i):
        at = pl.ds(pl.multiple_of(c * 128 + i * 32, 32), 32)
        gs = OWN2[rows(i), :] + RB3[rows(i), :].astype(F32)
        part, ggain, gbias = norm_back(gs, X[at, :].astype(F32), gain1)
        gin_ref[rows(i), :] = (GM[at, :] + part).astype(BF16)
        VA[0:1, :] += ggain
        VA[1:2, :] += gbias

    loop(4, ln1_back)
    vectors = jnp.concatenate([jnp.zeros((96, 1024), F32), VA[...], jnp.zeros((24, 1024), F32)], axis=0).T
    tile = slice(VTILE, VTILE + 128)
    Gd[:, :, :, :, tile] = (
        Gd[:, :, :, :, tile].astype(F32) + vectors.reshape(4, 4, 4, 16, 128)
    ).astype(BF16)
    r0 = r0 + back(0, 0, (2,))
    r2 = step(r2, 2, 2)
    r1 = step(r1, 1, 1)
    r0 = step(r0, 0, 0)
    r1 = step(r1, 1, 2)
    r0 = step(r0, 0, 1)
    r0 = step(r0, 0, 2)

    FSEND[...] = FIN[0:8, :] * c1 + FIN[8:16, :] * c0
    e_fin = remote(FSEND, FRECV, ex_s.at[7], ex_r.at[7], sibling)
    e_fin.start()
    e_fin.wait_recv()
    gvec_ref[...] = jnp.zeros((8, 128), F32)

    def halves(col, n):
        keep = FIN[0:8, col : col + n] * c0 + FIN[8:16, col : col + n] * c1
        got = FRECV[:, col : col + n]
        return keep * c0 + got * c1, keep * c1 + got * c0

    lo, hi = halves(VTILE, 128)
    gvec_ref[...] = lo + hi
    for ref, col in ((gq_ref, CQ), (gk_ref, CK)):
        lo, hi = halves(col, 512)
        ref[:, :512] = lo
        ref[:, 512:] = hi
    first96 = lax.broadcasted_iota(jnp.int32, (8, 128), 1) < 96
    for ref, col in (
        (gv_ref, CV), (gg_ref, CG), (go_ref, CO), (gmg_ref, CMG), (gmu_ref, CMU), (gmd_ref, CMD),
    ):
        lo, hi = halves(col, WIDE)
        moved = pltpu.roll(jnp.concatenate([hi, jnp.zeros((8, 128), F32)], axis=1), 96, 1)
        WS[:, 0:768] = lo[:, 0:768]
        WS[:, 768:896] = jnp.where(first96, lo[:, 768:896], moved[:, 0:128])
        WS[:, 896:1792] = moved[:, 128:1024]
        ref[...] = WS[:, :1728]
    for copy in pending:
        copy.wait_send()
    for copy in (e_pack, e_x, e_g, e_sec, e_norm, e_fin):
        copy.wait_send()


def scratch():
    def b(*shape):
        return pltpu.VMEM(shape, BF16)

    def f(*shape):
        return pltpu.VMEM(shape, F32)

    def sem(n):
        return pltpu.SemaphoreType.DMA((n,))

    return [
        b(4, 4, 4, 16, TOTAL), b(4, 4, 4, 16, TOTAL), b(3, 4, 4, 16, TOTAL),
        b(3, 4, 16, TOTAL), b(3, 16, TOTAL), f(16, TOTAL),
        b(256, 1024), b(256, 1024), f(8, 1792), b(16, TOTAL), b(2, 16, TOTAL), f(8, 1024), f(8, 1024),
        f(256, 128), f(256, 128),
        b(256, 1024), b(1024, 256), b(1024, 256), b(256, 512), b(256, 512), b(256, 512), b(256, 512),
        b(256, WIDE), f(256, WIDE), b(2, 256, 256), f(2, 256, 256), f(256, WIDE), f(256, WIDE),
        b(REAL, 256), b(3, REAL, 256), b(WIDE, 256), b(WIDE, 256),
        b(256, WIDE), f(256, 1024), b(256, 1024), b(256, 1024), b(128, 1024), b(128, 1024), f(128, 1024),
        b(256, 1024), b(128, 1024), f(128, 1024),
        b(256, 1024), f(256, WIDE), f(256, WIDE), b(256, WIDE), b(256, WIDE), b(256, WIDE),
        f(256, 1024), b(256, WIDE), b(256, 512), b(256, 512), b(256, WIDE),
        f(8, TOTAL), f(8, TOTAL),
        sem(108), sem(108), sem(108), sem(108), sem(6), sem(6), sem(8), sem(8), sem(2),
    ]


def per_device(
    inputs, cotangent, ln1_gain, ln1_bias, w_query, w_key, w_value, w_gate, w_out,
    ln2_gain, ln2_bias, w_mlp_gate, w_mlp_up, w_mlp_down,
):
    cosine, sine = tables()
    vectors = jnp.pad(jnp.stack([ln1_gain, ln1_bias, ln2_gain, ln2_bias], axis=1), ((0, 0), (96, 28)))
    vmem = pl.BlockSpec(memory_space=pltpu.VMEM)
    hbm = pl.BlockSpec(memory_space=pl.ANY)
    wide = jax.ShapeDtypeStruct((8, 1728), F32)
    square = jax.ShapeDtypeStruct((8, 1024), F32)
    out, gin, gvec, gq, gk, gv, gg, go, gmg, gmu, gmd = pl.pallas_call(
        kernel,
        out_shape=[
            jax.ShapeDtypeStruct((128, 1024), BF16), jax.ShapeDtypeStruct((128, 1024), BF16),
            jax.ShapeDtypeStruct((8, 128), F32), square, square, wide, wide, wide, wide, wide, wide,
        ],
        in_specs=[vmem] * 11 + [hbm] * 2,
        out_specs=[vmem] * 11,
        scratch_shapes=scratch(),
        compiler_params=pltpu.CompilerParams(
            collective_id=0, has_side_effects=True, vmem_limit_bytes=64 << 20
        ),
        name="block",
    )(
        inputs[0], cotangent[0], vectors, w_query, w_key, w_value, w_gate, w_out.T,
        w_mlp_gate, w_mlp_up, w_mlp_down.T, jnp.asarray(cosine), jnp.asarray(sine),
    )
    return (
        out[None], gin[None], gvec[:, 96], gvec[:, 97], gq, gk, gv, gg, go.T,
        gvec[:, 98], gvec[:, 99], gmg, gmu, gmd.T,
    )


def solution(mesh):
    both = ("dp", "seq")
    row, col, vec, tokens = P(both, None), P(None, both), P(both), P("dp", "seq", None)
    return jax.shard_map(
        per_device,
        mesh=mesh,
        in_specs=(tokens, tokens, vec, vec, row, row, row, row, col, vec, vec, row, row, col),
        out_specs=(tokens, tokens, vec, vec, row, row, row, row, col, vec, vec, row, row, col),
        check_vma=False,
    )
```

```python
import functools

import jax
import jax.numpy as jnp
import numpy as np
from jax import lax
from jax.experimental import pallas as pl
from jax.experimental.pallas import tpu as pltpu
from jax.sharding import PartitionSpec as P

MESH = pl.DeviceIdType.MESH
F32 = jnp.float32
BF16 = jnp.bfloat16
EPS = 1e-05
VH = 432

CQ, CK, CV, CG, CO, CMG, CMU, CMD, TOTAL = 0, 512, 1024, 1920, 2816, 3712, 4608, 5504, 6400
WIDE = 896
REAL = 864
OQ, OK, OWIDE, OVEC, OTOTAL = 0, 1024, tuple(range(2048, 12800, 1792)), 12800, 12928
VTILE = CV + 768

GROUPS = (
    ((0, 768), (768, 512), (1280, 640)),
    ((1920, 640), (2560, 512), (3072, 640)),
    ((3712, 640), (4352, 384), (4736, 768)),
    ((5504, 384), (5888, 256), (6144, 256)),
)
ORDERS = (("x", "y", "z"), ("y", "z", "x"), ("z", "x", "y"))
ZYX = ("z", "y", "x")


def tables():
    half = 128
    inverse = np.power(10000.0, -np.arange(half, dtype=np.float64) / half)
    angles = np.arange(1024, dtype=np.float64)[:, None] * inverse[None, :]
    return (
        np.cos(angles).astype(np.float32).reshape(4, 256, half),
        np.sin(angles).astype(np.float32).reshape(4, 256, half),
    )


def mm(a, b):
    return lax.dot_general(a, b, (((1,), (0,)), ((), ())), preferred_element_type=F32)


def mm_nt(a, b):
    return lax.dot_general(a, b, (((1,), (1,)), ((), ())), preferred_element_type=F32)


def loop(n, body):
    def step(i, carry):
        body(i)
        return carry

    lax.fori_loop(0, n, step, 0)


def kernel(
    x_in, g_in, vec_in, wq_in, wk_in, wv_in, wg_in, wo_in, wmg_in, wmu_in, wmd_in, cos_in, sin_in,
    out_ref, gin_ref, pack_ref, *scratch,
):
    (
        W, Gd, RA, RB1, R2, R3, FIN, X, G, WS, IN8, INW, INV, PACK, OUTV, PSEND, PRECV, VEC, VA, COS, SIN,
        NORM, NORMT, TT, Q, QS, K, KW, V, GATE, WT, MASK, MIX, GRP,
        UT, TOT, STATES, CT, GUT, GATED, MID, SB, RB, SBO, RBO, OWN1, RB2, RB3, OWN2,
        SEC, ACT, BCT, HID, GGL, GUL, GM, GMX, GQ, GK, GV, FSEND, FRECV,
        ag_s, ag_r, rs_s, rs_r, st_s, st_r, ex_s, ex_r, loc,
    ) = scratch
    S1, S2, VT, RSTD, GML, GGP = RB1.at[0], R2.at[0], TT.at[0:WIDE], MIX, SEC, HID
    dp = lax.axis_index("dp")
    sq = lax.axis_index("seq")
    me = {"z": dp // 4, "y": dp % 4, "x": sq // 2}
    c = sq % 2
    c0 = (c == 0).astype(F32)
    c1 = (c == 1).astype(F32)

    def shifted(axis, k):
        p = dict(me)
        p[axis] = (me[axis] + k) % 4
        return p

    def device(p, core):
        return (p["z"] * 4 + p["y"], p["x"] * 2 + core)

    sibling = device(me, 1 - c)

    def remote(src, dst, ss, rs, dev):
        return pltpu.make_async_remote_copy(
            src_ref=src, dst_ref=dst, send_sem=ss, recv_sem=rs, device_id=dev, device_id_type=MESH
        )

    rows_own = pl.ds(pl.multiple_of(c * 128, 128), 128)
    rows_sib = pl.ds(pl.multiple_of((1 - c) * 128, 128), 128)
    fetch = [
        pltpu.make_async_copy(src, dst, loc.at[i])
        for i, (src, dst) in enumerate(
            (
                (wq_in, IN8.at[0]), (wk_in, IN8.at[1]), (wv_in, INW.at[0]), (wg_in, INW.at[1]),
                (wo_in, INW.at[2]), (wmg_in, INW.at[3]), (wmu_in, INW.at[4]), (wmd_in, INW.at[5]),
                (vec_in, INV), (x_in, X.at[rows_own, :]), (g_in, G.at[rows_own, :]),
                (cos_in.at[me["x"]], COS), (sin_in.at[me["x"]], SIN),
            )
        )
    ]
    for copy in fetch:
        copy.start()
    barrier = pltpu.get_barrier_semaphore()
    pl.semaphore_signal(barrier, inc=1, device_id=sibling, device_id_type=MESH)
    for axis in ZYX:
        for k in (1, 2, 3):
            pl.semaphore_signal(
                barrier, inc=1, device_id=device(shifted(axis, k), c), device_id_type=MESH
            )

    def put(ref, col, own):
        both = jnp.concatenate([own * c0, own * c1], axis=0)
        ref[:, col : col + own.shape[1]] = both.astype(BF16)

    def pack(col, h0, h1):
        put(PRECV.at[0], col, h0 * c0 + h1 * c1)
        put(PSEND, col, h0 * c1 + h1 * c0)

    for copy in fetch[:9]:
        copy.wait()
    for i, col in enumerate((CQ, CK)):
        w = IN8[i].astype(F32)
        pack(col, w[:, :512], w[:, 512:])
    lane = lax.broadcasted_iota(jnp.int32, (8, WIDE), 1)
    for i, col in enumerate((CV, CG, CO, CMG, CMU, CMD)):
        WS[:, 1664:1792] = jnp.zeros((8, 128), F32)
        WS[:, :1728] = INW[i].astype(F32)
        h0 = jnp.where(lane < REAL, WS[:, :WIDE], 0.0)
        h1 = pltpu.roll(WS[:, 768:1792], 1024 - 96, 1)[:, :WIDE]
        h1 = jnp.where(lane < REAL, h1, 0.0)
        if col == CV:
            v = jnp.concatenate([INV[...], jnp.zeros((120, 128), F32)], axis=0).T
            v = pltpu.roll(v[0:8, :], 96, 1)
            v = jnp.concatenate([jnp.zeros((8, 768), F32), v], axis=1)
            h0 = h0 + v
            h1 = h1 + v
        pack(col, h0, h1)
    pl.semaphore_wait(barrier, 10)

    e_pack = remote(PSEND, PRECV.at[1], ex_s.at[0], ex_r.at[0], sibling)
    e_x = remote(X.at[rows_own, :], X.at[rows_own, :], ex_s.at[1], ex_r.at[1], sibling)
    e_g = remote(G.at[rows_own, :], G.at[rows_own, :], ex_s.at[2], ex_r.at[2], sibling)
    e_pack.start()
    fetch[9].wait()
    e_x.start()
    fetch[10].wait()
    e_g.start()
    e_pack.wait_recv()
    for col in range(0, TOTAL, 1280):
        s = pl.ds(col, 1280)
        W[me["z"], me["y"], me["x"], :, s] = (
            PRECV[0, :, s].astype(F32) + PRECV[1, :, s].astype(F32)
        ).astype(BF16)

    pending = []

    def send(copies):
        for copy in copies:
            copy.start()
        return copies

    def arrived(copies):
        for copy in copies:
            copy.wait_recv()
        pending.extend(copies)

    def gather(group, phase, forward=False):
        copies = []
        for part in range(3):
            order = ORDERS[part]
            axis = order[phase]
            col, n = GROUPS[group][part]
            base = (group * 3 + part) * 10 + (0, 3, 6)[phase] + (2 if forward else 0)
            for i, k in enumerate((1, 3) if phase == 2 else (1, 2, 3)):
                idx = []
                for a in ZYX:
                    if a == axis and forward:
                        idx.append((me[a] - k) % 4)
                    elif a in order[:phase]:
                        idx.append(slice(None))
                    else:
                        idx.append(me[a])
                if forward:
                    at = 0 if axis != "z" else 1
                    idx[at] = pl.ds(2 * i, 2)
                src = W.at[tuple(idx) + (slice(None), pl.ds(col, n))]
                dev = device(shifted(axis, k), c)
                copies.append(remote(src, src, ag_s.at[base + i], ag_r.at[base + i], dev))
        return send(copies)

    a1 = [gather(g, 0) for g in range(4)]
    arrived(a1[0])
    a2 = [gather(0, 1)]
    arrived(a1[1])
    a2.append(gather(1, 1))
    arrived(a2[0])
    a3 = [gather(0, 2)]
    arrived(a1[2])
    a2.append(gather(2, 1))
    arrived(a2[1])
    a3.append(gather(1, 2))
    arrived(a3[0])
    a4 = [gather(0, 2, True)]
    arrived(a1[3])
    a2.append(gather(3, 1))
    arrived(a2[2])
    a3.append(gather(2, 2))

    e_x.wait_recv()
    e_g.wait_recv()
    fetch[11].wait()
    fetch[12].wait()

    def wcols(col, n):
        return W[:, :, :, :, col : col + n].reshape(1024, n)

    def wrows(i, col, n):
        return W[i, :, :, :, col : col + n].reshape(256, n)

    def fwd(a, col, n, emit):
        for at in range(0, n, 256):
            w = min(256, n - at)
            emit(at, w, mm(a[...], wcols(col + at, w)))

    def grad(at, b, col):
        n = b.shape[1]

        def body(i):
            r = mm(at[pl.ds(pl.multiple_of(i * 256, 256), 256), :], b[...])
            Gd[i, :, :, :, col : col + n] = r.astype(BF16).reshape(4, 4, 16, n)

        loop(4, body)

    def rows(i, n=32):
        return pl.ds(pl.multiple_of(i * n, n), n)

    lanes = lax.broadcasted_iota(jnp.int32, (32, WIDE), 1)
    in0 = lanes < VH
    in1 = (lanes >= VH) & (lanes < REAL)
    real = lanes < REAL

    def log_gamma(hh):
        g0 = float(np.log(1.0 - 2.0 ** (-5.0 - hh)))
        g1 = float(np.log(1.0 - 2.0 ** (-7.0 - hh)))
        return jnp.where(c == 0, jnp.float32(g0), jnp.float32(g1))

    lg = [log_gamma(0), log_gamma(1)]

    def mask_body(i):
        ii = lax.broadcasted_iota(jnp.int32, (32, 256), 0) + i * 32
        jj = lax.broadcasted_iota(jnp.int32, (32, 256), 1)
        d = (ii - jj).astype(F32)
        for hh in range(2):
            MASK[hh, rows(i), :] = jnp.where(d >= 0, jnp.exp(jnp.maximum(d, 0.0) * lg[hh]), 0.0)

    loop(8, mask_body)
    VA[...] = jnp.zeros_like(VA)

    arrived(a4[0])
    VEC[...] = wcols(VTILE, 128).astype(F32).T[96:104, :]
    gain1, bias1 = VEC[0:1, :], VEC[1:2, :]
    gain2, bias2 = VEC[2:3, :], VEC[3:4, :]

    def norm(v):
        center = v - jnp.mean(v, axis=-1, keepdims=True)
        spread = jnp.mean(center * center, axis=-1, keepdims=True)
        rstd = lax.rsqrt(spread + EPS)
        return center * rstd, rstd

    def ln1(i):
        xh, _ = norm(X[rows(i), :].astype(F32))
        NORM[rows(i), :] = (xh * gain1 + bias1).astype(BF16)

    loop(8, ln1)

    def transpose(src, dst):
        dst[...] = src[...].T

    def rotated(dst, dst2, offset, sign, scale):
        def emit(at, w, r):
            hh = at // 256
            u, z = r[:, :128], r[:, 128:]
            co, si = COS[...], SIN[...]
            a0 = ((u * co - z * si) * scale).astype(BF16)
            a1 = ((u * si + z * co) * scale).astype(BF16)
            spot = lax.broadcasted_iota(jnp.int32, (256, 128), 0).astype(F32)
            sc = jnp.exp((spot * sign + offset) * lg[hh])
            dst[:, at : at + 128] = a0
            dst[:, at + 128 : at + 256] = a1
            dst2[:, at : at + 128] = (a0.astype(F32) * sc).astype(BF16)
            dst2[:, at + 128 : at + 256] = (a1.astype(F32) * sc).astype(BF16)

        return emit

    fwd(NORM, CK, 512, rotated(K, KW, 255.0, -1.0, 0.0625))

    def emit_v(at, w, r):
        col = lax.broadcasted_iota(jnp.int32, (256, w), 1) + at
        V[:, at : at + w] = jnp.where(col < REAL, r, 0.0).astype(BF16)

    fwd(NORM, CV, WIDE, emit_v)
    transpose(V, VT)
    for hh in range(2):
        r = mm(VT[VH * hh : VH * (hh + 1), :], KW[:, 256 * hh : 256 * (hh + 1)])
        UT[VH * hh : VH * (hh + 1), :] = r.astype(BF16)

    def head(hh):
        return slice(VH * hh, VH * (hh + 1))

    def states(src, base, back):
        x = me["x"]
        near = dict(me, x=x + 1 - 2 * (x % 2))
        far = dict(me, x=3 - x)
        low = x < 2
        sends = (x != 0) if back else (x != 3)
        gets = (x != 1) if back else (x != 2)
        passes = ~low if back else low
        steps = []
        for hh in range(2):
            t = base + hh
            slot = 1 if back else 0
            one = remote(src.at[head(hh)], STATES.at[slot, head(hh)], st_s.at[t], st_r.at[t], device(near, c))
            pl.when(sends)(one.start)
            steps.append(one)

        def second(hh):
            t = base + 2 + hh
            two = remote(TOT.at[head(hh)], STATES.at[2, head(hh)], st_s.at[t], st_r.at[t], device(far, c))

            def total():
                steps[hh].wait_recv()
                own = src[head(hh), :].astype(F32)
                got = STATES[slot, head(hh), :].astype(F32)
                g = jnp.exp(256.0 * lg[hh])
                first = (x % 2 == 1) if back else (x % 2 == 0)
                TOT[head(hh), :] = jnp.where(first, own * g + got, own + got * g).astype(BF16)
                two.start()

            pl.when(passes)(total)
            return two

        def finish(dst):
            dst[...] = jnp.zeros_like(dst)
            for hh, two in enumerate(twos):
                g = jnp.exp(256.0 * lg[hh])

                def single():
                    dst[head(hh), :] = STATES[slot, head(hh), :]

                def double():
                    two.wait_recv()
                    dst[head(hh), :] = STATES[2, head(hh), :]

                def triple():
                    steps[hh].wait_recv()
                    two.wait_recv()
                    total = STATES[2, head(hh), :].astype(F32) * g
                    dst[head(hh), :] = (total + STATES[slot, head(hh), :].astype(F32)).astype(BF16)

                one, pair, three = (2, 1, 0) if back else (1, 2, 3)
                pl.when(x == one)(single)
                pl.when(x == pair)(double)
                pl.when(x == three)(triple)
                pl.when(sends)(steps[hh].wait_send)
                pl.when(passes)(two.wait_send)

        twos = []

        def middle():
            twos.extend(second(hh) for hh in range(2))

        return middle, finish

    u_middle, u_finish = states(UT, 0, False)
    fwd(NORM, CQ, 512, rotated(Q, QS, 1.0, 1.0, 1.0))

    for hh in range(2):
        raw = mm_nt(Q[:, 256 * hh : 256 * (hh + 1)], K[:, 256 * hh : 256 * (hh + 1)])
        WT[hh] = (raw * MASK[hh]).astype(BF16)

    def join(dst, h0, h1):
        pick = lax.broadcasted_iota(jnp.int32, (256, 128), 1) < VH - 384
        dst[:, 0:384] = h0[:, :384]
        dst[:, 384:512] = jnp.where(pick, h0[:, 384:512], h1[:, :128])
        dst[:, 512:896] = h1[:, 128:512]

    join(MIX, mm(WT[0], V[:, 0:512]), mm(WT[1], V[:, 384:896]))
    u_middle()
    arrived(a3[1])
    a4.append(gather(1, 2, True))
    arrived(a2[3])
    a3.append(gather(3, 2))
    arrived(a4[1])

    def emit_gate(at, w, r):
        GATE[:, at : at + w] = r

    fwd(NORM, CG, WIDE, emit_gate)
    transpose(NORM, NORMT)
    u_finish(CT)
    join(GRP, mm_nt(QS[:, 0:256], CT[0:512, :]), mm_nt(QS[:, 256:512], CT[384:896, :]))

    def heads_mean(v):
        m0 = jnp.sum(jnp.where(in0, v, 0.0), axis=-1, keepdims=True) * (1.0 / VH)
        m1 = jnp.sum(jnp.where(in1, v, 0.0), axis=-1, keepdims=True) * (1.0 / VH)
        return jnp.where(in0, m0, m1)

    def group_norm(i):
        m = MIX[rows(i), :] + GRP[rows(i), :]
        center = m - heads_mean(m)
        rstd = lax.rsqrt(heads_mean(center * center) + EPS)
        grouped = jnp.where(real, center * rstd, 0.0)
        GRP[rows(i), :] = grouped
        RSTD[rows(i), :] = rstd
        gate = GATE[rows(i), :]
        GATED[rows(i), :] = (gate * jax.nn.sigmoid(gate) * grouped).astype(BF16)

    loop(8, group_norm)

    def out_body(i):
        r = mm_nt(GATED[...], wrows(i, CO, WIDE))
        s = pl.ds(pl.multiple_of(i * 256, 256), 256)
        MID[:, s] = r
        SB[:, s] = r.astype(BF16)

    loop(4, out_body)
    e_mid = remote(SB, RB, ex_s.at[3], ex_r.at[3], sibling)
    e_mid.start()
    arrived(a3[2])
    a4.append(gather(2, 2, True))
    arrived(a3[3])
    a4.append(gather(3, 2, True))
    arrived(a4[2])
    e_mid.wait_recv()

    def ln2(i):
        m = X[rows(i), :].astype(F32) + MID[rows(i), :] + RB[rows(i), :].astype(F32)
        MID[rows(i), :] = m
        xh, _ = norm(m)
        SEC[rows(i), :] = (xh * gain2 + bias2).astype(BF16)

    loop(8, ln2)

    def emit_act(at, w, r):
        ACT[:, at : at + w] = r

    def emit_bct(at, w, r):
        BCT[:, at : at + w] = r

    fwd(SEC, CMG, WIDE, emit_act)
    fwd(SEC, CMU, WIDE, emit_bct)

    def gelu(i):
        g = ACT[rows(i), :]
        u = BCT[rows(i), :]
        cdf = 0.5 * (1.0 + lax.erf(g * 0.7071067811865476))
        ge = g * cdf
        HID[rows(i), :] = (ge * u).astype(BF16)
        BCT[rows(i), :] = ge
        ACT[rows(i), :] = (cdf + g * jnp.exp(-0.5 * g * g) * 0.3989422804014327) * u

    loop(8, gelu)
    arrived(a4[3])

    def down_body(i):
        r = mm_nt(HID[...], wrows(i, CMD, WIDE))
        s = pl.ds(pl.multiple_of(i * 256, 256), 256)
        OWN1[:, s] = r[0:128] * c0 + r[128:256] * c1
        SBO[:, s] = (r[0:128] * c1 + r[128:256] * c0).astype(BF16)

    loop(4, down_body)
    e_out = remote(SBO, RBO, ex_s.at[4], ex_r.at[4], sibling)
    e_out.start()

    def place(axes, where, halves=None):
        return tuple(where.get(a, slice(None)) for a in axes)

    def others(part, phase):
        order = ORDERS[part][::-1]
        return order[phase], [a for a in ZYX if a not in order[: phase + 1]], [a for a in ZYX if a not in order[:phase]]

    def sems(group, part, i):
        t = (group * 3 + part) * 12 + i
        return rs_s.at[t], rs_r.at[t]

    def scatter0(group, parts=(0, 1, 2)):
        early, late = [], []
        for part in parts:
            axis, rest, left = others(part, 0)
            col, n = GROUPS[group][part]
            s = (slice(None), pl.ds(col, n))
            for i, k in enumerate((1, 3)):
                dev = device(shifted(axis, k), c)
                far, near = pl.ds(2 * i, 2), pl.ds(2 - 2 * i, 2)
                src = Gd.at[place(left, {axis: (me[axis] + 2) % 4, rest[0]: far}) + s]
                early.append(remote(src, RA.at[(i, slice(None), slice(None)) + s], *sems(group, part, i), dev))
                src = Gd.at[place(left, {axis: (me[axis] + k) % 4, rest[0]: near}) + s]
                late.append(remote(src, RB1.at[(i, near, slice(None)) + s], *sems(group, part, 2 + i), dev))
        send(early)
        return early, send(late)

    def scatter1(group, early, late, parts=(0, 1, 2)):
        arrived(early)
        for part in parts:
            axis, rest, left = others(part, 0)
            col, n = GROUPS[group][part]
            s = (slice(None), pl.ds(col, n))
            for i, k in enumerate((1, 3)):
                dev = device(shifted(axis, k), c)
                far = pl.ds(2 * i, 2)

                def body(j):
                    own = Gd[place(left, {axis: (me[axis] + k) % 4, rest[0]: 2 * i + j}) + s]
                    at = (i, j, slice(None)) + s
                    RA[at] = (own.astype(F32) + RA[at].astype(F32)).astype(BF16)

                loop(2, body)
                src = RA.at[(i, slice(None), slice(None)) + s]
                copy = remote(src, RB1.at[(i, far, slice(None)) + s], *sems(group, part, 4 + i), dev)
                late = late + send([copy])
        return late

    def scatter2(group, late, parts=(0, 1, 2)):
        arrived(late)
        copies = []
        for part in parts:
            axis, rest, left = others(part, 0)
            col, n = GROUPS[group][part]
            s = (slice(None), pl.ds(col, n))

            def body(j):
                own = Gd[place(left, {axis: me[axis], rest[0]: j}) + s].astype(F32)
                at = (j, slice(None)) + s
                RB1[(0,) + at] = (own + RB1[(0,) + at].astype(F32) + RB1[(1,) + at].astype(F32)).astype(BF16)

            loop(4, body)
            axis, rest, left = others(part, 1)
            for k in (1, 2, 3):
                to = shifted(axis, k)
                src = S1.at[place(left, {axis: to[axis]}) + s]
                copies.append(
                    remote(src, R2.at[(k - 1, slice(None)) + s], *sems(group, part, 5 + k), device(to, c))
                )
        return send(copies)

    def scatter3(group, copies):
        arrived(copies)
        copies = []
        for part in range(3):
            axis, rest, left = others(part, 1)
            col, n = GROUPS[group][part]
            s = (slice(None), pl.ds(col, n))
            t = S1[place(left, {axis: me[axis]}) + s].astype(F32)
            for k in range(3):
                t = t + R2[(k, slice(None)) + s].astype(F32)
            S2[(slice(None),) + s] = t.astype(BF16)
            axis, rest, left = others(part, 2)
            for k in (1, 2, 3):
                to = shifted(axis, k)
                src = S2.at[(to[axis],) + s]
                copies.append(remote(src, R3.at[(k - 1,) + s], *sems(group, part, 8 + k), device(to, c)))
        return send(copies)

    def scatter4(group, copies):
        arrived(copies)
        for part in range(3):
            axis, rest, left = others(part, 2)
            col, n = GROUPS[group][part]
            s = (slice(None), pl.ds(col, n))
            t = S2[(me[axis],) + s].astype(F32)
            for k in range(3):
                t = t + R3[(k,) + s].astype(F32)
            FIN[s] = t

    transpose(G, TT)
    grad(TT, HID, CMD)
    e3, r3 = scatter0(3)

    def emit_hidden(at, w, r):
        GGL[:, at : at + w] = (r * ACT[:, at : at + w]).astype(BF16)
        GUL[:, at : at + w] = (r * BCT[:, at : at + w]).astype(BF16)

    fwd(G, CMD, WIDE, emit_hidden)

    e_mid.wait_send()

    def second_body(i):
        r = mm_nt(GGL[...], wrows(i, CMG, WIDE)) + mm_nt(GUL[...], wrows(i, CMU, WIDE))
        s = pl.ds(pl.multiple_of(i * 256, 256), 256)
        GM[:, s] = r
        SB[:, s] = r.astype(BF16)

    loop(4, second_body)
    e_sec = remote(SB, RB2, ex_s.at[5], ex_r.at[5], sibling)
    e_sec.start()
    transpose(SEC, TT)
    grad(TT, GGL, CMG)
    grad(TT, GUL, CMU)
    r3 = scatter1(3, e3, r3)
    e2, r2 = scatter0(2)
    e_out.wait_recv()
    OUTV[0] = (MID[rows_own, :] + OWN1[...] + RBO[...].astype(F32)).astype(BF16)
    put_out = pltpu.make_async_copy(OUTV.at[0], out_ref, loc.at[13])
    put_out.start()
    e_sec.wait_recv()

    def norm_back(gs, v, gain):
        xh, rstd = norm(v)
        gx = gs * gain
        m0 = jnp.mean(gx, axis=-1, keepdims=True)
        m1 = jnp.mean(gx * xh, axis=-1, keepdims=True)
        return rstd * (gx - m0 - xh * m1), jnp.sum(gs * xh, axis=0, keepdims=True), jnp.sum(gs, axis=0, keepdims=True)

    def ln2_back(i):
        gs = GM[rows(i), :] + RB2[rows(i), :].astype(F32)
        part, ggain, gbias = norm_back(gs, MID[rows(i), :], gain2)
        gm = G[rows(i), :].astype(F32) + part
        GM[rows(i), :] = gm
        GML[rows(i), :] = gm.astype(BF16)
        mine = (i // 4 == c).astype(F32)
        VA[2:3, :] += ggain * mine
        VA[3:4, :] += gbias * mine

    loop(8, ln2_back)
    r3 = scatter2(3, r3)

    def emit_gated(at, w, r):
        ACT[:, at : at + w] = r

    fwd(GML, CO, WIDE, emit_gated)

    def group_back(i):
        gr = ACT[rows(i), :]
        z = GATE[rows(i), :]
        sg = jax.nn.sigmoid(z)
        grp = GRP[rows(i), :]
        GGP[rows(i), :] = (gr * (sg * (1.0 + z * (1.0 - sg))) * grp).astype(BF16)
        gg = gr * (z * sg)
        gmx = RSTD[rows(i), :] * (gg - heads_mean(gg) - grp * heads_mean(gg * grp))
        GMX[rows(i), :] = jnp.where(real, gmx, 0.0).astype(BF16)

    loop(8, group_back)
    transpose(GMX, VT)
    for hh in range(2):
        r = mm(VT[VH * hh : VH * (hh + 1), :], QS[:, 256 * hh : 256 * (hh + 1)])
        UT[VH * hh : VH * (hh + 1), :] = r.astype(BF16)
    c_middle, c_finish = states(UT, 4, True)
    r2 = scatter1(2, e2, r2)
    r3 = scatter3(3, r3)
    transpose(GML, TT)
    grad(TT, GATED, CO)
    grad(NORMT, GGP, CG)
    c_middle()
    e1, r1 = scatter0(1)
    scatter4(3, r3)
    r2 = scatter2(2, r2)

    wide = lax.broadcasted_iota(jnp.int32, (256, 512), 1)
    windows = (slice(0, 512), slice(384, 896))

    def window(ref, hh):
        a = ref[:, windows[hh]]
        keep = wide < VH if hh == 0 else wide >= VH - 384
        return jnp.where(keep, a, jnp.zeros_like(a))

    gvi = []
    for hh in range(2):
        h = slice(256 * hh, 256 * (hh + 1))
        gm = window(GMX, hh)
        vw = V[:, windows[hh]]
        graw = (mm_nt(gm, vw) * MASK[hh]).astype(BF16)
        grawt = graw.T
        wt = WT[hh].T
        ACT[:, h] = mm(graw, K[:, h])
        BCT[:, h] = mm(grawt, Q[:, h])
        gvi.append(mm(wt, gm))
    join(MIX, gvi[0], gvi[1])
    c_finish(GUT)

    def spots(hh, offset, sign):
        spot = lax.broadcasted_iota(jnp.int32, (256, 128), 0).astype(F32)
        return jnp.exp((spot * sign + offset) * lg[hh])

    gvs = []
    for hh in range(2):
        h = slice(256 * hh, 256 * (hh + 1))
        co, si = COS[...], SIN[...]
        cross = mm(window(GMX, hh), CT[windows[hh], :])
        sc = spots(hh, 1.0, 1.0)
        u = ACT[:, 256 * hh : 256 * hh + 128] + cross[:, :128] * sc
        z = ACT[:, 256 * hh + 128 : 256 * hh + 256] + cross[:, 128:] * sc
        GQ[:, 256 * hh : 256 * hh + 128] = (u * co + z * si).astype(BF16)
        GQ[:, 256 * hh + 128 : 256 * hh + 256] = (z * co - u * si).astype(BF16)
        cross = mm(window(V, hh), GUT[windows[hh], :])
        sc = spots(hh, 255.0, -1.0)
        u = (BCT[:, 256 * hh : 256 * hh + 128] + cross[:, :128] * sc) * 0.0625
        z = (BCT[:, 256 * hh + 128 : 256 * hh + 256] + cross[:, 128:] * sc) * 0.0625
        GK[:, 256 * hh : 256 * hh + 128] = (u * co + z * si).astype(BF16)
        GK[:, 256 * hh + 128 : 256 * hh + 256] = (z * co - u * si).astype(BF16)
        gvs.append(mm_nt(KW[:, h], GUT[windows[hh], :]))
    join(ACT, gvs[0], gvs[1])
    GV[...] = (MIX[...] + ACT[...]).astype(BF16)

    e_out.wait_send()

    def normed_body(i):
        r = mm_nt(GQ[...], wrows(i, CQ, 512)) + mm_nt(GK[...], wrows(i, CK, 512))
        r = r + mm_nt(GV[...], wrows(i, CV, WIDE)) + mm_nt(GGP[...], wrows(i, CG, WIDE))
        s = pl.ds(pl.multiple_of(i * 256, 256), 256)
        OWN2[:, s] = r[0:128] * c0 + r[128:256] * c1
        SBO[:, s] = (r[0:128] * c1 + r[128:256] * c0).astype(BF16)

    loop(4, normed_body)
    e_norm = remote(SBO, RB3, ex_s.at[6], ex_r.at[6], sibling)
    e_norm.start()
    r1 = scatter1(1, e1, r1)
    r2 = scatter3(2, r2)
    grad(NORMT, GQ, CQ)
    grad(NORMT, GK, CK)
    grad(NORMT, GV, CV)
    e0, r0 = scatter0(0, (0, 1))
    r1 = scatter2(1, r1)
    scatter4(2, r2)
    e_norm.wait_recv()

    def ln1_back(i):
        at = pl.ds(pl.multiple_of(c * 128 + i * 32, 32), 32)
        gs = OWN2[rows(i), :] + RB3[rows(i), :].astype(F32)
        part, ggain, gbias = norm_back(gs, X[at, :].astype(F32), gain1)
        OUTV[1, rows(i), :] = (GM[at, :] + part).astype(BF16)
        VA[0:1, :] += ggain
        VA[1:2, :] += gbias

    loop(4, ln1_back)
    put_gin = pltpu.make_async_copy(OUTV.at[1], gin_ref, loc.at[14])
    put_gin.start()
    vectors = jnp.concatenate([jnp.zeros((96, 1024), F32), VA[...], jnp.zeros((24, 1024), F32)], axis=0).T
    tile = slice(VTILE, VTILE + 128)
    Gd[:, :, :, :, tile] = (
        Gd[:, :, :, :, tile].astype(F32) + vectors.reshape(4, 4, 4, 16, 128)
    ).astype(BF16)
    e0c, r0c = scatter0(0, (2,))
    r0 = scatter1(0, e0, r0, (0, 1))
    r1 = scatter3(1, r1)
    r0 = r0 + scatter1(0, e0c, r0c, (2,))
    scatter4(1, r1)
    r0 = scatter2(0, r0)
    r0 = scatter3(0, r0)
    scatter4(0, r0)

    FSEND[...] = FIN[0:8, :] * c1 + FIN[8:16, :] * c0
    e_fin = remote(FSEND, FRECV, ex_s.at[7], ex_r.at[7], sibling)
    e_fin.start()
    e_fin.wait_recv()

    def halves(col, n):
        keep = FIN[0:8, col : col + n] * c0 + FIN[8:16, col : col + n] * c1
        got = FRECV[:, col : col + n]
        return keep * c0 + got * c1, keep * c1 + got * c0

    lo, hi = halves(VTILE, 128)
    PACK[:, OVEC : OVEC + 128] = lo + hi
    for at, col in ((OQ, CQ), (OK, CK)):
        lo, hi = halves(col, 512)
        PACK[:, at : at + 512] = lo
        PACK[:, at + 512 : at + 1024] = hi
    first96 = lax.broadcasted_iota(jnp.int32, (8, 128), 1) < 96
    for at, col in zip(OWIDE, (CV, CG, CO, CMG, CMU, CMD)):
        lo, hi = halves(col, WIDE)
        moved = pltpu.roll(jnp.concatenate([hi, jnp.zeros((8, 128), F32)], axis=1), 96, 1)
        PACK[:, at : at + 768] = lo[:, 0:768]
        PACK[:, at + 768 : at + 896] = jnp.where(first96, lo[:, 768:896], moved[:, 0:128])
        PACK[:, at + 896 : at + 1792] = moved[:, 128:1024]
    put_pack = pltpu.make_async_copy(PACK, pack_ref, loc.at[15])
    put_pack.start()
    put_out.wait()
    put_gin.wait()
    for copy in pending:
        copy.wait_send()
    for copy in (e_pack, e_x, e_g, e_sec, e_norm, e_fin):
        copy.wait_send()
    put_pack.wait()


def scratch():
    def b(*shape):
        return pltpu.VMEM(shape, BF16)

    def f(*shape):
        return pltpu.VMEM(shape, F32)

    def sem(n):
        return pltpu.SemaphoreType.DMA((n,))

    return [
        b(4, 4, 4, 16, TOTAL), b(4, 4, 4, 16, TOTAL), b(2, 2, 4, 16, TOTAL), b(2, 4, 4, 16, TOTAL),
        b(3, 4, 16, TOTAL), b(3, 16, TOTAL), f(16, TOTAL),
        b(256, 1024), b(256, 1024), f(8, 1792), b(2, 8, 1024), b(6, 8, 1728), f(8, 128), f(8, OTOTAL),
        b(2, 128, 1024), b(16, TOTAL), b(2, 16, TOTAL), f(8, 1024), f(8, 1024),
        f(256, 128), f(256, 128),
        b(256, 1024), b(1024, 256), b(1024, 256), b(256, 512), b(256, 512), b(256, 512), b(256, 512),
        b(256, WIDE), f(256, WIDE), b(2, 256, 256), f(2, 256, 256), f(256, WIDE), f(256, WIDE),
        b(REAL, 256), b(REAL, 256), b(3, REAL, 256), b(WIDE, 256), b(WIDE, 256),
        b(256, WIDE), f(256, 1024), b(256, 1024), b(256, 1024), b(128, 1024), b(128, 1024), f(128, 1024),
        b(256, 1024), b(128, 1024), f(128, 1024),
        b(256, 1024), f(256, WIDE), f(256, WIDE), b(256, WIDE), b(256, WIDE), b(256, WIDE),
        f(256, 1024), b(256, WIDE), b(256, 512), b(256, 512), b(256, WIDE),
        f(8, TOTAL), f(8, TOTAL),
        sem(120), sem(120), sem(144), sem(144), sem(8), sem(8), sem(8), sem(8), sem(16),
    ]


def per_device(
    inputs, cotangent, ln1_gain, ln1_bias, w_query, w_key, w_value, w_gate, w_out,
    ln2_gain, ln2_bias, w_mlp_gate, w_mlp_up, w_mlp_down,
):
    cosine, sine = tables()
    vectors = jnp.stack([ln1_gain, ln1_bias, ln2_gain, ln2_bias]).astype(F32)
    vectors = jnp.pad(vectors, ((0, 4), (0, 120)))
    out, gin, pack = pl.pallas_call(
        kernel,
        out_shape=[
            jax.ShapeDtypeStruct((128, 1024), BF16), jax.ShapeDtypeStruct((128, 1024), BF16),
            jax.ShapeDtypeStruct((8, OTOTAL), F32),
        ],
        in_specs=[pl.BlockSpec(memory_space=pl.ANY)] * 13,
        out_specs=[pl.BlockSpec(memory_space=pl.ANY)] * 3,
        scratch_shapes=scratch(),
        compiler_params=pltpu.CompilerParams(
            collective_id=0, has_side_effects=True, vmem_limit_bytes=64 << 20
        ),
        name="block",
    )(
        inputs[0], cotangent[0], vectors, w_query, w_key, w_value, w_gate, w_out.T,
        w_mlp_gate, w_mlp_up, w_mlp_down.T, jnp.asarray(cosine), jnp.asarray(sine),
    )
    gv, gg, go, gmg, gmu, gmd = (pack[:, at : at + 1728] for at in OWIDE)
    vec = [pack[:, OVEC + 96 + i] for i in range(4)]
    return (
        out[None], gin[None], vec[0], vec[1], pack[:, OQ : OQ + 1024], pack[:, OK : OK + 1024], gv, gg, go.T,
        vec[2], vec[3], gmg, gmu, gmd.T,
    )


def solution(mesh):
    both = ("dp", "seq")
    row, col, vec, tokens = P(both, None), P(None, both), P(both), P("dp", "seq", None)
    return jax.shard_map(
        per_device,
        mesh=mesh,
        in_specs=(tokens, tokens, vec, vec, row, row, row, row, col, vec, vec, row, row, col),
        out_specs=(tokens, tokens, vec, vec, row, row, row, row, col, vec, vec, row, row, col),
        check_vma=False,
    )
```

```python
import functools

import jax
import jax.numpy as jnp
import numpy as np
from jax import lax
from jax.experimental import pallas as pl
from jax.experimental.pallas import tpu as pltpu
from jax.sharding import PartitionSpec as P

MESH = pl.DeviceIdType.MESH
F32 = jnp.float32
BF16 = jnp.bfloat16
EPS = 1e-05
VH = 432

CK, CV, CQ, CG, CO, CMG, CMU, CMD, TOTAL = 0, 512, 1408, 1920, 2816, 3712, 4608, 5504, 6400
WIDE = 896
REAL = 864
VTILE = CV + 768
OVEC, OK, OV, OQ, OG, OO, OMG, OMU, OMD, OTOTAL = (
    0, 128, 1152, 2944, 3968, 5760, 7552, 9344, 11136, 12928,
)


def cut(start, *tiles):
    parts = []
    for part, n in enumerate(tiles):
        parts.append((part, start, 128 * n))
        start += 128 * n
    return tuple(parts)


GATHERS = (cut(CK, 4, 3, 4), cut(CQ, 4, 3, 4), cut(CO, 3, 2, 2), cut(CMG, 6, 3, 5), cut(CMD, 2, 2, 3))
KV = cut(CK, 4, 3, 4)
KV_EARLY, KV_LATE = cut(CK, 4, 3, 3), ((2, VTILE, 128),)
QGO, MLP, DOWN = cut(CQ, 7, 4, 7), cut(CMG, 5, 4, 5), cut(CMD, 3, 2, 2)
ORDERS = (("x", "y", "z"), ("y", "z", "x"), ("z", "x", "y"))
ZYX = ("z", "y", "x")


def tables():
    half = 128
    inverse = np.power(10000.0, -np.arange(half, dtype=np.float64) / half)
    angles = np.arange(1024, dtype=np.float64)[:, None] * inverse[None, :]
    return (
        np.cos(angles).astype(np.float32).reshape(4, 256, half),
        np.sin(angles).astype(np.float32).reshape(4, 256, half),
    )


def mm(a, b):
    return lax.dot_general(a, b, (((1,), (0,)), ((), ())), preferred_element_type=F32)


def mm_nt(a, b):
    return lax.dot_general(a, b, (((1,), (1,)), ((), ())), preferred_element_type=F32)


def loop(n, body):
    def step(i, carry):
        body(i)
        return carry

    lax.fori_loop(0, n, step, 0)


def kernel(
    x_in, g_in, vec_in, wq_in, wk_in, wv_in, wg_in, wo_in, wmg_in, wmu_in, wmd_in, cos_in, sin_in,
    out_ref, gin_ref, pack_ref, *scratch,
):
    (
        W, Gd, RA, RB1, R2, R3, X, G, WS, IN8, INW, INV, PACK, OUTV, PSEND, PRECV, VEC, VA, COS, SIN,
        NORM, NORMT, TT, Q, QS, K, KW, V, GGP, GATE, WT, MASK, MIX, GRP,
        UT, TOT, STATES, CT, GUT, GATED, MID, SB, RB, SBO, RBO, OWN1, RB2, RB3, OWN2,
        SEC, ACT, BCT, HID, GGL, GUL, GM, GMX, GQ, GK, GV, FSEND, FRECV, KEEP,
        way_s, way_r, st_s, st_r, ex_s, ex_r, loc,
    ) = scratch
    S1, S2, VT, RSTD, GML = RB1.at[0], R2.at[0], TT.at[0:WIDE], MIX, SEC
    dp = lax.axis_index("dp")
    sq = lax.axis_index("seq")
    me = {"z": dp // 4, "y": dp % 4, "x": sq // 2}
    c = sq % 2
    c0 = (c == 0).astype(F32)
    c1 = (c == 1).astype(F32)

    def shifted(axis, k):
        p = dict(me)
        p[axis] = (me[axis] + k) % 4
        return p

    def device(p, core):
        return (p["z"] * 4 + p["y"], p["x"] * 2 + core)

    sibling = device(me, 1 - c)

    def remote(src, dst, ss, rs, dev):
        return pltpu.make_async_remote_copy(
            src_ref=src, dst_ref=dst, send_sem=ss, recv_sem=rs, device_id=dev, device_id_type=MESH
        )

    rows_own = pl.ds(pl.multiple_of(c * 128, 128), 128)
    rows_sib = pl.ds(pl.multiple_of((1 - c) * 128, 128), 128)
    fetch = [
        pltpu.make_async_copy(src, dst, loc.at[i])
        for i, (src, dst) in enumerate(
            (
                (wq_in, IN8.at[0]), (wk_in, IN8.at[1]), (wv_in, INW.at[0]), (wg_in, INW.at[1]),
                (wo_in, INW.at[2]), (wmg_in, INW.at[3]), (wmu_in, INW.at[4]), (wmd_in, INW.at[5]),
                (vec_in, INV), (x_in, X.at[rows_own, :]), (g_in, G.at[rows_own, :]),
                (cos_in.at[me["x"]], COS), (sin_in.at[me["x"]], SIN),
            )
        )
    ]
    for copy in fetch:
        copy.start()
    barrier = pltpu.get_barrier_semaphore()
    pl.semaphore_signal(barrier, inc=1, device_id=sibling, device_id_type=MESH)
    for axis in ZYX:
        for k in (1, 2, 3):
            pl.semaphore_signal(
                barrier, inc=1, device_id=device(shifted(axis, k), c), device_id_type=MESH
            )

    def put(ref, col, own):
        both = jnp.concatenate([own * c0, own * c1], axis=0)
        ref[:, col : col + own.shape[1]] = both.astype(BF16)

    def pack(col, h0, h1):
        put(PRECV.at[0], col, h0 * c0 + h1 * c1)
        put(PSEND, col, h0 * c1 + h1 * c0)

    for copy in fetch[:9]:
        copy.wait()
    for i, col in enumerate((CQ, CK)):
        w = IN8[i].astype(F32)
        pack(col, w[:, :512], w[:, 512:])
    lane = lax.broadcasted_iota(jnp.int32, (8, WIDE), 1)
    for i, col in enumerate((CV, CG, CO, CMG, CMU, CMD)):
        WS[:, 1664:1792] = jnp.zeros((8, 128), F32)
        WS[:, :1728] = INW[i].astype(F32)
        h0 = jnp.where(lane < REAL, WS[:, :WIDE], 0.0)
        h1 = pltpu.roll(WS[:, 768:1792], 1024 - 96, 1)[:, :WIDE]
        h1 = jnp.where(lane < REAL, h1, 0.0)
        if col == CV:
            v = jnp.concatenate([INV[...], jnp.zeros((120, 128), F32)], axis=0).T
            v = pltpu.roll(v[0:8, :], 96, 1)
            v = jnp.concatenate([jnp.zeros((8, 768), F32), v], axis=1)
            h0 = h0 + v
            h1 = h1 + v
        pack(col, h0, h1)
    pl.semaphore_wait(barrier, 10)

    e_pack = remote(PSEND, PRECV.at[1], ex_s.at[0], ex_r.at[0], sibling)
    e_x = remote(X.at[rows_own, :], X.at[rows_own, :], ex_s.at[1], ex_r.at[1], sibling)
    e_g = remote(G.at[rows_own, :], G.at[rows_own, :], ex_s.at[2], ex_r.at[2], sibling)
    e_pack.start()
    fetch[9].wait()
    e_x.start()
    fetch[10].wait()
    e_g.start()
    e_pack.wait_recv()
    for col in range(0, TOTAL, 1280):
        s = pl.ds(col, 1280)
        W[me["z"], me["y"], me["x"], :, s] = (
            PRECV[0, :, s].astype(F32) + PRECV[1, :, s].astype(F32)
        ).astype(BF16)

    pending = []
    count = [0]

    def stage(total):
        count[0] += 1
        return way_s.at[count[0] - 1], way_r.at[count[0] - 1], total

    def send(where, src, dst, dev):
        remote(src, dst, where[0], where[1], dev).start()

    def arrived(where):
        ss, rs, total = where
        remote(total, total, ss, rs, sibling).wait_recv()
        pending.append(where)

    def columns(parts):
        return pl.ds(parts[0][1], sum(n for _, _, n in parts))

    def gather(group, phase, forward=False):
        s = columns(GATHERS[group])
        if phase == 0:
            where = stage(W.at[0, 0, 0:3, :, s])
        elif phase == 1:
            where = stage(W.at[0, 0:3, :, :, s])
        else:
            where = stage(W.at[0, :, :, :, s] if forward else W.at[0:2, :, :, :, s])
        for part, col, n in GATHERS[group]:
            order = ORDERS[part]
            axis = order[phase]
            for i, k in enumerate((1, 3) if phase == 2 else (1, 2, 3)):
                idx = []
                for a in ZYX:
                    if a == axis and forward:
                        idx.append((me[a] - k) % 4)
                    elif a in order[:phase]:
                        idx.append(slice(None))
                    else:
                        idx.append(me[a])
                if forward:
                    at = 0 if axis != "z" else 1
                    idx[at] = pl.ds(2 * i, 2)
                src = W.at[tuple(idx) + (slice(None), pl.ds(col, n))]
                send(where, src, src, device(shifted(axis, k), c))
        return where

    p1 = [gather(g, 0) for g in range(5)]
    p2, p3, p4 = {}, {}, {}
    arrived(p1[0])
    p2[0] = gather(0, 1)
    arrived(p1[1])
    p2[1] = gather(1, 1)
    arrived(p2[0])
    p3[0] = gather(0, 2)
    for g in (2, 3, 4):
        arrived(p1[g])
    p2[2] = gather(2, 1)
    arrived(p3[0])
    p4[0] = gather(0, 2, True)
    arrived(p2[1])
    p3[1] = gather(1, 2)
    p2[3] = gather(3, 1)
    p2[4] = gather(4, 1)

    e_x.wait_recv()
    e_g.wait_recv()
    fetch[11].wait()
    fetch[12].wait()

    def wcols(col, n):
        return W[:, :, :, :, col : col + n].reshape(1024, n)

    def wrows(i, col, n):
        return W[i, :, :, :, col : col + n].reshape(256, n)

    def fwd(a, col, n, emit):
        for at in range(0, n, 256):
            w = min(256, n - at)
            emit(at, w, mm(a[...], wcols(col + at, w)))

    def grad(at, b, col):
        n = b.shape[1]

        def body(i):
            r = mm(at[pl.ds(pl.multiple_of(i * 256, 256), 256), :], b[...])
            Gd[i, :, :, :, col : col + n] = r.astype(BF16).reshape(4, 4, 16, n)

        loop(4, body)

    def rows(i, n=32):
        return pl.ds(pl.multiple_of(i * n, n), n)

    lanes = lax.broadcasted_iota(jnp.int32, (32, WIDE), 1)
    in0 = lanes < VH
    in1 = (lanes >= VH) & (lanes < REAL)
    real = lanes < REAL

    def log_gamma(hh):
        g0 = float(np.log(1.0 - 2.0 ** (-5.0 - hh)))
        g1 = float(np.log(1.0 - 2.0 ** (-7.0 - hh)))
        return jnp.where(c == 0, jnp.float32(g0), jnp.float32(g1))

    lg = [log_gamma(0), log_gamma(1)]

    def mask_body(i):
        ii = lax.broadcasted_iota(jnp.int32, (32, 256), 0) + i * 32
        jj = lax.broadcasted_iota(jnp.int32, (32, 256), 1)
        d = (ii - jj).astype(F32)
        for hh in range(2):
            MASK[hh, rows(i), :] = jnp.where(d >= 0, jnp.exp(jnp.maximum(d, 0.0) * lg[hh]), 0.0)

    loop(8, mask_body)
    VA[...] = jnp.zeros_like(VA)

    arrived(p4[0])
    VEC[...] = wcols(VTILE, 128).astype(F32).T[96:104, :]
    gain1, bias1 = VEC[0:1, :], VEC[1:2, :]
    gain2, bias2 = VEC[2:3, :], VEC[3:4, :]

    def norm(v):
        center = v - jnp.mean(v, axis=-1, keepdims=True)
        spread = jnp.mean(center * center, axis=-1, keepdims=True)
        rstd = lax.rsqrt(spread + EPS)
        return center * rstd, rstd

    def ln1(i):
        xh, _ = norm(X[rows(i), :].astype(F32))
        NORM[rows(i), :] = (xh * gain1 + bias1).astype(BF16)

    loop(8, ln1)

    def transpose(src, dst):
        dst[...] = src[...].T

    def rotated(dst, dst2, offset, sign, scale):
        def emit(at, w, r):
            hh = at // 256
            u, z = r[:, :128], r[:, 128:]
            co, si = COS[...], SIN[...]
            a0 = ((u * co - z * si) * scale).astype(BF16)
            a1 = ((u * si + z * co) * scale).astype(BF16)
            spot = lax.broadcasted_iota(jnp.int32, (256, 128), 0).astype(F32)
            sc = jnp.exp((spot * sign + offset) * lg[hh])
            dst[:, at : at + 128] = a0
            dst[:, at + 128 : at + 256] = a1
            dst2[:, at : at + 128] = (a0.astype(F32) * sc).astype(BF16)
            dst2[:, at + 128 : at + 256] = (a1.astype(F32) * sc).astype(BF16)

        return emit

    fwd(NORM, CK, 512, rotated(K, KW, 255.0, -1.0, 0.0625))

    def emit_v(at, w, r):
        col = lax.broadcasted_iota(jnp.int32, (256, w), 1) + at
        V[:, at : at + w] = jnp.where(col < REAL, r, 0.0).astype(BF16)

    fwd(NORM, CV, WIDE, emit_v)
    transpose(V, VT)
    for hh in range(2):
        r = mm(VT[VH * hh : VH * (hh + 1), :], KW[:, 256 * hh : 256 * (hh + 1)])
        UT[VH * hh : VH * (hh + 1), :] = r.astype(BF16)

    def head(hh):
        return slice(VH * hh, VH * (hh + 1))

    def states(src, base, back):
        x = me["x"]
        near = dict(me, x=x + 1 - 2 * (x % 2))
        far = dict(me, x=3 - x)
        low = x < 2
        sends = (x != 0) if back else (x != 3)
        gets = (x != 1) if back else (x != 2)
        passes = ~low if back else low
        steps = []
        for hh in range(2):
            t = base + hh
            slot = 1 if back else 0
            one = remote(src.at[head(hh)], STATES.at[slot, head(hh)], st_s.at[t], st_r.at[t], device(near, c))
            pl.when(sends)(one.start)
            steps.append(one)

        def second(hh):
            t = base + 2 + hh
            two = remote(TOT.at[head(hh)], STATES.at[2, head(hh)], st_s.at[t], st_r.at[t], device(far, c))

            def total():
                steps[hh].wait_recv()
                own = src[head(hh), :].astype(F32)
                got = STATES[slot, head(hh), :].astype(F32)
                g = jnp.exp(256.0 * lg[hh])
                first = (x % 2 == 1) if back else (x % 2 == 0)
                TOT[head(hh), :] = jnp.where(first, own * g + got, own + got * g).astype(BF16)
                two.start()

            pl.when(passes)(total)
            return two

        def finish(dst):
            dst[...] = jnp.zeros_like(dst)
            for hh, two in enumerate(twos):
                g = jnp.exp(256.0 * lg[hh])

                def single():
                    dst[head(hh), :] = STATES[slot, head(hh), :]

                def double():
                    two.wait_recv()
                    dst[head(hh), :] = STATES[2, head(hh), :]

                def triple():
                    steps[hh].wait_recv()
                    two.wait_recv()
                    total = STATES[2, head(hh), :].astype(F32) * g
                    dst[head(hh), :] = (total + STATES[slot, head(hh), :].astype(F32)).astype(BF16)

                one, pair, three = (2, 1, 0) if back else (1, 2, 3)
                pl.when(x == one)(single)
                pl.when(x == pair)(double)
                pl.when(x == three)(triple)
                pl.when(sends)(steps[hh].wait_send)
                pl.when(passes)(two.wait_send)

        twos = []

        def middle():
            twos.extend(second(hh) for hh in range(2))

        return middle, finish

    u_middle, u_finish = states(UT, 0, False)
    arrived(p3[1])
    p4[1] = gather(1, 2, True)
    arrived(p2[2])
    p3[2] = gather(2, 2)
    arrived(p2[3])
    p3[3] = gather(3, 2)
    transpose(NORM, NORMT)
    transpose(G, TT)
    arrived(p4[1])
    fwd(NORM, CQ, 512, rotated(Q, QS, 1.0, 1.0, 1.0))

    for hh in range(2):
        raw = mm_nt(Q[:, 256 * hh : 256 * (hh + 1)], K[:, 256 * hh : 256 * (hh + 1)])
        WT[hh] = (raw * MASK[hh]).astype(BF16)

    def join(dst, h0, h1):
        pick = lax.broadcasted_iota(jnp.int32, (256, 128), 1) < VH - 384
        dst[:, 0:384] = h0[:, :384]
        dst[:, 384:512] = jnp.where(pick, h0[:, 384:512], h1[:, :128])
        dst[:, 512:896] = h1[:, 128:512]

    join(MIX, mm(WT[0], V[:, 0:512]), mm(WT[1], V[:, 384:896]))
    u_middle()

    def emit_gate(at, w, r):
        GATE[:, at : at + w] = r

    fwd(NORM, CG, WIDE, emit_gate)
    arrived(p3[2])
    p4[2] = gather(2, 2, True)
    arrived(p2[4])
    p3[4] = gather(4, 2)
    u_finish(CT)
    join(GRP, mm_nt(QS[:, 0:256], CT[0:512, :]), mm_nt(QS[:, 256:512], CT[384:896, :]))

    def heads_mean(v):
        m0 = jnp.sum(jnp.where(in0, v, 0.0), axis=-1, keepdims=True) * (1.0 / VH)
        m1 = jnp.sum(jnp.where(in1, v, 0.0), axis=-1, keepdims=True) * (1.0 / VH)
        return jnp.where(in0, m0, m1)

    def group_norm(i):
        m = MIX[rows(i), :] + GRP[rows(i), :]
        center = m - heads_mean(m)
        rstd = lax.rsqrt(heads_mean(center * center) + EPS)
        grouped = jnp.where(real, center * rstd, 0.0)
        GRP[rows(i), :] = grouped
        RSTD[rows(i), :] = rstd
        gate = GATE[rows(i), :]
        GATED[rows(i), :] = (gate * jax.nn.sigmoid(gate) * grouped).astype(BF16)

    loop(8, group_norm)
    arrived(p3[3])
    p4[3] = gather(3, 2, True)
    arrived(p4[2])

    def out_body(i):
        r = mm_nt(GATED[...], wrows(i, CO, WIDE))
        s = pl.ds(pl.multiple_of(i * 256, 256), 256)
        MID[:, s] = r
        SB[:, s] = r.astype(BF16)

    loop(4, out_body)
    e_mid = remote(SB, RB, ex_s.at[3], ex_r.at[3], sibling)
    e_mid.start()
    arrived(p3[4])
    p4[4] = gather(4, 2, True)
    e_mid.wait_recv()

    def ln2(i):
        m = X[rows(i), :].astype(F32) + MID[rows(i), :] + RB[rows(i), :].astype(F32)
        MID[rows(i), :] = m
        xh, _ = norm(m)
        SEC[rows(i), :] = (xh * gain2 + bias2).astype(BF16)

    loop(8, ln2)
    arrived(p4[3])

    def emit_act(at, w, r):
        ACT[:, at : at + w] = r

    def emit_bct(at, w, r):
        BCT[:, at : at + w] = r

    fwd(SEC, CMG, WIDE, emit_act)
    fwd(SEC, CMU, WIDE, emit_bct)

    def gelu(i):
        g = ACT[rows(i), :]
        u = BCT[rows(i), :]
        cdf = 0.5 * (1.0 + lax.erf(g * 0.7071067811865476))
        ge = g * cdf
        HID[rows(i), :] = (ge * u).astype(BF16)
        BCT[rows(i), :] = ge
        ACT[rows(i), :] = (cdf + g * jnp.exp(-0.5 * g * g) * 0.3989422804014327) * u

    loop(8, gelu)
    arrived(p4[4])

    def place(axes, where):
        return tuple(where.get(a, slice(None)) for a in axes)

    def others(part, phase):
        order = ORDERS[part][::-1]
        return order[phase], [a for a in ZYX if a not in order[: phase + 1]], [a for a in ZYX if a not in order[:phase]]

    def scatter0(parts, late=None):
        s = columns(parts)
        early = stage(RA.at[:, :, :, :, s])
        late = late or stage(RB1.at[:, :, :, :, s])
        for where in (early, late):
            for part, col, n in parts:
                axis, rest, left = others(part, 0)
                s = (slice(None), pl.ds(col, n))
                for i, k in enumerate((1, 3)):
                    dev = device(shifted(axis, k), c)
                    if where is early:
                        src = Gd.at[place(left, {axis: (me[axis] + 2) % 4, rest[0]: pl.ds(2 * i, 2)}) + s]
                        send(where, src, RA.at[(i, slice(None), slice(None)) + s], dev)
                    else:
                        near = pl.ds(2 - 2 * i, 2)
                        src = Gd.at[place(left, {axis: (me[axis] + k) % 4, rest[0]: near}) + s]
                        send(where, src, RB1.at[(i, near, slice(None)) + s], dev)
        return early, late

    def scatter1(parts, where):
        early, late = where
        arrived(early)
        for part, col, n in parts:
            axis, rest, left = others(part, 0)
            s = (slice(None), pl.ds(col, n))
            for i, k in enumerate((1, 3)):

                def body(j):
                    own = Gd[place(left, {axis: (me[axis] + k) % 4, rest[0]: 2 * i + j}) + s]
                    at = (i, j, slice(None)) + s
                    RA[at] = (own.astype(F32) + RA[at].astype(F32)).astype(BF16)

                loop(2, body)
                src = RA.at[(i, slice(None), slice(None)) + s]
                dst = RB1.at[(i, pl.ds(2 * i, 2), slice(None)) + s]
                send(late, src, dst, device(shifted(axis, k), c))
        return late

    def scatter2(parts, late):
        arrived(late)
        where = stage(R2.at[:, :, :, columns(parts)])
        for part, col, n in parts:
            axis, rest, left = others(part, 0)
            s = (slice(None), pl.ds(col, n))

            def body(j):
                own = Gd[place(left, {axis: me[axis], rest[0]: j}) + s].astype(F32)
                at = (j, slice(None)) + s
                RB1[(0,) + at] = (own + RB1[(0,) + at].astype(F32) + RB1[(1,) + at].astype(F32)).astype(BF16)

            loop(4, body)
            axis, rest, left = others(part, 1)
            for k in (1, 2, 3):
                to = shifted(axis, k)
                src = S1.at[place(left, {axis: to[axis]}) + s]
                send(where, src, R2.at[(k - 1, slice(None)) + s], device(to, c))
        return where

    def scatter3(parts, where):
        arrived(where)
        where = stage(R3.at[:, :, columns(parts)])
        for part, col, n in parts:
            axis, rest, left = others(part, 1)
            s = (slice(None), pl.ds(col, n))
            t = S1[place(left, {axis: me[axis]}) + s].astype(F32)
            for k in range(3):
                t = t + R2[(k, slice(None)) + s].astype(F32)
            S2[(slice(None),) + s] = t.astype(BF16)
            axis, rest, left = others(part, 2)
            for k in (1, 2, 3):
                to = shifted(axis, k)
                send(where, S2.at[(to[axis],) + s], R3.at[(k - 1,) + s], device(to, c))
        return where

    def scatter4(parts, where, i):
        arrived(where)
        for part, col, n in parts:
            axis, rest, left = others(part, 2)
            s = (slice(None), pl.ds(col, n))
            t = S2[(me[axis],) + s].astype(F32)
            for k in range(3):
                t = t + R3[(k,) + s].astype(F32)
            KEEP[:, s[1]] = t[0:8, :] * c0 + t[8:16, :] * c1
            FSEND[:, s[1]] = t[0:8, :] * c1 + t[8:16, :] * c0
        s = columns(parts)
        copy = remote(FSEND.at[:, s], FRECV.at[:, s], ex_s.at[7 + i], ex_r.at[7 + i], sibling)
        copy.start()
        return copy

    def halves(col, n):
        keep = KEEP[:, col : col + n]
        got = FRECV[:, col : col + n]
        return keep * c0 + got * c1, keep * c1 + got * c0

    def finish(copy, first, last, where, i):
        copy.wait_recv()
        if first == OVEC:
            lo, hi = halves(VTILE, 128)
            PACK[:, OVEC:OK] = lo + hi
        for at, col in where:
            if col in (CQ, CK):
                lo, hi = halves(col, 512)
                PACK[:, at : at + 512] = lo
                PACK[:, at + 512 : at + 1024] = hi
            else:
                lo, hi = halves(col, WIDE)
                moved = pltpu.roll(jnp.concatenate([hi, jnp.zeros((8, 128), F32)], axis=1), 96, 1)
                first96 = lax.broadcasted_iota(jnp.int32, (8, 128), 1) < 96
                PACK[:, at : at + 768] = lo[:, 0:768]
                PACK[:, at + 768 : at + 896] = jnp.where(first96, lo[:, 768:896], moved[:, 0:128])
                PACK[:, at + 896 : at + 1792] = moved[:, 128:1024]
        out = pltpu.make_async_copy(PACK.at[:, first:last], pack_ref.at[:, first:last], loc.at[15 + i])
        out.start()
        return copy, out

    grad(TT, HID, CMD)
    r_down = scatter0(DOWN)

    def emit_hidden(at, w, r):
        GGL[:, at : at + w] = (r * ACT[:, at : at + w]).astype(BF16)
        GUL[:, at : at + w] = (r * BCT[:, at : at + w]).astype(BF16)

    fwd(G, CMD, WIDE, emit_hidden)

    e_mid.wait_send()

    def second_body(i):
        r = mm_nt(GGL[...], wrows(i, CMG, WIDE)) + mm_nt(GUL[...], wrows(i, CMU, WIDE))
        s = pl.ds(pl.multiple_of(i * 256, 256), 256)
        GM[:, s] = r
        SB[:, s] = r.astype(BF16)

    loop(4, second_body)
    e_sec = remote(SB, RB2, ex_s.at[5], ex_r.at[5], sibling)
    e_sec.start()
    transpose(SEC, TT)
    grad(TT, GGL, CMG)
    grad(TT, GUL, CMU)
    r_down = scatter1(DOWN, r_down)
    r_mlp = scatter0(MLP)
    e_sec.wait_recv()

    def norm_back(gs, v, gain):
        xh, rstd = norm(v)
        gx = gs * gain
        m0 = jnp.mean(gx, axis=-1, keepdims=True)
        m1 = jnp.mean(gx * xh, axis=-1, keepdims=True)
        return rstd * (gx - m0 - xh * m1), jnp.sum(gs * xh, axis=0, keepdims=True), jnp.sum(gs, axis=0, keepdims=True)

    def ln2_back(i):
        gs = GM[rows(i), :] + RB2[rows(i), :].astype(F32)
        part, ggain, gbias = norm_back(gs, MID[rows(i), :], gain2)
        gm = G[rows(i), :].astype(F32) + part
        GM[rows(i), :] = gm
        GML[rows(i), :] = gm.astype(BF16)
        mine = (i // 4 == c).astype(F32)
        VA[2:3, :] += ggain * mine
        VA[3:4, :] += gbias * mine

    loop(8, ln2_back)
    r_down = scatter2(DOWN, r_down)

    def emit_gated(at, w, r):
        ACT[:, at : at + w] = r

    fwd(GML, CO, WIDE, emit_gated)

    def group_back(i):
        gr = ACT[rows(i), :]
        z = GATE[rows(i), :]
        sg = jax.nn.sigmoid(z)
        grp = GRP[rows(i), :]
        GGP[rows(i), :] = (gr * (sg * (1.0 + z * (1.0 - sg))) * grp).astype(BF16)
        gg = gr * (z * sg)
        gmx = RSTD[rows(i), :] * (gg - heads_mean(gg) - grp * heads_mean(gg * grp))
        GMX[rows(i), :] = jnp.where(real, gmx, 0.0).astype(BF16)

    loop(8, group_back)
    transpose(GMX, VT)
    for hh in range(2):
        r = mm(VT[VH * hh : VH * (hh + 1), :], QS[:, 256 * hh : 256 * (hh + 1)])
        UT[VH * hh : VH * (hh + 1), :] = r.astype(BF16)
    c_middle, c_finish = states(UT, 4, True)
    r_mlp = scatter1(MLP, r_mlp)
    r_down = scatter3(DOWN, r_down)
    transpose(GML, TT)
    grad(TT, GATED, CO)
    grad(NORMT, GGP, CG)

    wide = lax.broadcasted_iota(jnp.int32, (256, 512), 1)
    windows = (slice(0, 512), slice(384, 896))

    def window(ref, hh):
        a = ref[:, windows[hh]]
        keep = wide < VH if hh == 0 else wide >= VH - 384
        return jnp.where(keep, a, jnp.zeros_like(a))

    def spots(hh, offset, sign):
        spot = lax.broadcasted_iota(jnp.int32, (256, 128), 0).astype(F32)
        return jnp.exp((spot * sign + offset) * lg[hh])

    def unrotated(dst, src, hh, cross, offset, sign, scale):
        sc = spots(hh, offset, sign)
        co, si = COS[...], SIN[...]
        a, b = slice(256 * hh, 256 * hh + 128), slice(256 * hh + 128, 256 * hh + 256)
        u = (src[:, a] + cross[:, :128] * sc) * scale
        z = (src[:, b] + cross[:, 128:] * sc) * scale
        dst[:, a] = (u * co + z * si).astype(BF16)
        dst[:, b] = (z * co - u * si).astype(BF16)

    gvi = []
    for hh in range(2):
        h = slice(256 * hh, 256 * (hh + 1))
        gm = window(GMX, hh)
        vw = V[:, windows[hh]]
        graw = (mm_nt(gm, vw) * MASK[hh]).astype(BF16)
        ACT[:, h] = mm(graw, K[:, h])
        BCT[:, h] = mm(graw.T, Q[:, h])
        gvi.append(mm(WT[hh].T, gm))
        unrotated(GQ, ACT, hh, mm(gm, CT[windows[hh], :]), 1.0, 1.0, 1.0)
    join(MIX, gvi[0], gvi[1])
    grad(NORMT, GQ, CQ)
    r_qgo = scatter0(QGO)
    c_middle()
    r_mlp = scatter2(MLP, r_mlp)
    f_down = scatter4(DOWN, r_down, 0)

    def down_body(i):
        r = mm_nt(HID[...], wrows(i, CMD, WIDE))
        s = pl.ds(pl.multiple_of(i * 256, 256), 256)
        OWN1[:, s] = r[0:128] * c0 + r[128:256] * c1
        SBO[:, s] = (r[0:128] * c1 + r[128:256] * c0).astype(BF16)

    loop(4, down_body)
    e_out = remote(SBO, RBO, ex_s.at[4], ex_r.at[4], sibling)
    e_out.start()
    r_qgo = scatter1(QGO, r_qgo)
    r_mlp = scatter3(MLP, r_mlp)
    e_out.wait_recv()
    OUTV[0] = (MID[rows_own, :] + OWN1[...] + RBO[...].astype(F32)).astype(BF16)
    put_out = pltpu.make_async_copy(OUTV.at[0], out_ref, loc.at[13])
    put_out.start()

    def normed_first(i):
        r = mm_nt(GQ[...], wrows(i, CQ, 512)) + mm_nt(GGP[...], wrows(i, CG, WIDE))
        MID[:, pl.ds(pl.multiple_of(i * 256, 256), 256)] = r

    loop(4, normed_first)
    f_down = finish(f_down, OMD, OTOTAL, ((OMD, CMD),), 0)
    c_finish(GUT)

    gvs = []
    for hh in range(2):
        h = slice(256 * hh, 256 * (hh + 1))
        unrotated(GK, BCT, hh, mm(window(V, hh), GUT[windows[hh], :]), 255.0, -1.0, 0.0625)
        gvs.append(mm_nt(KW[:, h], GUT[windows[hh], :]))
    join(ACT, gvs[0], gvs[1])
    GV[...] = (MIX[...] + ACT[...]).astype(BF16)
    grad(NORMT, GK, CK)
    grad(NORMT, GV, CV)
    r_kv = scatter0(KV_EARLY, stage(RB1.at[:, :, :, :, columns(KV)]))
    e_out.wait_send()

    def normed_body(i):
        s = pl.ds(pl.multiple_of(i * 256, 256), 256)
        r = MID[:, s] + mm_nt(GK[...], wrows(i, CK, 512)) + mm_nt(GV[...], wrows(i, CV, WIDE))
        OWN2[:, s] = r[0:128] * c0 + r[128:256] * c1
        SBO[:, s] = (r[0:128] * c1 + r[128:256] * c0).astype(BF16)

    loop(4, normed_body)
    e_norm = remote(SBO, RB3, ex_s.at[6], ex_r.at[6], sibling)
    e_norm.start()
    r_qgo = scatter2(QGO, r_qgo)
    f_mlp = scatter4(MLP, r_mlp, 1)
    e_norm.wait_recv()

    def ln1_back(i):
        at = pl.ds(pl.multiple_of(c * 128 + i * 32, 32), 32)
        gs = OWN2[rows(i), :] + RB3[rows(i), :].astype(F32)
        part, ggain, gbias = norm_back(gs, X[at, :].astype(F32), gain1)
        OUTV[1, rows(i), :] = (GM[at, :] + part).astype(BF16)
        VA[0:1, :] += ggain
        VA[1:2, :] += gbias

    loop(4, ln1_back)
    put_gin = pltpu.make_async_copy(OUTV.at[1], gin_ref, loc.at[14])
    put_gin.start()
    vectors = jnp.concatenate([jnp.zeros((96, 1024), F32), VA[...], jnp.zeros((24, 1024), F32)], axis=0).T
    tile = slice(VTILE, VTILE + 128)
    Gd[:, :, :, :, tile] = (
        Gd[:, :, :, :, tile].astype(F32) + vectors.reshape(4, 4, 4, 16, 128)
    ).astype(BF16)
    r_vec = scatter0(KV_LATE, r_kv[1])
    r_kv = scatter1(KV_EARLY, r_kv)
    r_qgo = scatter3(QGO, r_qgo)
    scatter1(KV_LATE, r_vec)
    f_mlp = finish(f_mlp, OMG, OMD, ((OMG, CMG), (OMU, CMU)), 1)
    f_qgo = scatter4(QGO, r_qgo, 2)
    r_kv = scatter2(KV, r_kv)
    f_qgo = finish(f_qgo, OQ, OMG, ((OQ, CQ), (OG, CG), (OO, CO)), 2)
    r_kv = scatter3(KV, r_kv)
    f_kv = scatter4(KV, r_kv, 3)
    f_kv = finish(f_kv, 0, OQ, ((OK, CK), (OV, CV)), 3)
    put_out.wait()
    put_gin.wait()
    for where in pending:
        remote(where[2], where[2], where[0], where[1], sibling).wait_send()
    for copy in (e_pack, e_x, e_g, e_sec, e_norm):
        copy.wait_send()
    for copy, out in (f_down, f_mlp, f_qgo, f_kv):
        copy.wait_send()
        out.wait()


def scratch():
    def b(*shape):
        return pltpu.VMEM(shape, BF16)

    def f(*shape):
        return pltpu.VMEM(shape, F32)

    def sem(n):
        return pltpu.SemaphoreType.DMA((n,))

    return [
        b(4, 4, 4, 16, TOTAL), b(4, 4, 4, 16, TOTAL), b(2, 2, 4, 16, TOTAL), b(2, 4, 4, 16, TOTAL),
        b(3, 4, 16, TOTAL), b(3, 16, TOTAL),
        b(256, 1024), b(256, 1024), f(8, 1792), b(2, 8, 1024), b(6, 8, 1728), f(8, 128), f(8, OTOTAL),
        b(2, 128, 1024), b(16, TOTAL), b(2, 16, TOTAL), f(8, 1024), f(8, 1024),
        f(256, 128), f(256, 128),
        b(256, 1024), b(1024, 256), b(1024, 256), b(256, 512), b(256, 512), b(256, 512), b(256, 512),
        b(256, WIDE), b(256, WIDE), f(256, WIDE), b(2, 256, 256), f(2, 256, 256), f(256, WIDE), f(256, WIDE),
        b(REAL, 256), b(REAL, 256), b(3, REAL, 256), b(WIDE, 256), b(WIDE, 256),
        b(256, WIDE), f(256, 1024), b(256, 1024), b(256, 1024), b(128, 1024), b(128, 1024), f(128, 1024),
        b(256, 1024), b(128, 1024), f(128, 1024),
        b(256, 1024), f(256, WIDE), f(256, WIDE), b(256, WIDE), b(256, WIDE), b(256, WIDE),
        f(256, 1024), b(256, WIDE), b(256, 512), b(256, 512), b(256, WIDE),
        f(8, TOTAL), f(8, TOTAL), f(8, TOTAL),
        sem(40), sem(40), sem(8), sem(8), sem(11), sem(11), sem(19),
    ]


def per_device(
    inputs, cotangent, ln1_gain, ln1_bias, w_query, w_key, w_value, w_gate, w_out,
    ln2_gain, ln2_bias, w_mlp_gate, w_mlp_up, w_mlp_down,
):
    cosine, sine = tables()
    vectors = jnp.stack([ln1_gain, ln1_bias, ln2_gain, ln2_bias]).astype(F32)
    vectors = jnp.pad(vectors, ((0, 4), (0, 120)))
    out, gin, pack = pl.pallas_call(
        kernel,
        out_shape=[
            jax.ShapeDtypeStruct((128, 1024), BF16), jax.ShapeDtypeStruct((128, 1024), BF16),
            jax.ShapeDtypeStruct((8, OTOTAL), F32),
        ],
        in_specs=[pl.BlockSpec(memory_space=pl.ANY)] * 13,
        out_specs=[pl.BlockSpec(memory_space=pl.ANY)] * 3,
        scratch_shapes=scratch(),
        compiler_params=pltpu.CompilerParams(
            collective_id=0, has_side_effects=True, vmem_limit_bytes=64 << 20
        ),
        name="block",
    )(
        inputs[0], cotangent[0], vectors, w_query, w_key, w_value, w_gate, w_out.T,
        w_mlp_gate, w_mlp_up, w_mlp_down.T, jnp.asarray(cosine), jnp.asarray(sine),
    )
    gv, gg, go, gmg, gmu, gmd = (pack[:, at : at + 1728] for at in (OV, OG, OO, OMG, OMU, OMD))
    vec = [pack[:, OVEC + 96 + i] for i in range(4)]
    return (
        out[None], gin[None], vec[0], vec[1], pack[:, OQ : OQ + 1024], pack[:, OK : OK + 1024], gv, gg, go.T,
        vec[2], vec[3], gmg, gmu, gmd.T,
    )


def solution(mesh):
    both = ("dp", "seq")
    row, col, vec, tokens = P(both, None), P(None, both), P(both), P("dp", "seq", None)
    return jax.shard_map(
        per_device,
        mesh=mesh,
        in_specs=(tokens, tokens, vec, vec, row, row, row, row, col, vec, vec, row, row, col),
        out_specs=(tokens, tokens, vec, vec, row, row, row, row, col, vec, vec, row, row, col),
        check_vma=False,
    )
```

```python
import functools

import jax
import jax.numpy as jnp
import numpy as np
from jax import lax
from jax.experimental import pallas as pl
from jax.experimental.pallas import tpu as pltpu
from jax.sharding import PartitionSpec as P

MESH = pl.DeviceIdType.MESH
F32 = jnp.float32
BF16 = jnp.bfloat16
EPS = 1e-05
VH = 432

CK, CV, CQ, CG, CO, CMG, CMU, CMD, TOTAL = 0, 512, 1408, 1920, 2816, 3712, 4608, 5504, 6400
WIDE = 896
REAL = 864
VTILE = CV + 768
OVEC, OK, OV, OQ, OG, OO, OMG, OMU, OMD, OTOTAL = (
    0, 128, 1152, 2944, 3968, 5760, 7552, 9344, 11136, 12928,
)


def cut(start, *tiles):
    parts = []
    for part, n in enumerate(tiles):
        parts.append((part, start, 128 * n))
        start += 128 * n
    return tuple(parts)


GATHERS = (cut(CK, 4, 4, 3), cut(CQ, 4, 3, 4), cut(CO, 3, 1, 3), cut(CMG, 6, 3, 5), cut(CMD, 2, 3, 2))
KV = cut(CK, 4, 4, 3)
KV_EARLY, KV_LATE = cut(CK, 4, 4, 2), ((2, VTILE, 128),)
QG, OUT, MLP, DOWN = cut(CQ, 5, 3, 3), cut(CO, 2, 2, 3), cut(CMG, 6, 2, 6), cut(CMD, 3, 2, 2)
PIECES = ((slice(0, 224), 0), (slice(224, 432), 0), (slice(432, 656), 1), (slice(656, 864), 1))
ORDERS = (("x", "y", "z"), ("y", "z", "x"), ("z", "x", "y"))
ZYX = ("z", "y", "x")


def tables():
    half = 128
    inverse = np.power(10000.0, -np.arange(half, dtype=np.float64) / half)
    angles = np.arange(1024, dtype=np.float64)[:, None] * inverse[None, :]
    return (
        np.cos(angles).astype(np.float32).reshape(4, 256, half),
        np.sin(angles).astype(np.float32).reshape(4, 256, half),
    )


def mm(a, b):
    return lax.dot_general(a, b, (((1,), (0,)), ((), ())), preferred_element_type=F32)


def mm_nt(a, b):
    return lax.dot_general(a, b, (((1,), (1,)), ((), ())), preferred_element_type=F32)


def loop(n, body):
    def step(i, carry):
        body(i)
        return carry

    lax.fori_loop(0, n, step, 0)


def kernel(
    x_in, g_in, vec_in, wq_in, wk_in, wv_in, wg_in, wo_in, wmg_in, wmu_in, wmd_in, cos_in, sin_in,
    out_ref, gin_ref, pack_ref, *scratch,
):
    (
        W, Gd, RA, RB1, R2, R3, X, G, WS, IN8, INW, INV, PACK, OUTV, PSEND, PRECV, VEC, VA, COS, SIN, STAT,
        NORM, NORMT, TT, Q, QS, K, KW, V, GGP, GATE, WT, MASK, MIX, GRP,
        UT, TOT, STATES, CT, GUT, GATED, MID, SB, RB, SBO, RBO, OWN1, RB2, RB3, OWN2,
        SEC, ACT, BCT, HID, GGL, GUL, GM, GMX, GQ, GK, GV, FSEND, FRECV, KEEP,
        way_s, way_r, st_s, st_r, ex_s, ex_r, loc,
    ) = scratch
    S1, S2, VT, RSTD, GML = RB1.at[0], R2.at[0], TT.at[0:WIDE], MIX, SEC
    dp = lax.axis_index("dp")
    sq = lax.axis_index("seq")
    me = {"z": dp // 4, "y": dp % 4, "x": sq // 2}
    c = sq % 2
    c0 = (c == 0).astype(F32)
    c1 = (c == 1).astype(F32)

    def shifted(axis, k):
        p = dict(me)
        p[axis] = (me[axis] + k) % 4
        return p

    def device(p, core):
        return (p["z"] * 4 + p["y"], p["x"] * 2 + core)

    sibling = device(me, 1 - c)

    def remote(src, dst, ss, rs, dev):
        return pltpu.make_async_remote_copy(
            src_ref=src, dst_ref=dst, send_sem=ss, recv_sem=rs, device_id=dev, device_id_type=MESH
        )

    rows_own = pl.ds(pl.multiple_of(c * 128, 128), 128)
    rows_sib = pl.ds(pl.multiple_of((1 - c) * 128, 128), 128)
    fetch = [
        pltpu.make_async_copy(src, dst, loc.at[i])
        for i, (src, dst) in enumerate(
            (
                (wq_in, IN8.at[0]), (wk_in, IN8.at[1]), (wv_in, INW.at[0]), (wg_in, INW.at[1]),
                (wo_in, INW.at[2]), (wmg_in, INW.at[3]), (wmu_in, INW.at[4]), (wmd_in, INW.at[5]),
                (vec_in, INV), (x_in, X.at[rows_own, :]), (g_in, G.at[rows_own, :]),
                (cos_in.at[me["x"]], COS), (sin_in.at[me["x"]], SIN),
            )
        )
    ]
    for copy in fetch:
        copy.start()
    barrier = pltpu.get_barrier_semaphore()
    pl.semaphore_signal(barrier, inc=1, device_id=sibling, device_id_type=MESH)
    for axis in ZYX:
        for k in (1, 2, 3):
            pl.semaphore_signal(
                barrier, inc=1, device_id=device(shifted(axis, k), c), device_id_type=MESH
            )

    def put(ref, col, own):
        both = jnp.concatenate([own * c0, own * c1], axis=0)
        ref[:, col : col + own.shape[1]] = both.astype(BF16)

    def pack(col, h0, h1):
        put(PRECV.at[0], col, h0 * c0 + h1 * c1)
        put(PSEND, col, h0 * c1 + h1 * c0)

    for copy in fetch[:9]:
        copy.wait()
    for i, col in enumerate((CQ, CK)):
        w = IN8[i].astype(F32)
        pack(col, w[:, :512], w[:, 512:])
    lane = lax.broadcasted_iota(jnp.int32, (8, WIDE), 1)
    for i, col in enumerate((CV, CG, CO, CMG, CMU, CMD)):
        WS[:, 1664:1792] = jnp.zeros((8, 128), F32)
        WS[:, :1728] = INW[i].astype(F32)
        h0 = jnp.where(lane < REAL, WS[:, :WIDE], 0.0)
        h1 = pltpu.roll(WS[:, 768:1792], 1024 - 96, 1)[:, :WIDE]
        h1 = jnp.where(lane < REAL, h1, 0.0)
        if col == CV:
            v = jnp.concatenate([INV[...], jnp.zeros((120, 128), F32)], axis=0).T
            v = pltpu.roll(v[0:8, :], 96, 1)
            v = jnp.concatenate([jnp.zeros((8, 768), F32), v], axis=1)
            h0 = h0 + v
            h1 = h1 + v
        pack(col, h0, h1)
    pl.semaphore_wait(barrier, 10)

    e_pack = remote(PSEND, PRECV.at[1], ex_s.at[0], ex_r.at[0], sibling)
    e_x = remote(X.at[rows_own, :], X.at[rows_own, :], ex_s.at[1], ex_r.at[1], sibling)
    e_g = remote(G.at[rows_own, :], G.at[rows_own, :], ex_s.at[2], ex_r.at[2], sibling)
    e_pack.start()
    fetch[9].wait()
    e_x.start()
    fetch[10].wait()
    e_g.start()
    e_pack.wait_recv()
    for col in range(0, TOTAL, 1280):
        s = pl.ds(col, 1280)
        W[me["z"], me["y"], me["x"], :, s] = (
            PRECV[0, :, s].astype(F32) + PRECV[1, :, s].astype(F32)
        ).astype(BF16)

    pending = []
    count = [0]

    def stage(total):
        count[0] += 1
        return way_s.at[count[0] - 1], way_r.at[count[0] - 1], total

    def send(where, src, dst, dev):
        remote(src, dst, where[0], where[1], dev).start()

    def arrived(where):
        ss, rs, total = where
        remote(total, total, ss, rs, sibling).wait_recv()
        pending.append(where)

    def columns(parts):
        return pl.ds(parts[0][1], sum(n for _, _, n in parts))

    def gather(group, phase, forward=False):
        s = columns(GATHERS[group])
        if phase == 0:
            where = stage(W.at[0, 0, 0:3, :, s])
        elif phase == 1:
            where = stage(W.at[0, 0:3, :, :, s])
        else:
            where = stage(W.at[0, :, :, :, s] if forward else W.at[0:2, :, :, :, s])
        for part, col, n in GATHERS[group]:
            order = ORDERS[part]
            axis = order[phase]
            for i, k in enumerate((1, 3) if phase == 2 else (1, 2, 3)):
                idx = []
                for a in ZYX:
                    if a == axis and forward:
                        idx.append((me[a] - k) % 4)
                    elif a in order[:phase]:
                        idx.append(slice(None))
                    else:
                        idx.append(me[a])
                if forward:
                    at = 0 if axis != "z" else 1
                    idx[at] = pl.ds(2 * i, 2)
                src = W.at[tuple(idx) + (slice(None), pl.ds(col, n))]
                send(where, src, src, device(shifted(axis, k), c))
        return where

    p1 = [gather(g, 0) for g in range(5)]
    p2, p3, p4 = {}, {}, {}
    def step1(g):
        arrived(p1[g])
        p2[g] = gather(g, 1)

    def step2(g):
        arrived(p2[g])
        p3[g] = gather(g, 2)

    def step3(g):
        arrived(p3[g])
        p4[g] = gather(g, 2, True)

    step1(0)
    step1(2)
    step1(1)
    step2(0)
    step2(1)

    e_x.wait_recv()
    e_g.wait_recv()
    fetch[11].wait()
    fetch[12].wait()

    def wcols(col, n):
        return W[:, :, :, :, col : col + n].reshape(1024, n)

    def wrows(i, col, n):
        return W[i, :, :, :, col : col + n].reshape(256, n)

    def fwd(a, col, n, emit):
        for at in range(0, n, 256):
            w = min(256, n - at)
            emit(at, w, mm(a[...], wcols(col + at, w)))

    def grad(at, b, col):
        n = b.shape[1]

        def body(i):
            r = mm(at[pl.ds(pl.multiple_of(i * 256, 256), 256), :], b[...])
            Gd[i, :, :, :, col : col + n] = r.astype(BF16).reshape(4, 4, 16, n)

        loop(4, body)

    def rows(i, n=32):
        return pl.ds(pl.multiple_of(i * n, n), n)

    lanes = lax.broadcasted_iota(jnp.int32, (32, WIDE), 1)
    in0 = lanes < VH
    in1 = (lanes >= VH) & (lanes < REAL)
    real = lanes < REAL

    def log_gamma(hh):
        g0 = float(np.log(1.0 - 2.0 ** (-5.0 - hh)))
        g1 = float(np.log(1.0 - 2.0 ** (-7.0 - hh)))
        return jnp.where(c == 0, jnp.float32(g0), jnp.float32(g1))

    lg = [log_gamma(0), log_gamma(1)]

    def mask_body(i):
        ii = lax.broadcasted_iota(jnp.int32, (32, 256), 0) + i * 32
        jj = lax.broadcasted_iota(jnp.int32, (32, 256), 1)
        d = (ii - jj).astype(F32)
        for hh in range(2):
            MASK[hh, rows(i), :] = jnp.where(d >= 0, jnp.exp(jnp.maximum(d, 0.0) * lg[hh]), 0.0)

    loop(8, mask_body)
    VA[...] = jnp.zeros_like(VA)

    def norm(v):
        mean = jnp.mean(v, axis=-1, keepdims=True)
        center = v - mean
        spread = jnp.mean(center * center, axis=-1, keepdims=True)
        rstd = lax.rsqrt(spread + EPS)
        return center * rstd, rstd, mean

    def ln1_stats(i):
        xh, rstd, mean = norm(X[rows(i), :].astype(F32))
        GM[rows(i), :] = xh
        STAT[0, rows(i), :] = jnp.broadcast_to(mean, (32, 128))
        STAT[1, rows(i), :] = jnp.broadcast_to(rstd, (32, 128))

    loop(8, ln1_stats)
    step3(0)
    step1(3)
    step3(1)
    step2(2)
    arrived(p4[0])
    VEC[...] = wcols(VTILE, 128).astype(F32).T[96:104, :]
    gain1, bias1 = VEC[0:1, :], VEC[1:2, :]
    gain2, bias2 = VEC[2:3, :], VEC[3:4, :]

    def ln1(i):
        NORM[rows(i), :] = (GM[rows(i), :] * gain1 + bias1).astype(BF16)

    loop(8, ln1)

    def transpose(src, dst):
        dst[...] = src[...].T

    def rotated(dst, dst2, offset, sign, scale):
        def emit(at, w, r):
            hh = at // 256
            u, z = r[:, :128], r[:, 128:]
            co, si = COS[...], SIN[...]
            a0 = ((u * co - z * si) * scale).astype(BF16)
            a1 = ((u * si + z * co) * scale).astype(BF16)
            spot = lax.broadcasted_iota(jnp.int32, (256, 128), 0).astype(F32)
            sc = jnp.exp((spot * sign + offset) * lg[hh])
            dst[:, at : at + 128] = a0
            dst[:, at + 128 : at + 256] = a1
            dst2[:, at : at + 128] = (a0.astype(F32) * sc).astype(BF16)
            dst2[:, at + 128 : at + 256] = (a1.astype(F32) * sc).astype(BF16)

        return emit

    fwd(NORM, CK, 512, rotated(K, KW, 255.0, -1.0, 0.0625))

    def emit_v(at, w, r):
        col = lax.broadcasted_iota(jnp.int32, (256, w), 1) + at
        V[:, at : at + w] = jnp.where(col < REAL, r, 0.0).astype(BF16)

    fwd(NORM, CV, WIDE, emit_v)
    transpose(V, VT)
    for hh in range(2):
        r = mm(VT[VH * hh : VH * (hh + 1), :], KW[:, 256 * hh : 256 * (hh + 1)])
        UT[VH * hh : VH * (hh + 1), :] = r.astype(BF16)

    def states(src, base, back):
        x = me["x"]
        near = dict(me, x=x + 1 - 2 * (x % 2))
        far = dict(me, x=3 - x)
        low = x < 2
        sends = (x != 0) if back else (x != 3)
        gets = (x != 1) if back else (x != 2)
        passes = ~low if back else low
        steps = []
        for i, (at, hh) in enumerate(PIECES):
            t = base + i
            slot = 1 if back else 0
            one = remote(src.at[at], STATES.at[slot, at], st_s.at[t], st_r.at[t], device(near, c))
            pl.when(sends)(one.start)
            steps.append(one)

        def second(i):
            at, hh = PIECES[i]
            t = base + 4 + i
            two = remote(TOT.at[at], STATES.at[2, at], st_s.at[t], st_r.at[t], device(far, c))

            def total():
                steps[i].wait_recv()
                own = src[at, :].astype(F32)
                got = STATES[slot, at, :].astype(F32)
                g = jnp.exp(256.0 * lg[hh])
                first = (x % 2 == 1) if back else (x % 2 == 0)
                TOT[at, :] = jnp.where(first, own * g + got, own + got * g).astype(BF16)
                two.start()

            pl.when(passes)(total)
            return two

        def finish(dst):
            dst[...] = jnp.zeros_like(dst)
            for i, two in enumerate(twos):
                at, hh = PIECES[i]
                g = jnp.exp(256.0 * lg[hh])

                def single():
                    dst[at, :] = STATES[slot, at, :]

                def double():
                    two.wait_recv()
                    dst[at, :] = STATES[2, at, :]

                def triple():
                    steps[i].wait_recv()
                    two.wait_recv()
                    total = STATES[2, at, :].astype(F32) * g
                    dst[at, :] = (total + STATES[slot, at, :].astype(F32)).astype(BF16)

                one, pair, three = (2, 1, 0) if back else (1, 2, 3)
                pl.when(x == one)(single)
                pl.when(x == pair)(double)
                pl.when(x == three)(triple)

        def sent():
            for one, two in zip(steps, twos):
                pl.when(sends)(one.wait_send)
                pl.when(passes)(two.wait_send)

        twos = []

        def middle(*pieces):
            twos.extend(second(i) for i in pieces)

        return middle, finish, sent

    u_middle, u_finish, u_sent = states(UT, 0, False)
    step1(4)
    step2(3)
    u_middle(0, 1, 2, 3)
    step3(2)
    transpose(NORM, NORMT)
    transpose(G, TT)
    step2(4)
    arrived(p4[1])
    fwd(NORM, CQ, 512, rotated(Q, QS, 1.0, 1.0, 1.0))

    for hh in range(2):
        raw = mm_nt(Q[:, 256 * hh : 256 * (hh + 1)], K[:, 256 * hh : 256 * (hh + 1)])
        WT[hh] = (raw * MASK[hh]).astype(BF16)

    def join(dst, h0, h1):
        pick = lax.broadcasted_iota(jnp.int32, (256, 128), 1) < VH - 384
        dst[:, 0:384] = h0[:, :384]
        dst[:, 384:512] = jnp.where(pick, h0[:, 384:512], h1[:, :128])
        dst[:, 512:896] = h1[:, 128:512]

    join(MIX, mm(WT[0], V[:, 0:512]), mm(WT[1], V[:, 384:896]))

    def emit_gate(at, w, r):
        GATE[:, at : at + w] = r

    fwd(NORM, CG, WIDE, emit_gate)
    u_finish(CT)
    step3(3)
    join(GRP, mm_nt(QS[:, 0:256], CT[0:512, :]), mm_nt(QS[:, 256:512], CT[384:896, :]))

    def heads_mean(v):
        m0 = jnp.sum(jnp.where(in0, v, 0.0), axis=-1, keepdims=True) * (1.0 / VH)
        m1 = jnp.sum(jnp.where(in1, v, 0.0), axis=-1, keepdims=True) * (1.0 / VH)
        return jnp.where(in0, m0, m1)

    def group_norm(i):
        m = MIX[rows(i), :] + GRP[rows(i), :]
        center = m - heads_mean(m)
        rstd = lax.rsqrt(heads_mean(center * center) + EPS)
        grouped = jnp.where(real, center * rstd, 0.0)
        GRP[rows(i), :] = grouped
        RSTD[rows(i), :] = rstd
        gate = GATE[rows(i), :]
        GATED[rows(i), :] = (gate * jax.nn.sigmoid(gate) * grouped).astype(BF16)

    loop(8, group_norm)
    arrived(p4[2])

    def out_body(i):
        r = mm_nt(GATED[...], wrows(i, CO, WIDE))
        s = pl.ds(pl.multiple_of(i * 256, 256), 256)
        MID[:, s] = r
        SB[:, s] = r.astype(BF16)
        remote(SB.at[:, s], RB.at[:, s], ex_s.at[3], ex_r.at[3], sibling).start()

    loop(4, out_body)
    e_mid = remote(SB, RB, ex_s.at[3], ex_r.at[3], sibling)
    step3(4)
    e_mid.wait_recv()

    def ln2(i):
        m = X[rows(i), :].astype(F32) + MID[rows(i), :] + RB[rows(i), :].astype(F32)
        MID[rows(i), :] = m
        xh, rstd, mean = norm(m)
        STAT[2, rows(i), :] = jnp.broadcast_to(mean, (32, 128))
        STAT[3, rows(i), :] = jnp.broadcast_to(rstd, (32, 128))
        SEC[rows(i), :] = (xh * gain2 + bias2).astype(BF16)

    loop(8, ln2)
    arrived(p4[3])

    def emit_act(at, w, r):
        ACT[:, at : at + w] = r

    def emit_bct(at, w, r):
        BCT[:, at : at + w] = r

    fwd(SEC, CMG, WIDE, emit_act)
    fwd(SEC, CMU, WIDE, emit_bct)

    def gelu(i):
        g = ACT[rows(i), :]
        u = BCT[rows(i), :]
        cdf = 0.5 * (1.0 + lax.erf(g * 0.7071067811865476))
        ge = g * cdf
        HID[rows(i), :] = (ge * u).astype(BF16)
        BCT[rows(i), :] = ge
        ACT[rows(i), :] = (cdf + g * jnp.exp(-0.5 * g * g) * 0.3989422804014327) * u

    loop(8, gelu)
    arrived(p4[4])

    def place(axes, where):
        return tuple(where.get(a, slice(None)) for a in axes)

    def others(part, phase):
        order = ORDERS[part][::-1]
        return order[phase], [a for a in ZYX if a not in order[: phase + 1]], [a for a in ZYX if a not in order[:phase]]

    def scatter0(parts, late=None):
        s = columns(parts)
        early = stage(RA.at[:, :, :, :, s])
        late = late or stage(RB1.at[:, :, :, :, s])
        for where in (early, late):
            for part, col, n in parts:
                axis, rest, left = others(part, 0)
                s = (slice(None), pl.ds(col, n))
                for i, k in enumerate((1, 3)):
                    dev = device(shifted(axis, k), c)
                    if where is early:
                        src = Gd.at[place(left, {axis: (me[axis] + 2) % 4, rest[0]: pl.ds(2 * i, 2)}) + s]
                        send(where, src, RA.at[(i, slice(None), slice(None)) + s], dev)
                    else:
                        near = pl.ds(2 - 2 * i, 2)
                        src = Gd.at[place(left, {axis: (me[axis] + k) % 4, rest[0]: near}) + s]
                        send(where, src, RB1.at[(i, near, slice(None)) + s], dev)
        return early, late

    def scatter1(parts, where):
        early, late = where
        arrived(early)
        for part, col, n in parts:
            axis, rest, left = others(part, 0)
            s = (slice(None), pl.ds(col, n))
            for i, k in enumerate((1, 3)):

                def body(j):
                    own = Gd[place(left, {axis: (me[axis] + k) % 4, rest[0]: 2 * i + j}) + s]
                    at = (i, j, slice(None)) + s
                    RA[at] = (own.astype(F32) + RA[at].astype(F32)).astype(BF16)

                loop(2, body)
                src = RA.at[(i, slice(None), slice(None)) + s]
                dst = RB1.at[(i, pl.ds(2 * i, 2), slice(None)) + s]
                send(late, src, dst, device(shifted(axis, k), c))
        return late

    def scatter2(parts, late):
        arrived(late)
        where = stage(R2.at[:, :, :, columns(parts)])
        for part, col, n in parts:
            axis, rest, left = others(part, 0)
            s = (slice(None), pl.ds(col, n))

            def body(j):
                own = Gd[place(left, {axis: me[axis], rest[0]: j}) + s].astype(F32)
                at = (j, slice(None)) + s
                RB1[(0,) + at] = (own + RB1[(0,) + at].astype(F32) + RB1[(1,) + at].astype(F32)).astype(BF16)

            loop(4, body)
            axis, rest, left = others(part, 1)
            for k in (1, 2, 3):
                to = shifted(axis, k)
                src = S1.at[place(left, {axis: to[axis]}) + s]
                send(where, src, R2.at[(k - 1, slice(None)) + s], device(to, c))
        return where

    def scatter3(parts, where):
        arrived(where)
        where = stage(R3.at[:, :, columns(parts)])
        for part, col, n in parts:
            axis, rest, left = others(part, 1)
            s = (slice(None), pl.ds(col, n))
            t = S1[place(left, {axis: me[axis]}) + s].astype(F32)
            for k in range(3):
                t = t + R2[(k, slice(None)) + s].astype(F32)
            S2[(slice(None),) + s] = t.astype(BF16)
            axis, rest, left = others(part, 2)
            for k in (1, 2, 3):
                to = shifted(axis, k)
                send(where, S2.at[(to[axis],) + s], R3.at[(k - 1,) + s], device(to, c))
        return where

    def scatter4(parts, where, i):
        arrived(where)
        for part, col, n in parts:
            axis, rest, left = others(part, 2)
            s = (slice(None), pl.ds(col, n))
            t = S2[(me[axis],) + s].astype(F32)
            for k in range(3):
                t = t + R3[(k,) + s].astype(F32)
            KEEP[:, s[1]] = t[0:8, :] * c0 + t[8:16, :] * c1
            FSEND[:, s[1]] = t[0:8, :] * c1 + t[8:16, :] * c0
        s = columns(parts)
        copy = remote(FSEND.at[:, s], FRECV.at[:, s], ex_s.at[7 + i], ex_r.at[7 + i], sibling)
        copy.start()
        return copy

    def halves(col, n):
        keep = KEEP[:, col : col + n]
        got = FRECV[:, col : col + n]
        return keep * c0 + got * c1, keep * c1 + got * c0

    def finish(copy, first, last, where, i):
        copy.wait_recv()
        if first == OVEC:
            lo, hi = halves(VTILE, 128)
            PACK[:, OVEC:OK] = lo + hi
        for at, col in where:
            if col in (CQ, CK):
                lo, hi = halves(col, 512)
                PACK[:, at : at + 512] = lo
                PACK[:, at + 512 : at + 1024] = hi
            else:
                lo, hi = halves(col, WIDE)
                moved = pltpu.roll(jnp.concatenate([hi, jnp.zeros((8, 128), F32)], axis=1), 96, 1)
                first96 = lax.broadcasted_iota(jnp.int32, (8, 128), 1) < 96
                PACK[:, at : at + 768] = lo[:, 0:768]
                PACK[:, at + 768 : at + 896] = jnp.where(first96, lo[:, 768:896], moved[:, 0:128])
                PACK[:, at + 896 : at + 1792] = moved[:, 128:1024]
        out = pltpu.make_async_copy(PACK.at[:, first:last], pack_ref.at[:, first:last], loc.at[15 + i])
        out.start()
        return copy, out

    def emit_hidden(at, w, r):
        GGL[:, at : at + w] = (r * ACT[:, at : at + w]).astype(BF16)
        GUL[:, at : at + w] = (r * BCT[:, at : at + w]).astype(BF16)

    grad(TT, HID, CMD)
    r_down = scatter0(DOWN)
    fwd(G, CMD, WIDE, emit_hidden)
    transpose(SEC, TT)
    grad(TT, GGL, CMG)
    e_mid.wait_send()

    def second_body(i):
        r = mm_nt(GGL[...], wrows(i, CMG, WIDE)) + mm_nt(GUL[...], wrows(i, CMU, WIDE))
        s = pl.ds(pl.multiple_of(i * 256, 256), 256)
        GM[:, s] = r
        SB[:, s] = r.astype(BF16)
        remote(SB.at[:, s], RB2.at[:, s], ex_s.at[5], ex_r.at[5], sibling).start()

    loop(4, second_body)
    e_sec = remote(SB, RB2, ex_s.at[5], ex_r.at[5], sibling)
    grad(TT, GUL, CMU)
    r_mlp = scatter0(MLP)
    r_down = scatter1(DOWN, r_down)
    e_sec.wait_recv()

    def norm_back(gs, v, gain, at, which):
        rstd = STAT[which + 1, at, 0:1]
        xh = (v - STAT[which, at, 0:1]) * rstd
        gx = gs * gain
        m0 = jnp.mean(gx, axis=-1, keepdims=True)
        m1 = jnp.mean(gx * xh, axis=-1, keepdims=True)
        return rstd * (gx - m0 - xh * m1), jnp.sum(gs * xh, axis=0, keepdims=True), jnp.sum(gs, axis=0, keepdims=True)

    def ln2_back(i):
        gs = GM[rows(i), :] + RB2[rows(i), :].astype(F32)
        part, ggain, gbias = norm_back(gs, MID[rows(i), :], gain2, rows(i), 2)
        gm = G[rows(i), :].astype(F32) + part
        GM[rows(i), :] = gm
        GML[rows(i), :] = gm.astype(BF16)
        mine = (i // 4 == c).astype(F32)
        VA[2:3, :] += ggain * mine
        VA[3:4, :] += gbias * mine

    loop(8, ln2_back)
    transpose(GML, TT)
    grad(TT, GATED, CO)

    def emit_gated(at, w, r):
        ACT[:, at : at + w] = r

    fwd(GML, CO, WIDE, emit_gated)
    r_out = scatter0(OUT)

    def group_back(i):
        gr = ACT[rows(i), :]
        z = GATE[rows(i), :]
        sg = jax.nn.sigmoid(z)
        grp = GRP[rows(i), :]
        GGP[rows(i), :] = (gr * (sg * (1.0 + z * (1.0 - sg))) * grp).astype(BF16)
        gg = gr * (z * sg)
        gmx = RSTD[rows(i), :] * (gg - heads_mean(gg) - grp * heads_mean(gg * grp))
        GMX[rows(i), :] = jnp.where(real, gmx, 0.0).astype(BF16)

    loop(8, group_back)
    r_mlp = scatter1(MLP, r_mlp)
    transpose(GMX, VT)
    u_sent()
    for hh in range(2):
        r = mm(VT[VH * hh : VH * (hh + 1), :], QS[:, 256 * hh : 256 * (hh + 1)])
        UT[VH * hh : VH * (hh + 1), :] = r.astype(BF16)
    c_middle, c_finish, c_sent = states(UT, 8, True)
    wide = lax.broadcasted_iota(jnp.int32, (256, 512), 1)
    windows = (slice(0, 512), slice(384, 896))

    def window(ref, hh):
        a = ref[:, windows[hh]]
        keep = wide < VH if hh == 0 else wide >= VH - 384
        return jnp.where(keep, a, jnp.zeros_like(a))

    def spots(hh, offset, sign):
        spot = lax.broadcasted_iota(jnp.int32, (256, 128), 0).astype(F32)
        return jnp.exp((spot * sign + offset) * lg[hh])

    def unrotated(dst, src, hh, cross, offset, sign, scale):
        sc = spots(hh, offset, sign)
        co, si = COS[...], SIN[...]
        a, b = slice(256 * hh, 256 * hh + 128), slice(256 * hh + 128, 256 * hh + 256)
        u = (src[:, a] + cross[:, :128] * sc) * scale
        z = (src[:, b] + cross[:, 128:] * sc) * scale
        dst[:, a] = (u * co + z * si).astype(BF16)
        dst[:, b] = (z * co - u * si).astype(BF16)

    gvi = []
    for hh in range(2):
        h = slice(256 * hh, 256 * (hh + 1))
        gm = window(GMX, hh)
        vw = V[:, windows[hh]]
        graw = (mm_nt(gm, vw) * MASK[hh]).astype(BF16)
        ACT[:, h] = mm(graw, K[:, h])
        BCT[:, h] = mm(graw.T, Q[:, h])
        gvi.append(mm(WT[hh].T, gm))
        unrotated(GQ, ACT, hh, mm(gm, CT[windows[hh], :]), 1.0, 1.0, 1.0)
    join(MIX, gvi[0], gvi[1])
    grad(NORMT, GGP, CG)
    grad(NORMT, GQ, CQ)
    r_down = scatter2(DOWN, r_down)
    r_qg = scatter0(QG)
    c_middle(0, 1)

    def down_body(i):
        r = mm_nt(HID[...], wrows(i, CMD, WIDE))
        s = pl.ds(pl.multiple_of(i * 256, 256), 256)
        OWN1[:, s] = r[0:128] * c0 + r[128:256] * c1
        SBO[:, s] = (r[0:128] * c1 + r[128:256] * c0).astype(BF16)

    loop(4, down_body)
    e_out = remote(SBO, RBO, ex_s.at[4], ex_r.at[4], sibling)
    e_out.start()
    c_middle(2, 3)
    r_mlp = scatter2(MLP, r_mlp)
    e_out.wait_recv()
    OUTV[0] = (MID[rows_own, :] + OWN1[...] + RBO[...].astype(F32)).astype(BF16)
    put_out = pltpu.make_async_copy(OUTV.at[0], out_ref, loc.at[13])
    put_out.start()

    def normed_first(i):
        r = mm_nt(GQ[...], wrows(i, CQ, 512)) + mm_nt(GGP[...], wrows(i, CG, WIDE))
        MID[:, pl.ds(pl.multiple_of(i * 256, 256), 256)] = r

    loop(4, normed_first)
    r_qg = scatter1(QG, r_qg)
    c_finish(GUT)

    gvs = []
    for hh in range(2):
        h = slice(256 * hh, 256 * (hh + 1))
        unrotated(GK, BCT, hh, mm(window(V, hh), GUT[windows[hh], :]), 255.0, -1.0, 0.0625)
        gvs.append(mm_nt(KW[:, h], GUT[windows[hh], :]))
    join(ACT, gvs[0], gvs[1])
    GV[...] = (MIX[...] + ACT[...]).astype(BF16)
    grad(NORMT, GV, CV)
    grad(NORMT, GK, CK)
    r_kv = scatter0(KV_EARLY, stage(RB1.at[:, :, :, :, columns(KV)]))
    e_out.wait_send()

    def normed_body(i):
        s = pl.ds(pl.multiple_of(i * 256, 256), 256)
        r = MID[:, s] + mm_nt(GK[...], wrows(i, CK, 512)) + mm_nt(GV[...], wrows(i, CV, WIDE))
        OWN2[:, s] = r[0:128] * c0 + r[128:256] * c1
        SBO[:, s] = (r[0:128] * c1 + r[128:256] * c0).astype(BF16)
        remote(SBO.at[:, s], RB3.at[:, s], ex_s.at[6], ex_r.at[6], sibling).start()

    loop(4, normed_body)
    e_norm = remote(SBO, RB3, ex_s.at[6], ex_r.at[6], sibling)
    r_out = scatter1(OUT, r_out)
    e_norm.wait_recv()

    def ln1_back(i):
        at = pl.ds(pl.multiple_of(c * 128 + i * 32, 32), 32)
        gs = OWN2[rows(i), :] + RB3[rows(i), :].astype(F32)
        part, ggain, gbias = norm_back(gs, X[at, :].astype(F32), gain1, at, 0)
        OUTV[1, rows(i), :] = (GM[at, :] + part).astype(BF16)
        VA[0:1, :] += ggain
        VA[1:2, :] += gbias

    loop(4, ln1_back)
    put_gin = pltpu.make_async_copy(OUTV.at[1], gin_ref, loc.at[14])
    put_gin.start()
    vectors = jnp.concatenate([jnp.zeros((96, 1024), F32), VA[...], jnp.zeros((24, 1024), F32)], axis=0).T
    tile = slice(VTILE, VTILE + 128)
    Gd[:, :, :, :, tile] = (
        Gd[:, :, :, :, tile].astype(F32) + vectors.reshape(4, 4, 4, 16, 128)
    ).astype(BF16)
    r_vec = scatter0(KV_LATE, r_kv[1])
    r_kv = scatter1(KV_EARLY, r_kv)
    scatter1(KV_LATE, r_vec)
    r_qg = scatter2(QG, r_qg)
    r_out = scatter2(OUT, r_out)
    r_kv = scatter2(KV, r_kv)
    r_mlp = scatter3(MLP, r_mlp)
    r_qg = scatter3(QG, r_qg)
    r_down = scatter3(DOWN, r_down)
    r_out = scatter3(OUT, r_out)
    r_kv = scatter3(KV, r_kv)
    f_out = scatter4(OUT, r_out, 2)
    f_down = scatter4(DOWN, r_down, 0)
    f_mlp = scatter4(MLP, r_mlp, 1)
    f_qg = scatter4(QG, r_qg, 3)
    f_out = finish(f_out, OO, OMG, ((OO, CO),), 2)
    f_down = finish(f_down, OMD, OTOTAL, ((OMD, CMD),), 0)
    f_mlp = finish(f_mlp, OMG, OMD, ((OMG, CMG), (OMU, CMU)), 1)
    f_kv = scatter4(KV, r_kv, 4)
    f_qg = finish(f_qg, OQ, OO, ((OQ, CQ), (OG, CG)), 3)
    f_kv = finish(f_kv, 0, OQ, ((OK, CK), (OV, CV)), 4)
    c_sent()
    put_out.wait()
    put_gin.wait()
    for where in pending:
        remote(where[2], where[2], where[0], where[1], sibling).wait_send()
    for copy in (e_pack, e_x, e_g, e_sec, e_norm):
        copy.wait_send()
    for copy, out in (f_down, f_mlp, f_out, f_qg, f_kv):
        copy.wait_send()
        out.wait()


def scratch():
    def b(*shape):
        return pltpu.VMEM(shape, BF16)

    def f(*shape):
        return pltpu.VMEM(shape, F32)

    def sem(n):
        return pltpu.SemaphoreType.DMA((n,))

    return [
        b(4, 4, 4, 16, TOTAL), b(4, 4, 4, 16, TOTAL), b(2, 2, 4, 16, TOTAL), b(2, 4, 4, 16, TOTAL),
        b(3, 4, 16, TOTAL), b(3, 16, TOTAL),
        b(256, 1024), b(256, 1024), f(8, 1792), b(2, 8, 1024), b(6, 8, 1728), f(8, 128), f(8, OTOTAL),
        b(2, 128, 1024), b(16, TOTAL), b(2, 16, TOTAL), f(8, 1024), f(8, 1024),
        f(256, 128), f(256, 128), f(4, 256, 128),
        b(256, 1024), b(1024, 256), b(1024, 256), b(256, 512), b(256, 512), b(256, 512), b(256, 512),
        b(256, WIDE), b(256, WIDE), f(256, WIDE), b(2, 256, 256), f(2, 256, 256), f(256, WIDE), f(256, WIDE),
        b(REAL, 256), b(REAL, 256), b(3, REAL, 256), b(WIDE, 256), b(WIDE, 256),
        b(256, WIDE), f(256, 1024), b(256, 1024), b(256, 1024), b(128, 1024), b(128, 1024), f(128, 1024),
        b(256, 1024), b(128, 1024), f(128, 1024),
        b(256, 1024), f(256, WIDE), f(256, WIDE), b(256, WIDE), b(256, WIDE), b(256, WIDE),
        f(256, 1024), b(256, WIDE), b(256, 512), b(256, 512), b(256, WIDE),
        f(8, TOTAL), f(8, TOTAL), f(8, TOTAL),
        sem(44), sem(44), sem(16), sem(16), sem(12), sem(12), sem(20),
    ]


def per_device(
    inputs, cotangent, ln1_gain, ln1_bias, w_query, w_key, w_value, w_gate, w_out,
    ln2_gain, ln2_bias, w_mlp_gate, w_mlp_up, w_mlp_down,
):
    cosine, sine = tables()
    vectors = jnp.stack([ln1_gain, ln1_bias, ln2_gain, ln2_bias]).astype(F32)
    vectors = jnp.pad(vectors, ((0, 4), (0, 120)))
    out, gin, pack = pl.pallas_call(
        kernel,
        out_shape=[
            jax.ShapeDtypeStruct((128, 1024), BF16), jax.ShapeDtypeStruct((128, 1024), BF16),
            jax.ShapeDtypeStruct((8, OTOTAL), F32),
        ],
        in_specs=[pl.BlockSpec(memory_space=pl.ANY)] * 13,
        out_specs=[pl.BlockSpec(memory_space=pl.ANY)] * 3,
        scratch_shapes=scratch(),
        compiler_params=pltpu.CompilerParams(
            collective_id=0, has_side_effects=True, vmem_limit_bytes=64 << 20
        ),
        name="block",
    )(
        inputs[0], cotangent[0], vectors, w_query, w_key, w_value, w_gate, w_out.T,
        w_mlp_gate, w_mlp_up, w_mlp_down.T, jnp.asarray(cosine), jnp.asarray(sine),
    )
    gv, gg, go, gmg, gmu, gmd = (pack[:, at : at + 1728] for at in (OV, OG, OO, OMG, OMU, OMD))
    vec = [pack[:, OVEC + 96 + i] for i in range(4)]
    return (
        out[None], gin[None], vec[0], vec[1], pack[:, OQ : OQ + 1024], pack[:, OK : OK + 1024], gv, gg, go.T,
        vec[2], vec[3], gmg, gmu, gmd.T,
    )


def solution(mesh):
    both = ("dp", "seq")
    row, col, vec, tokens = P(both, None), P(None, both), P(both), P("dp", "seq", None)
    return jax.shard_map(
        per_device,
        mesh=mesh,
        in_specs=(tokens, tokens, vec, vec, row, row, row, row, col, vec, vec, row, row, col),
        out_specs=(tokens, tokens, vec, vec, row, row, row, row, col, vec, vec, row, row, col),
        check_vma=False,
    )
```

```python
import functools

import jax
import jax.numpy as jnp
import numpy as np
from jax import lax
from jax.experimental import pallas as pl
from jax.experimental.pallas import tpu as pltpu
from jax.sharding import PartitionSpec as P

MESH = pl.DeviceIdType.MESH
F32 = jnp.float32
BF16 = jnp.bfloat16
EPS = 1e-05
VH = 432

CK, CV, CQ, CG, CO, CMG, CMU, CMD, TOTAL = 0, 512, 1408, 1920, 2816, 3712, 4608, 5504, 6400
WIDE = 896
REAL = 864
VTILE = CV + 768


def cut(start, *tiles):
    parts = []
    for part, n in enumerate(tiles):
        parts.append((part, start, 128 * n))
        start += 128 * n
    return tuple(parts)


GATHERS = (
    cut(CK, 4, 3, 4), cut(CQ, 4, 4, 3), cut(CO, 2, 2, 3), cut(CMG, 6, 2, 6), cut(CMD, 3, 2, 2),
)
KV = cut(CK, 4, 4, 3)
KV_EARLY, KV_LATE = cut(CK, 4, 4, 2), ((2, VTILE, 128),)
QG, OUT, MLP, DOWN = cut(CQ, 5, 3, 3), cut(CO, 1, 2, 4), cut(CMG, 6, 2, 6), cut(CMD, 3, 3, 1)
FORWARD_GATHERS = (1, 2, 3, 4,)
PIECES = ((slice(0, 224), 0), (slice(224, 432), 0), (slice(432, 656), 1), (slice(656, 864), 1))
ORDERS = (("x", "y", "z"), ("y", "z", "x"), ("z", "x", "y"))
ZYX = ("z", "y", "x")


def tables():
    half = 128
    inverse = np.power(10000.0, -np.arange(half, dtype=np.float64) / half)
    angles = np.arange(1024, dtype=np.float64)[:, None] * inverse[None, :]
    return (
        np.cos(angles).astype(np.float32).reshape(4, 256, half),
        np.sin(angles).astype(np.float32).reshape(4, 256, half),
    )


def mm(a, b):
    return lax.dot_general(a, b, (((1,), (0,)), ((), ())), preferred_element_type=F32)


def mm_nt(a, b):
    return lax.dot_general(a, b, (((1,), (1,)), ((), ())), preferred_element_type=F32)


def loop(n, body):
    def step(i, carry):
        body(i)
        return carry

    lax.fori_loop(0, n, step, 0)


def each(n, body):
    for i in range(n):
        body(i)


def kernel(
    gain1_in, bias1_in, gain2_in, bias2_in, x_in, g_in, wq_in, wk_in, wv_in, wg_in, wo_in, wmg_in, wmu_in, wmd_in,
    cos_in, sin_in, out_ref, gin_ref, vec_ref, gq_ref, gk_ref, gv_ref, gg_ref, go_ref, gmg_ref, gmu_ref, gmd_ref,
    *scratch,
):
    (
        W, Gd, RA, RB1, R2A, R2B, R2C, R3, X, G, WS, IN8, INW, INV, OUT8, OUTW, OUTVEC, OUTV, PSEND, PRECV, VEC, VA, COS, SIN, STAT,
        NORM, NORMT, TT, Q, QS, K, KW, V, GGP, GATE, WT, MASK, MIX, GRP,
        UT, TOT, STATES, CT, GUT, GATED, MID, SB, RB, SBO, RBO, OWN1, RB2, RB3, OWN2,
        SEC, ACT, BCT, HID, GGL, GUL, GM, GMX, GQ, GK, GV, FSEND, FRECV, KEEP,
        way_s, way_r, st_s, st_r, ex_s, ex_r, loc,
    ) = scratch
    S1, S2, VT, RSTD, GML = RB1.at[0], R2B.at[0], TT.at[0:WIDE], MIX, SEC
    dp = lax.axis_index("dp")
    sq = lax.axis_index("seq")
    me = {"z": dp // 4, "y": dp % 4, "x": sq // 2}
    c = sq % 2
    c0 = (c == 0).astype(F32)
    c1 = (c == 1).astype(F32)

    def shifted(axis, k):
        p = dict(me)
        p[axis] = (me[axis] + k) % 4
        return p

    def device(p, core):
        return (p["z"] * 4 + p["y"], p["x"] * 2 + core)

    sibling = device(me, 1 - c)

    def remote(src, dst, ss, rs, dev):
        return pltpu.make_async_remote_copy(
            src_ref=src, dst_ref=dst, send_sem=ss, recv_sem=rs, device_id=dev, device_id_type=MESH
        )

    rows_own = pl.ds(pl.multiple_of(c * 128, 128), 128)
    rows_sib = pl.ds(pl.multiple_of((1 - c) * 128, 128), 128)
    fetch = [
        pltpu.make_async_copy(src, dst, loc.at[i])
        for i, (src, dst) in enumerate(
            (
                (wq_in, IN8.at[0]), (wk_in, IN8.at[1]), (wv_in, INW.at[0]), (wg_in, INW.at[1]),
                (wo_in, INW.at[2]), (wmg_in, INW.at[3]), (wmu_in, INW.at[4]), (wmd_in, INW.at[5]),
                (x_in, X.at[rows_own, :]), (g_in, G.at[rows_own, :]),
                (cos_in.at[me["x"]], COS), (sin_in.at[me["x"]], SIN),
            )
        )
    ]
    for copy in fetch:
        copy.start()
    barrier = pltpu.get_barrier_semaphore()
    pl.semaphore_signal(barrier, inc=1, device_id=sibling, device_id_type=MESH)
    for axis in ZYX:
        for k in (1, 2, 3):
            pl.semaphore_signal(
                barrier, inc=1, device_id=device(shifted(axis, k), c), device_id_type=MESH
            )

    def put(ref, col, own):
        both = jnp.concatenate([own * c0, own * c1], axis=0)
        ref[:, col : col + own.shape[1]] = both.astype(BF16)

    def pack(col, h0, h1):
        put(PRECV.at[0], col, h0 * c0 + h1 * c1)
        put(PSEND, col, h0 * c1 + h1 * c0)

    def pack_square(i, col):
        w = IN8[i].astype(F32)
        pack(col, w[:, :512], w[:, 512:])

    def pack_wide(i, col):
        lane = lax.broadcasted_iota(jnp.int32, (8, WIDE), 1)
        WS[:, 1664:1792] = jnp.zeros((8, 128), F32)
        WS[:, :1728] = INW[i].astype(F32)
        h0 = jnp.where(lane < REAL, WS[:, :WIDE], 0.0)
        h1 = pltpu.roll(WS[:, 768:1792], 1024 - 96, 1)[:, :WIDE]
        h1 = jnp.where(lane < REAL, h1, 0.0)
        if col == CV:
            v = jnp.concatenate([INV[...], jnp.zeros((120, 128), F32)], axis=0).T
            v = pltpu.roll(v[0:8, :], 96, 1)
            v = jnp.concatenate([jnp.zeros((8, 768), F32), v], axis=1)
            h0 = h0 + v
            h1 = h1 + v
        pack(col, h0, h1)

    def exchange(first, last, i):
        s = pl.ds(first, last - first)
        copy = remote(PSEND.at[:, s], PRECV.at[1, :, s], ex_s.at[i], ex_r.at[i], sibling)
        copy.start()
        return copy

    def assemble(copy, first, last):
        copy.wait_recv()
        for col in range(first, last, 640):
            s = pl.ds(col, min(640, last - col))
            W[me["z"], me["y"], me["x"], :, s] = (
                PRECV[0, :, s].astype(F32) + PRECV[1, :, s].astype(F32)
            ).astype(BF16)

    INV[...] = jnp.zeros_like(INV)
    for i, ref in enumerate((gain1_in, bias1_in, gain2_in, bias2_in)):
        INV[i : i + 1, 0:8] = ref[...].astype(F32)
    for copy in fetch[:8]:
        copy.wait()
    pack_square(1, CK)
    pack_wide(0, CV)
    pl.semaphore_wait(barrier, 10)
    e_first = exchange(0, CQ, 0)
    pack_square(0, CQ)
    for i, col in enumerate((CG, CO, CMG, CMU, CMD)):
        pack_wide(i + 1, col)
    e_rest = exchange(CQ, TOTAL, 12)
    fetch[8].wait()
    e_x = remote(X.at[rows_own, :], X.at[rows_own, :], ex_s.at[1], ex_r.at[1], sibling)
    e_x.start()
    fetch[9].wait()
    e_g = remote(G.at[rows_own, :], G.at[rows_own, :], ex_s.at[2], ex_r.at[2], sibling)
    e_g.start()

    pending = []
    count = [0]

    def stage(total):
        count[0] += 1
        return way_s.at[count[0] - 1], way_r.at[count[0] - 1], total

    def send(where, src, dst, dev):
        remote(src, dst, where[0], where[1], dev).start()

    def arrived(where):
        ss, rs, total = where
        remote(total, total, ss, rs, sibling).wait_recv()
        pending.append(where)

    def columns(parts):
        return pl.ds(parts[0][1], sum(n for _, _, n in parts))

    def gather(group, phase, forward=False):
        s = columns(GATHERS[group])
        halves = phase == 2 or (phase == 1 and group in FORWARD_GATHERS)
        if phase == 1:
            where = stage(W.at[0, 0 : 1 if forward else 2 if halves else 3, :, :, s])
        else:
            where = stage(W.at[0, :, :, :, s] if forward else W.at[0:2, :, :, :, s])
        gather_parts(where, GATHERS[group], phase, halves, forward)
        return where

    def gather_parts(where, parts, phase, halves, forward):
        for part, col, n in parts:
            order = ORDERS[part]
            axis = order[phase]
            for i, k in enumerate((1, 3) if halves else (1, 2, 3)):
                idx = {a: me[a] for a in ZYX}
                for a in order[:phase]:
                    idx[a] = slice(None)
                if forward:
                    idx[axis] = (me[axis] - k) % 4
                    idx[[a for a in ZYX if a in order[:phase]][0]] = pl.ds(2 * i, 2)
                src = W.at[tuple(idx[a] for a in ZYX) + (slice(None), pl.ds(col, n))]
                send(where, src, src, device(shifted(axis, k), c))

    def first_phase(groups, first, last):
        where = stage(W.at[0, 0, 0:3, :, first:last])
        for g in groups:
            gather_parts(where, GATHERS[g], 0, False, False)
        return where

    assemble(e_first, 0, CQ)
    p1 = {0: first_phase((0,), 0, CQ)}
    assemble(e_rest, CQ, TOTAL)
    p1[1] = first_phase((1, 2, 3, 4), CQ, TOTAL)
    p2, p3, p4, p5 = {}, {}, {}, {}
    waited = []

    def w1(g):
        at = min(g, 1)
        if at not in waited:
            waited.append(at)
            arrived(p1[at])
        p2[g] = gather(g, 1)

    def w2(g):
        if g in FORWARD_GATHERS:
            arrived(p2[g])
            p3[g] = gather(g, 1, True)

    def w3(g):
        arrived(p3[g] if g in FORWARD_GATHERS else p2[g])
        p4[g] = gather(g, 2)

    def w4(g):
        arrived(p4[g])
        p5[g] = gather(g, 2, True)

    def w5(g):
        arrived(p5[g])

    def wcols(col, n):
        return W[:, :, :, :, col : col + n].reshape(1024, n)

    def wrows(i, col, n):
        return W[i, :, :, :, col : col + n].reshape(256, n)

    def fwd(a, col, n, emit):
        for at in range(0, n, 256):
            w = min(256, n - at)
            emit(at, w, mm(a[...], wcols(col + at, w)))

    def grad(at, b, col):
        n = b.shape[1]

        def body(i):
            r = mm(at[pl.ds(i * 256, 256), :], b[...])
            Gd[i, :, :, :, col : col + n] = r.astype(BF16).reshape(4, 4, 16, n)

        each(4, body)

    def rows(i, n=64):
        return pl.ds(pl.multiple_of(i * n, n), n)

    lanes = lax.broadcasted_iota(jnp.int32, (64, WIDE), 1)
    in0 = lanes < VH
    in1 = (lanes >= VH) & (lanes < REAL)
    real = lanes < REAL

    def log_gamma(hh):
        g0 = float(np.log(1.0 - 2.0 ** (-5.0 - hh)))
        g1 = float(np.log(1.0 - 2.0 ** (-7.0 - hh)))
        return jnp.where(c == 0, jnp.float32(g0), jnp.float32(g1))

    lg = [log_gamma(0), log_gamma(1)]

    def mask_body(i):
        ii = lax.broadcasted_iota(jnp.int32, (64, 256), 0) + i * 64
        jj = lax.broadcasted_iota(jnp.int32, (64, 256), 1)
        d = (ii - jj).astype(F32)
        for hh in range(2):
            MASK[hh, rows(i), :] = jnp.where(d >= 0, jnp.exp(jnp.maximum(d, 0.0) * lg[hh]), 0.0)

    loop(4, mask_body)
    VA[...] = jnp.zeros_like(VA)
    e_x.wait_recv()
    e_g.wait_recv()

    def norm(v):
        mean = jnp.mean(v, axis=-1, keepdims=True)
        center = v - mean
        spread = jnp.mean(center * center, axis=-1, keepdims=True)
        rstd = lax.rsqrt(spread + EPS)
        return center * rstd, rstd, mean

    def ln1_stats(i):
        xh, rstd, mean = norm(X[rows(i), :].astype(F32))
        GM[rows(i), :] = xh
        STAT[0, rows(i), :] = jnp.broadcast_to(mean, (64, 128))
        STAT[1, rows(i), :] = jnp.broadcast_to(rstd, (64, 128))

    loop(4, ln1_stats)
    fetch[10].wait()
    fetch[11].wait()

    def transpose(src, dst):
        dst[...] = src[...].T

    def vector(i):
        return VEC[i : i + 1, :]

    def ln1():
        VEC[...] = wcols(VTILE, 128).astype(F32).T[96:104, :]
        gain1, bias1 = vector(0), vector(1)

        def ln1(i):
            NORM[rows(i), :] = (GM[rows(i), :] * gain1 + bias1).astype(BF16)

        loop(4, ln1)

    def rotated(dst, dst2, offset, sign, scale):
        def emit(at, w, r):
            hh = at // 256
            u, z = r[:, :128], r[:, 128:]
            co, si = COS[...], SIN[...]
            a0 = ((u * co - z * si) * scale).astype(BF16)
            a1 = ((u * si + z * co) * scale).astype(BF16)
            spot = lax.broadcasted_iota(jnp.int32, (256, 128), 0).astype(F32)
            sc = jnp.exp((spot * sign + offset) * lg[hh])
            dst[:, at : at + 128] = a0
            dst[:, at + 128 : at + 256] = a1
            dst2[:, at : at + 128] = (a0.astype(F32) * sc).astype(BF16)
            dst2[:, at + 128 : at + 256] = (a1.astype(F32) * sc).astype(BF16)

        return emit

    def emit_v(at, w, r):
        col = lax.broadcasted_iota(jnp.int32, (256, w), 1) + at
        V[:, at : at + w] = jnp.where(col < REAL, r, 0.0).astype(BF16)

    def kvu():
        fwd(NORM, CK, 512, rotated(K, KW, 255.0, -1.0, 0.0625))
        fwd(NORM, CV, WIDE, emit_v)
        transpose(V, VT)
        for hh in range(2):
            r = mm(VT[VH * hh : VH * (hh + 1), :], KW[:, 256 * hh : 256 * (hh + 1)])
            UT[VH * hh : VH * (hh + 1), :] = r.astype(BF16)

    def states(src, base, back):
        x = me["x"]
        near = dict(me, x=x + 1 - 2 * (x % 2))
        far = dict(me, x=3 - x)
        low = x < 2
        sends = (x != 0) if back else (x != 3)
        gets = (x != 1) if back else (x != 2)
        passes = ~low if back else low
        steps = []
        for i, (at, hh) in enumerate(PIECES):
            t = base + i
            slot = 1 if back else 0
            one = remote(src.at[at], STATES.at[slot, at], st_s.at[t], st_r.at[t], device(near, c))
            pl.when(sends)(one.start)
            steps.append(one)

        def second(i):
            at, hh = PIECES[i]
            t = base + 4 + i
            two = remote(TOT.at[at], STATES.at[2, at], st_s.at[t], st_r.at[t], device(far, c))

            def total():
                steps[i].wait_recv()
                own = src[at, :].astype(F32)
                got = STATES[slot, at, :].astype(F32)
                g = jnp.exp(256.0 * lg[hh])
                first = (x % 2 == 1) if back else (x % 2 == 0)
                TOT[at, :] = jnp.where(first, own * g + got, own + got * g).astype(BF16)
                two.start()

            pl.when(passes)(total)
            return two

        def finish(dst):
            dst[...] = jnp.zeros_like(dst)
            for i, two in enumerate(twos):
                at, hh = PIECES[i]
                g = jnp.exp(256.0 * lg[hh])

                def single():
                    dst[at, :] = STATES[slot, at, :]

                def double():
                    two.wait_recv()
                    dst[at, :] = STATES[2, at, :]

                def triple():
                    steps[i].wait_recv()
                    two.wait_recv()
                    total = STATES[2, at, :].astype(F32) * g
                    dst[at, :] = (total + STATES[slot, at, :].astype(F32)).astype(BF16)

                one, pair, three = (2, 1, 0) if back else (1, 2, 3)
                pl.when(x == one)(single)
                pl.when(x == pair)(double)
                pl.when(x == three)(triple)

        def sent():
            for one, two in zip(steps, twos):
                pl.when(sends)(one.wait_send)
                pl.when(passes)(two.wait_send)

        twos = []

        def middle(*pieces):
            twos.extend(second(i) for i in pieces)

        return middle, finish, sent

    def join(dst, h0, h1):
        pick = lax.broadcasted_iota(jnp.int32, (256, 128), 1) < VH - 384
        dst[:, 0:384] = h0[:, :384]
        dst[:, 384:512] = jnp.where(pick, h0[:, 384:512], h1[:, :128])
        dst[:, 512:896] = h1[:, 128:512]

    def qi():
        fwd(NORM, CQ, 512, rotated(Q, QS, 1.0, 1.0, 1.0))
        for hh in range(2):
            raw = mm_nt(Q[:, 256 * hh : 256 * (hh + 1)], K[:, 256 * hh : 256 * (hh + 1)])
            WT[hh] = (raw * MASK[hh]).astype(BF16)
        join(MIX, mm(WT[0], V[:, 0:512]), mm(WT[1], V[:, 384:896]))

    def emit_gate(at, w, r):
        GATE[:, at : at + w] = r

    def gate():
        fwd(NORM, CG, WIDE, emit_gate)

    def cross():
        join(GRP, mm_nt(QS[:, 0:256], CT[0:512, :]), mm_nt(QS[:, 256:512], CT[384:896, :]))

    def heads_mean(v):
        m0 = jnp.sum(jnp.where(in0, v, 0.0), axis=-1, keepdims=True) * (1.0 / VH)
        m1 = jnp.sum(jnp.where(in1, v, 0.0), axis=-1, keepdims=True) * (1.0 / VH)
        return jnp.where(in0, m0, m1)

    def group_norm(i):
        m = MIX[rows(i), :] + GRP[rows(i), :]
        center = m - heads_mean(m)
        rstd = lax.rsqrt(heads_mean(center * center) + EPS)
        grouped = jnp.where(real, center * rstd, 0.0)
        GRP[rows(i), :] = grouped
        RSTD[rows(i), :] = rstd
        gate = GATE[rows(i), :]
        GATED[rows(i), :] = (gate * jax.nn.sigmoid(gate) * grouped).astype(BF16)

    def gn():
        loop(4, group_norm)

    def out_body(i):
        r = mm_nt(GATED[...], wrows(i, CO, WIDE))
        s = pl.ds(i * 256, 256)
        MID[:, s] = r
        SB[:, s] = r.astype(BF16)
        remote(SB.at[:, s], RB.at[:, s], ex_s.at[3], ex_r.at[3], sibling).start()

    def out():
        each(4, out_body)

    e_mid = remote(SB, RB, ex_s.at[3], ex_r.at[3], sibling)

    def ln2():
        gain2, bias2 = vector(2), vector(3)

        def ln2_rows(i):
            m = X[rows(i), :].astype(F32) + MID[rows(i), :] + RB[rows(i), :].astype(F32)
            MID[rows(i), :] = m
            xh, rstd, mean = norm(m)
            STAT[2, rows(i), :] = jnp.broadcast_to(mean, (64, 128))
            STAT[3, rows(i), :] = jnp.broadcast_to(rstd, (64, 128))
            SEC[rows(i), :] = (xh * gain2 + bias2).astype(BF16)

        e_mid.wait_recv()
        loop(4, ln2_rows)

    def emit_act(at, w, r):
        ACT[:, at : at + w] = r

    def emit_bct(at, w, r):
        BCT[:, at : at + w] = r

    def gelu_rows(i):
        g = ACT[rows(i), :]
        u = BCT[rows(i), :]
        cdf = 0.5 * (1.0 + lax.erf(g * 0.7071067811865476))
        ge = g * cdf
        HID[rows(i), :] = (ge * u).astype(BF16)
        BCT[rows(i), :] = ge
        ACT[rows(i), :] = (cdf + g * jnp.exp(-0.5 * g * g) * 0.3989422804014327) * u

    def mlp():
        fwd(SEC, CMG, WIDE, emit_act)
        fwd(SEC, CMU, WIDE, emit_bct)

    def gelu():
        loop(4, gelu_rows)

    def place(axes, where):
        return tuple(where.get(a, slice(None)) for a in axes)

    def others(part, phase):
        order = ORDERS[part][::-1]
        return order[phase], [a for a in ZYX if a not in order[: phase + 1]], [a for a in ZYX if a not in order[:phase]]

    def scatter0(parts, late=None):
        s = columns(parts)
        early = stage(RA.at[:, :, :, :, s])
        late = late or stage(RB1.at[:, :, :, :, s])
        for where in (early, late):
            for part, col, n in parts:
                axis, rest, left = others(part, 0)
                s = (slice(None), pl.ds(col, n))
                for i, k in enumerate((1, 3)):
                    dev = device(shifted(axis, k), c)
                    if where is early:
                        src = Gd.at[place(left, {axis: (me[axis] + 2) % 4, rest[0]: pl.ds(2 * i, 2)}) + s]
                        send(where, src, RA.at[(i, slice(None), slice(None)) + s], dev)
                    else:
                        near = pl.ds(2 - 2 * i, 2)
                        src = Gd.at[place(left, {axis: (me[axis] + k) % 4, rest[0]: near}) + s]
                        send(where, src, RB1.at[(i, near, slice(None)) + s], dev)
        return early, late

    def scatter1(parts, where):
        early, late = where
        arrived(early)
        for part, col, n in parts:
            axis, rest, left = others(part, 0)
            s = (slice(None), pl.ds(col, n))
            for i, k in enumerate((1, 3)):

                def body(j):
                    own = Gd[place(left, {axis: (me[axis] + k) % 4, rest[0]: 2 * i + j}) + s]
                    at = (i, j, slice(None)) + s
                    RA[at] = (own.astype(F32) + RA[at].astype(F32)).astype(BF16)

                loop(2, body)
                src = RA.at[(i, slice(None), slice(None)) + s]
                dst = RB1.at[(i, pl.ds(2 * i, 2), slice(None)) + s]
                send(late, src, dst, device(shifted(axis, k), c))
        return late

    def scatter2(parts, late):
        arrived(late)
        direct = parts is KV
        if direct:
            early = stage(R2C.at[:, :, :, columns(parts)])
        else:
            early, late = stage(R2A.at[:, :, :, columns(parts)]), stage(R2B.at[:, :, :, columns(parts)])
        for part, col, n in parts:
            axis, rest, left = others(part, 0)
            s = (slice(None), pl.ds(col, n))

            def body(j):
                own = Gd[place(left, {axis: me[axis], rest[0]: j}) + s].astype(F32)
                at = (j, slice(None)) + s
                RB1[(0,) + at] = (own + RB1[(0,) + at].astype(F32) + RB1[(1,) + at].astype(F32)).astype(BF16)

            loop(4, body)
            axis, rest, left = others(part, 1)
            if direct:
                for k in (1, 2, 3):
                    to = shifted(axis, k)
                    src = S1.at[place(left, {axis: to[axis]}) + s]
                    send(early, src, R2C.at[(k - 1, slice(None)) + s], device(to, c))
                continue
            for i, k in enumerate((1, 3)):
                dev = device(shifted(axis, k), c)
                src = S1.at[place(left, {axis: (me[axis] + 2) % 4, rest[0]: pl.ds(2 * i, 2)}) + s]
                send(early, src, R2A.at[(i, slice(None)) + s], dev)
                near = pl.ds(2 - 2 * i, 2)
                src = S1.at[place(left, {axis: (me[axis] + k) % 4, rest[0]: near}) + s]
                send(late, src, R2B.at[(i, near) + s], dev)
        return early, late

    def scatter3(parts, where):
        if parts is KV:
            return where[0]
        early, late = where
        arrived(early)
        for part, col, n in parts:
            axis, rest, left = others(part, 1)
            s = (slice(None), pl.ds(col, n))
            for i, k in enumerate((1, 3)):
                half = pl.ds(2 * i, 2)
                own = S1[place(left, {axis: (me[axis] + k) % 4, rest[0]: half}) + s]
                at = (i, slice(None)) + s
                R2A[at] = (own.astype(F32) + R2A[at].astype(F32)).astype(BF16)
                send(late, R2A.at[at], R2B.at[(i, half) + s], device(shifted(axis, k), c))
        return late

    def scatter4(parts, where):
        arrived(where)
        where = stage(R3.at[:, :, columns(parts)])
        came = [R2C.at[k] for k in range(3)] if parts is KV else [R2B.at[k] for k in range(2)]
        for part, col, n in parts:
            axis, rest, left = others(part, 1)
            s = (slice(None), pl.ds(col, n))
            t = S1[place(left, {axis: me[axis]}) + s].astype(F32)
            for ref in came:
                t = t + ref[(slice(None),) + s].astype(F32)
            S2[(slice(None),) + s] = t.astype(BF16)
            axis, rest, left = others(part, 2)
            for k in (1, 2, 3):
                to = shifted(axis, k)
                send(where, S2.at[(to[axis],) + s], R3.at[(k - 1,) + s], device(to, c))
        return where

    def scatter5(parts, where, i):
        arrived(where)
        for part, col, n in parts:
            axis, rest, left = others(part, 2)
            s = (slice(None), pl.ds(col, n))
            t = S2[(me[axis],) + s].astype(F32)
            for k in range(3):
                t = t + R3[(k,) + s].astype(F32)
            KEEP[:, s[1]] = t[0:8, :] * c0 + t[8:16, :] * c1
            FSEND[:, s[1]] = t[0:8, :] * c1 + t[8:16, :] * c0
        s = columns(parts)
        copy = remote(FSEND.at[:, s], FRECV.at[:, s], ex_s.at[7 + i], ex_r.at[7 + i], sibling)
        copy.start()
        return copy

    def halves(col, n):
        keep = KEEP[:, col : col + n]
        got = FRECV[:, col : col + n]
        return keep * c0 + got * c1, keep * c1 + got * c0

    def finish(copy, *cols):
        copy.wait_recv()
        puts = []
        for col in cols:
            if col in (CQ, CK):
                i = (CQ, CK).index(col)
                lo, hi = halves(col, 512)
                OUT8[i, :, :512] = lo
                OUT8[i, :, 512:] = hi
                puts.append((OUT8.at[i], (gq_ref, gk_ref)[i]))
            elif col == VTILE:
                lo, hi = halves(col, 128)
                OUTVEC[...] = jnp.concatenate([lo + hi, jnp.zeros((120, 128), F32)], axis=0).T[96:104, :]
                puts.append((OUTVEC, vec_ref))
            else:
                i = (CV, CG, CO, CMG, CMU, CMD).index(col)
                lo, hi = halves(col, WIDE)
                moved = pltpu.roll(jnp.concatenate([hi, jnp.zeros((8, 128), F32)], axis=1), 96, 1)
                first96 = lax.broadcasted_iota(jnp.int32, (8, 128), 1) < 96
                OUTW[i, :, 0:768] = lo[:, 0:768]
                OUTW[i, :, 768:896] = jnp.where(first96, lo[:, 768:896], moved[:, 0:128])
                OUTW[i, :, 896:1728] = moved[:, 128:960]
                puts.append((OUTW.at[i], (gv_ref, gg_ref, go_ref, gmg_ref, gmu_ref, gmd_ref)[i]))
        for src, dst in puts:
            out = pltpu.make_async_copy(src, dst, loc.at[14 + len(written)])
            out.start()
            written.append(out)
        return copy

    written = []

    def emit_hidden(at, w, r):
        GGL[:, at : at + w] = (r * ACT[:, at : at + w]).astype(BF16)
        GUL[:, at : at + w] = (r * BCT[:, at : at + w]).astype(BF16)

    def gmd():
        transpose(G, TT)
        grad(TT, HID, CMD)

    def gh():
        fwd(G, CMD, WIDE, emit_hidden)

    def second_body(i):
        r = mm_nt(GGL[...], wrows(i, CMG, WIDE)) + mm_nt(GUL[...], wrows(i, CMU, WIDE))
        s = pl.ds(i * 256, 256)
        GM[:, s] = r
        SB[:, s] = r.astype(BF16)
        remote(SB.at[:, s], RB2.at[:, s], ex_s.at[5], ex_r.at[5], sibling).start()

    def gs():
        e_mid.wait_send()
        each(4, second_body)

    e_sec = remote(SB, RB2, ex_s.at[5], ex_r.at[5], sibling)

    def gmg():
        transpose(SEC, TT)
        grad(TT, GGL, CMG)

    def gmu():
        transpose(SEC, TT)
        grad(TT, GUL, CMU)

    def norm_back(gs, v, gain, at, which):
        rstd = STAT[which + 1, at, 0:1]
        xh = (v - STAT[which, at, 0:1]) * rstd
        gx = gs * gain
        m0 = jnp.mean(gx, axis=-1, keepdims=True)
        m1 = jnp.mean(gx * xh, axis=-1, keepdims=True)
        return rstd * (gx - m0 - xh * m1), jnp.sum(gs * xh, axis=0, keepdims=True), jnp.sum(gs, axis=0, keepdims=True)

    def ln2b():
        gain2 = vector(2)

        def ln2_back(i):
            gs = GM[rows(i), :] + RB2[rows(i), :].astype(F32)
            part, ggain, gbias = norm_back(gs, MID[rows(i), :], gain2, rows(i), 2)
            gm = G[rows(i), :].astype(F32) + part
            GM[rows(i), :] = gm
            GML[rows(i), :] = gm.astype(BF16)
            mine = (i // 2 == c).astype(F32)
            VA[2:3, :] += ggain * mine
            VA[3:4, :] += gbias * mine

        e_sec.wait_recv()
        loop(4, ln2_back)

    def gout():
        transpose(GML, TT)
        grad(TT, GATED, CO)

    def emit_gated(at, w, r):
        ACT[:, at : at + w] = r

    def gated():
        fwd(GML, CO, WIDE, emit_gated)

    def group_back(i):
        gr = ACT[rows(i), :]
        z = GATE[rows(i), :]
        sg = jax.nn.sigmoid(z)
        grp = GRP[rows(i), :]
        GGP[rows(i), :] = (gr * (sg * (1.0 + z * (1.0 - sg))) * grp).astype(BF16)
        gg = gr * (z * sg)
        gmx = RSTD[rows(i), :] * (gg - heads_mean(gg) - grp * heads_mean(gg * grp))
        GMX[rows(i), :] = jnp.where(real, gmx, 0.0).astype(BF16)

    def groupb():
        loop(4, group_back)

    def gc():
        transpose(GMX, VT)
        u_sent()
        for hh in range(2):
            r = mm(VT[VH * hh : VH * (hh + 1), :], QS[:, 256 * hh : 256 * (hh + 1)])
            UT[VH * hh : VH * (hh + 1), :] = r.astype(BF16)

    def gg():
        grad(NORMT, GGP, CG)

    def gq():
        grad(NORMT, GQ, CQ)

    wide = lax.broadcasted_iota(jnp.int32, (256, 512), 1)
    windows = (slice(0, 512), slice(384, 896))

    def window(ref, hh):
        a = ref[:, windows[hh]]
        keep = wide < VH if hh == 0 else wide >= VH - 384
        return jnp.where(keep, a, jnp.zeros_like(a))

    def spots(hh, offset, sign):
        spot = lax.broadcasted_iota(jnp.int32, (256, 128), 0).astype(F32)
        return jnp.exp((spot * sign + offset) * lg[hh])

    def unrotated(dst, src, hh, cross, offset, sign, scale):
        sc = spots(hh, offset, sign)
        co, si = COS[...], SIN[...]
        a, b = slice(256 * hh, 256 * hh + 128), slice(256 * hh + 128, 256 * hh + 256)
        u = (src[:, a] + cross[:, :128] * sc) * scale
        z = (src[:, b] + cross[:, 128:] * sc) * scale
        dst[:, a] = (u * co + z * si).astype(BF16)
        dst[:, b] = (z * co - u * si).astype(BF16)

    def intra():
        gvi = []
        for hh in range(2):
            h = slice(256 * hh, 256 * (hh + 1))
            gm = window(GMX, hh)
            vw = V[:, windows[hh]]
            graw = (mm_nt(gm, vw) * MASK[hh]).astype(BF16)
            ACT[:, h] = mm(graw, K[:, h])
            BCT[:, h] = mm(graw.T, Q[:, h])
            gvi.append(mm(WT[hh].T, gm))
            unrotated(GQ, ACT, hh, mm(gm, CT[windows[hh], :]), 1.0, 1.0, 1.0)
        join(MIX, gvi[0], gvi[1])

    def down_body(i):
        r = mm_nt(HID[...], wrows(i, CMD, WIDE))
        s = pl.ds(i * 256, 256)
        OWN1[:, s] = r[0:128] * c0 + r[128:256] * c1
        SBO[:, s] = (r[0:128] * c1 + r[128:256] * c0).astype(BF16)

    e_out = remote(SBO, RBO, ex_s.at[4], ex_r.at[4], sibling)
    put_out = pltpu.make_async_copy(OUTV.at[0], out_ref, loc.at[12])
    put_gin = pltpu.make_async_copy(OUTV.at[1], gin_ref, loc.at[13])

    def down():
        each(4, down_body)
        e_out.start()

    def normed_first(i):
        r = mm_nt(GQ[...], wrows(i, CQ, 512)) + mm_nt(GGP[...], wrows(i, CG, WIDE))
        MID[:, pl.ds(i * 256, 256)] = r

    def pn1():
        e_out.wait_recv()
        OUTV[0] = (MID[rows_own, :] + OWN1[...] + RBO[...].astype(F32)).astype(BF16)
        put_out.start()
        each(4, normed_first)

    def kvb():
        gvs = []
        for hh in range(2):
            h = slice(256 * hh, 256 * (hh + 1))
            unrotated(GK, BCT, hh, mm(window(V, hh), GUT[windows[hh], :]), 255.0, -1.0, 0.0625)
            gvs.append(mm_nt(KW[:, h], GUT[windows[hh], :]))
        join(ACT, gvs[0], gvs[1])
        GV[...] = (MIX[...] + ACT[...]).astype(BF16)

    def gk():
        grad(NORMT, GK, CK)

    def gv():
        grad(NORMT, GV, CV)

    def normed_body(i):
        s = pl.ds(i * 256, 256)
        r = MID[:, s] + mm_nt(GK[...], wrows(i, CK, 512)) + mm_nt(GV[...], wrows(i, CV, WIDE))
        OWN2[:, s] = r[0:128] * c0 + r[128:256] * c1
        SBO[:, s] = (r[0:128] * c1 + r[128:256] * c0).astype(BF16)
        remote(SBO.at[:, s], RB3.at[:, s], ex_s.at[6], ex_r.at[6], sibling).start()

    def pn2():
        e_out.wait_send()
        each(4, normed_body)

    e_norm = remote(SBO, RB3, ex_s.at[6], ex_r.at[6], sibling)

    def ln1b():
        gain1 = vector(0)

        def ln1_back(i):
            at = pl.ds(pl.multiple_of(c * 128 + i * 64, 64), 64)
            gs = OWN2[rows(i), :] + RB3[rows(i), :].astype(F32)
            part, ggain, gbias = norm_back(gs, X[at, :].astype(F32), gain1, at, 0)
            OUTV[1, rows(i), :] = (GM[at, :] + part).astype(BF16)
            VA[0:1, :] += ggain
            VA[1:2, :] += gbias

        e_norm.wait_recv()
        loop(2, ln1_back)
        put_gin.start()
        vectors = jnp.concatenate([jnp.zeros((96, 1024), F32), VA[...], jnp.zeros((24, 1024), F32)], axis=0).T
        tile = slice(VTILE, VTILE + 128)
        Gd[:, :, :, :, tile] = (
            Gd[:, :, :, :, tile].astype(F32) + vectors.reshape(4, 4, 4, 16, 128)
        ).astype(BF16)

    w1(0)
    w1(2)
    w1(1)
    w1(4)
    w1(3)
    w2(2)
    w2(1)
    w3(0)
    w3(1)
    w4(0)
    w2(3)
    w3(2)
    w2(4)
    w4(1)
    w5(0)
    ln1()
    kvu()
    u_middle, u_finish, u_sent = states(UT, 0, False)
    w3(3)
    w3(4)
    u_middle(0, 1, 2, 3)
    w5(1)
    w4(2)
    w4(3)
    transpose(NORM, NORMT)
    gate()
    qi()
    u_finish(CT)
    cross()
    gn()
    w5(2)
    out()
    w4(4)
    ln2()
    w5(3)
    mlp()
    gelu()
    gmd()
    w5(4)
    r_down = scatter0(DOWN)
    gh()
    gs()
    gmg()
    gmu()
    r_mlp = scatter0(MLP)
    ln2b()
    r_down = scatter1(DOWN, r_down)
    gout()
    gated()
    groupb()
    gc()
    c_middle, c_finish, c_sent = states(UT, 8, True)
    r_out = scatter0(OUT)
    intra()
    down()
    gq()
    gg()
    r_qg = scatter0(QG)
    c_middle(0, 1)
    c_middle(2, 3)
    r_mlp = scatter1(MLP, r_mlp)
    r_out = scatter1(OUT, r_out)
    r_qg = scatter1(QG, r_qg)
    c_finish(GUT)
    kvb()
    gv()
    gk()
    r_kv = scatter0(KV_EARLY, stage(RB1.at[:, :, :, :, columns(KV)]))
    r_mlp = scatter2(MLP, r_mlp)
    pn1()
    pn2()
    ln1b()
    r_vec = scatter0(KV_LATE, r_kv[1])
    r_kv = scatter1(KV_EARLY, r_kv)
    scatter1(KV_LATE, r_vec)
    r_down = scatter2(DOWN, r_down)
    r_qg = scatter2(QG, r_qg)
    r_out = scatter2(OUT, r_out)
    r_mlp = scatter3(MLP, r_mlp)
    r_down = scatter3(DOWN, r_down)
    r_kv = scatter2(KV, r_kv)
    r_out = scatter3(OUT, r_out)
    r_qg = scatter3(QG, r_qg)
    r_mlp = scatter4(MLP, r_mlp)
    r_down = scatter4(DOWN, r_down)
    r_kv = scatter3(KV, r_kv)
    r_kv = scatter4(KV, r_kv)
    r_out = scatter4(OUT, r_out)
    r_qg = scatter4(QG, r_qg)
    f_mlp = scatter5(MLP, r_mlp, 1)
    f_out = scatter5(OUT, r_out, 2)
    f_down = scatter5(DOWN, r_down, 0)
    f_kv = scatter5(KV, r_kv, 4)
    f_qg = scatter5(QG, r_qg, 3)
    f_mlp = finish(f_mlp, CMG, CMU)
    f_out = finish(f_out, CO)
    f_down = finish(f_down, CMD)
    f_kv = finish(f_kv, CK, CV, VTILE)
    f_qg = finish(f_qg, CQ, CG)
    c_sent()
    put_out.wait()
    put_gin.wait()
    for where in pending:
        remote(where[2], where[2], where[0], where[1], sibling).wait_send()
    for copy in (e_first, e_rest, e_x, e_g, e_sec, e_norm):
        copy.wait_send()
    for copy in (f_down, f_mlp, f_out, f_qg, f_kv):
        copy.wait_send()
    for out in written:
        out.wait()


def hand_over(*refs):
    vec, results, smalls, outs, rows, held = refs[0], refs[1:11], refs[11:15], refs[15:25], refs[25], refs[26:36]
    sems = refs[36]
    fetch = [pltpu.make_async_copy(a, b, sems.at[i]) for i, (a, b) in enumerate(zip(results, held))]
    write = [pltpu.make_async_copy(a, b, sems.at[10 + i]) for i, (a, b) in enumerate(zip(held, outs))]
    last = pltpu.make_async_copy(vec, rows, sems.at[20])
    for copy in fetch:
        copy.start()
    last.start()
    for a, b in zip(fetch, write):
        a.wait()
        b.start()
    last.wait()
    for i, ref in enumerate(smalls):
        ref[...] = rows[i : i + 1, 0:8]
    for copy in write:
        copy.wait()


def scratch():
    def b(*shape):
        return pltpu.VMEM(shape, BF16)

    def f(*shape):
        return pltpu.VMEM(shape, F32)

    def sem(n):
        return pltpu.SemaphoreType.DMA((n,))

    return [
        b(4, 4, 4, 16, TOTAL), b(4, 4, 4, 16, TOTAL), b(2, 2, 4, 16, TOTAL), b(2, 4, 4, 16, TOTAL),
        b(2, 2, 16, TOTAL), b(2, 4, 16, TOTAL), b(3, 4, 16, CQ), b(3, 16, TOTAL),
        b(256, 1024), b(256, 1024), f(8, 1792), b(2, 8, 1024), b(6, 8, 1728), f(8, 128), f(2, 8, 1024), f(6, 8, 1728), f(8, 128),
        b(2, 128, 1024), b(16, TOTAL), b(2, 16, TOTAL), f(8, 1024), f(8, 1024),
        f(256, 128), f(256, 128), f(4, 256, 128),
        b(256, 1024), b(1024, 256), b(1024, 256), b(256, 512), b(256, 512), b(256, 512), b(256, 512),
        b(256, WIDE), b(256, WIDE), f(256, WIDE), b(2, 256, 256), f(2, 256, 256), f(256, WIDE), f(256, WIDE),
        b(REAL, 256), b(REAL, 256), b(3, REAL, 256), b(WIDE, 256), b(WIDE, 256),
        b(256, WIDE), f(256, 1024), b(256, 1024), b(256, 1024), b(128, 1024), b(128, 1024), f(128, 1024),
        b(256, 1024), b(128, 1024), f(128, 1024),
        b(256, 1024), f(256, WIDE), f(256, WIDE), b(256, WIDE), b(256, WIDE), b(256, WIDE),
        f(256, 1024), b(256, WIDE), b(256, 512), b(256, 512), b(256, WIDE),
        f(8, TOTAL), f(8, TOTAL), f(8, TOTAL),
        sem(52), sem(52), sem(16), sem(16), sem(13), sem(13), sem(24),
    ]


def per_device(
    inputs, cotangent, ln1_gain, ln1_bias, w_query, w_key, w_value, w_gate, w_out,
    ln2_gain, ln2_bias, w_mlp_gate, w_mlp_up, w_mlp_down,
):
    cosine, sine = tables()
    anywhere = pl.BlockSpec(memory_space=pl.ANY)
    here = pl.BlockSpec(memory_space=pltpu.VMEM)
    tokens = jax.ShapeDtypeStruct((128, 1024), BF16)
    square = jax.ShapeDtypeStruct((8, 1024), F32)
    wide = jax.ShapeDtypeStruct((8, 1728), F32)
    small = jax.ShapeDtypeStruct((1, 8), F32)
    results = [tokens] * 2 + [square] * 2 + [wide] * 6
    vectors = (ln1_gain, ln1_bias, ln2_gain, ln2_bias)
    out, gin, vec, *grads = pl.pallas_call(
        kernel,
        out_shape=results[:2] + [jax.ShapeDtypeStruct((8, 128), F32)] + results[2:],
        in_specs=[here] * 4 + [anywhere] * 12,
        out_specs=[anywhere] * 11,
        scratch_shapes=scratch(),
        compiler_params=pltpu.CompilerParams(
            collective_id=0, has_side_effects=True, vmem_limit_bytes=64 << 20
        ),
        name="block",
    )(
        *(v.reshape(1, 8) for v in vectors), inputs[0], cotangent[0], w_query, w_key, w_value, w_gate, w_out.T,
        w_mlp_gate, w_mlp_up, w_mlp_down.T, jnp.asarray(cosine), jnp.asarray(sine),
    )
    *smalls, out, gin, gq, gk, gv, gg, go, gmg, gmu, gmd = pl.pallas_call(
        hand_over,
        out_shape=[small] * 4 + results,
        in_specs=[anywhere] * 11,
        out_specs=[here] * 4 + [anywhere] * 10,
        scratch_shapes=[pltpu.VMEM((8, 128), F32)]
        + [pltpu.VMEM(r.shape, r.dtype) for r in results]
        + [pltpu.SemaphoreType.DMA((21,))],
        compiler_params=pltpu.CompilerParams(vmem_limit_bytes=64 << 20),
        name="hand_over",
    )(vec, out, gin, *grads)
    a, b, c, d = (v.reshape(8) for v in smalls)
    return out[None], gin[None], a, b, gq, gk, gv, gg, go.T, c, d, gmg, gmu, gmd.T


def solution(mesh):
    both = ("dp", "seq")
    row, col, vec, tokens = P(both, None), P(None, both), P(both), P("dp", "seq", None)
    return jax.shard_map(
        per_device,
        mesh=mesh,
        in_specs=(tokens, tokens, vec, vec, row, row, row, row, col, vec, vec, row, row, col),
        out_specs=(tokens, tokens, vec, vec, row, row, row, row, col, vec, vec, row, row, col),
        check_vma=False,
    )
```

```python
import functools

import jax
import jax.numpy as jnp
import numpy as np
from jax import lax
from jax.experimental import pallas as pl
from jax.experimental.pallas import tpu as pltpu
from jax.sharding import PartitionSpec as P

MESH = pl.DeviceIdType.MESH
F32 = jnp.float32
BF16 = jnp.bfloat16
EPS = 1e-05
VH = 432

CK, CV, CQ, CG, CO, CMG, CMU, CMD, TOTAL = 0, 512, 1408, 1920, 2816, 3712, 4608, 5504, 6400
WIDE = 896
REAL = 864
VTILE = CV + 768


def cut(start, *tiles):
    parts = []
    for part, n in enumerate(tiles):
        parts.append((part, start, 128 * n))
        start += 128 * n
    return tuple(parts)


GATHERS = (
    cut(CK, 4, 4, 3), cut(CQ, 5, 1, 5), cut(CO, 2, 2, 3), cut(CMG, 6, 4, 4), cut(CMD, 2, 2, 3),
)
KV = cut(CK, 4, 4, 3)
KV_EARLY, KV_LATE = cut(CK, 4, 4, 2), ((2, VTILE, 128),)
QG, OUT, MLP, DOWN = cut(CQ, 4, 2, 5), cut(CO, 2, 2, 3), cut(CMG, 7, 3, 4), cut(CMD, 1, 3, 3)
FORWARD_GATHERS = (1, 2, 3, 4,)
PIECES = ((slice(0, 224), 0), (slice(224, 432), 0), (slice(432, 656), 1), (slice(656, 864), 1))
ORDERS = (("x", "y", "z"), ("y", "z", "x"), ("z", "x", "y"))
ZYX = ("z", "y", "x")


def tables():
    half = 128
    inverse = np.power(10000.0, -np.arange(half, dtype=np.float64) / half)
    angles = np.arange(1024, dtype=np.float64)[:, None] * inverse[None, :]
    return (
        np.cos(angles).astype(np.float32).reshape(4, 256, half),
        np.sin(angles).astype(np.float32).reshape(4, 256, half),
    )


def mm(a, b):
    return lax.dot_general(a, b, (((1,), (0,)), ((), ())), preferred_element_type=F32)


def mm_nt(a, b):
    return lax.dot_general(a, b, (((1,), (1,)), ((), ())), preferred_element_type=F32)


def loop(n, body):
    def step(i, carry):
        body(i)
        return carry

    lax.fori_loop(0, n, step, 0)


def each(n, body):
    for i in range(n):
        body(i)


def kernel(
    gain1_in, bias1_in, gain2_in, bias2_in, x_in, g_in, wq_in, wk_in, wv_in, wg_in, wo_in, wmg_in, wmu_in, wmd_in,
    cos_in, sin_in, out_ref, gin_ref, vec_ref, gq_ref, gk_ref, gv_ref, gg_ref, go_ref, gmg_ref, gmu_ref, gmd_ref,
    *scratch,
):
    (
        W, Gd, RA, RB1, R2A, R2B, R2C, R3, X, G, WS, IN8, INW, INV, OUT8, OUTW, OUTVEC, OUTV, PSEND, PRECV, VEC, VA, COS, SIN, STAT,
        NORM, NORMT, TT, Q, QS, K, KW, V, GGP, GATE, WT, MASK, MIX, GRP,
        UT, TOT, STATES, CT, GUT, GATED, MID, SB, RB, SBO, RBO, OWN1, RB2, RB3, OWN2,
        SEC, ACT, BCT, HID, GGL, GUL, GM, GMX, GQ, GK, GV, FSEND, FRECV, KEEP,
        way_s, way_r, st_s, st_r, ex_s, ex_r, loc,
    ) = scratch
    S1, S2, VT, RSTD, GML = RB1.at[0], R2B.at[0], TT.at[0:WIDE], MIX, SEC
    dp = lax.axis_index("dp")
    sq = lax.axis_index("seq")
    me = {"z": dp // 4, "y": dp % 4, "x": sq // 2}
    c = sq % 2
    c0 = (c == 0).astype(F32)
    c1 = (c == 1).astype(F32)

    def shifted(axis, k):
        p = dict(me)
        p[axis] = (me[axis] + k) % 4
        return p

    def device(p, core):
        return (p["z"] * 4 + p["y"], p["x"] * 2 + core)

    sibling = device(me, 1 - c)

    def remote(src, dst, ss, rs, dev):
        return pltpu.make_async_remote_copy(
            src_ref=src, dst_ref=dst, send_sem=ss, recv_sem=rs, device_id=dev, device_id_type=MESH
        )

    rows_own = pl.ds(pl.multiple_of(c * 128, 128), 128)
    rows_sib = pl.ds(pl.multiple_of((1 - c) * 128, 128), 128)
    fetch = [
        pltpu.make_async_copy(src, dst, loc.at[i])
        for src, dst, i in (
            (wq_in, IN8.at[0], 0), (wk_in, IN8.at[1], 0), (wv_in, INW.at[0], 1), (wg_in, INW.at[1], 1),
            (wo_in, INW.at[2], 1), (wmg_in, INW.at[3], 1), (wmu_in, INW.at[4], 1), (wmd_in, INW.at[5], 1),
            (x_in, X.at[rows_own, :], 2), (g_in, G.at[rows_own, :], 3),
            (cos_in.at[me["x"]], COS, 4), (sin_in.at[me["x"]], SIN, 5),
        )
    ]
    for copy in fetch:
        copy.start()
    barrier = pltpu.get_barrier_semaphore()
    pl.semaphore_signal(barrier, inc=1, device_id=sibling, device_id_type=MESH)
    for axis in ZYX:
        for k in (1, 2, 3):
            pl.semaphore_signal(
                barrier, inc=1, device_id=device(shifted(axis, k), c), device_id_type=MESH
            )

    def put(ref, col, own):
        both = jnp.concatenate([own * c0, own * c1], axis=0)
        ref[:, col : col + own.shape[1]] = both.astype(BF16)

    def pack(col, h0, h1):
        put(PRECV.at[0], col, h0 * c0 + h1 * c1)
        put(PSEND, col, h0 * c1 + h1 * c0)

    def pack_square(i, col):
        w = IN8[i].astype(F32)
        pack(col, w[:, :512], w[:, 512:])

    def pack_wide(i, col):
        lane = lax.broadcasted_iota(jnp.int32, (8, WIDE), 1)
        WS[:, 1664:1792] = jnp.zeros((8, 128), F32)
        WS[:, :1728] = INW[i].astype(F32)
        h0 = jnp.where(lane < REAL, WS[:, :WIDE], 0.0)
        h1 = pltpu.roll(WS[:, 768:1792], 1024 - 96, 1)[:, :WIDE]
        h1 = jnp.where(lane < REAL, h1, 0.0)
        if col == CV:
            v = jnp.concatenate([INV[...], jnp.zeros((120, 128), F32)], axis=0).T
            v = pltpu.roll(v[0:8, :], 96, 1)
            v = jnp.concatenate([jnp.zeros((8, 768), F32), v], axis=1)
            h0 = h0 + v
            h1 = h1 + v
        pack(col, h0, h1)

    def exchange(first, last, i):
        s = pl.ds(first, last - first)
        copy = remote(PSEND.at[:, s], PRECV.at[1, :, s], ex_s.at[i], ex_r.at[i], sibling)
        copy.start()
        return copy

    def assemble(copy, first, last):
        copy.wait_recv()
        for col in range(first, last, 640):
            s = pl.ds(col, min(640, last - col))
            W[me["z"], me["y"], me["x"], :, s] = (
                PRECV[0, :, s].astype(F32) + PRECV[1, :, s].astype(F32)
            ).astype(BF16)

    INV[...] = jnp.zeros_like(INV)
    for i, ref in enumerate((gain1_in, bias1_in, gain2_in, bias2_in)):
        INV[i : i + 1, 0:8] = ref[...].astype(F32)
    pltpu.make_async_copy(IN8, IN8, loc.at[0]).wait()
    pltpu.make_async_copy(INW, INW, loc.at[1]).wait()
    pack_square(1, CK)
    pack_wide(0, CV)
    pl.semaphore_wait(barrier, 10)
    e_first = exchange(0, CQ, 0)
    pack_square(0, CQ)
    for i, col in enumerate((CG, CO, CMG, CMU, CMD)):
        pack_wide(i + 1, col)
    e_rest = exchange(CQ, TOTAL, 8)
    fetch[8].wait()
    e_x = remote(X.at[rows_own, :], X.at[rows_own, :], ex_s.at[1], ex_r.at[1], sibling)
    e_x.start()
    fetch[9].wait()
    e_g = remote(G.at[rows_own, :], G.at[rows_own, :], ex_s.at[2], ex_r.at[2], sibling)
    e_g.start()

    count = [0]

    def stage(kind, total):
        count[0] += 1
        return way_s.at[kind], way_r.at[count[0] - 1], total

    def send(where, src, dst, dev):
        remote(src, dst, where[0], where[1], dev).start()

    def arrived(where):
        ss, rs, total = where
        remote(total, total, ss, rs, sibling).wait_recv()

    def columns(parts):
        return pl.ds(parts[0][1], sum(n for _, _, n in parts))

    def gather(group, phase, forward=False):
        s = columns(GATHERS[group])
        halves = phase == 2 or (phase == 1 and group in FORWARD_GATHERS)
        if phase == 1:
            where = stage(3 if forward else 2 if halves else 1, W.at[0, 0 : 1 if forward else 2 if halves else 3, :, :, s])
        else:
            where = stage(5, W.at[0, :, :, :, s]) if forward else stage(4, W.at[0:2, :, :, :, s])
        gather_parts(where, GATHERS[group], phase, halves, forward)
        return where

    def gather_parts(where, parts, phase, halves, forward):
        for part, col, n in parts:
            order = ORDERS[part]
            axis = order[phase]
            for i, k in enumerate((1, 3) if halves else (1, 2, 3)):
                idx = {a: me[a] for a in ZYX}
                for a in order[:phase]:
                    idx[a] = slice(None)
                if forward:
                    idx[axis] = (me[axis] - k) % 4
                    idx[[a for a in ZYX if a in order[:phase]][0]] = pl.ds(2 * i, 2)
                src = W.at[tuple(idx[a] for a in ZYX) + (slice(None), pl.ds(col, n))]
                send(where, src, src, device(shifted(axis, k), c))

    def early_third(g):
        p4[g] = stage(4, W.at[0:2, :, :, :, columns(GATHERS[g])])
        for part, col, n in GATHERS[g]:
            a, b, axis = ORDERS[part]
            idx = {a: slice(None), b: me[b], axis: me[axis]}
            src = W.at[tuple(idx[q] for q in ZYX) + (slice(None), pl.ds(col, n))]
            for k in (1, 3):
                send(p4[g], src, src, device(shifted(axis, k), c))

    def late_third(g):
        for part, col, n in GATHERS[g]:
            a, b, axis = ORDERS[part]
            for j in (1, 2, 3):
                idx = {a: slice(None), b: (me[b] + j) % 4, axis: me[axis]}
                src = W.at[tuple(idx[q] for q in ZYX) + (slice(None), pl.ds(col, n))]
                for k in (1, 3):
                    send(p4[g], src, src, device(shifted(axis, k), c))

    def first_phase(groups, first, last):
        where = stage(0, W.at[0, 0, 0:3, :, first:last])
        for g in groups:
            gather_parts(where, GATHERS[g], 0, False, False)
        return where

    assemble(e_first, 0, CQ)
    p1 = {0: first_phase((0,), 0, CQ)}
    assemble(e_rest, CQ, TOTAL)
    p1[1] = first_phase((1, 2, 3, 4), CQ, TOTAL)
    p2, p3, p4, p5 = {}, {}, {}, {}
    waited = []

    def w1(g):
        at = min(g, 1)
        if at not in waited:
            waited.append(at)
            arrived(p1[at])
        p2[g] = gather(g, 1)

    def w2(g):
        if g in FORWARD_GATHERS:
            arrived(p2[g])
            p3[g] = gather(g, 1, True)

    def w3(g):
        arrived(p3[g] if g in FORWARD_GATHERS else p2[g])
        late_third(g)

    def w4(g):
        arrived(p4[g])
        p5[g] = gather(g, 2, True)

    def w5(g):
        arrived(p5[g])

    def wcols(col, n):
        return W[:, :, :, :, col : col + n].reshape(1024, n)

    def wrows(i, col, n):
        return W[i, :, :, :, col : col + n].reshape(256, n)

    def fwd(a, col, n, emit):
        for at in range(0, n, 256):
            w = min(256, n - at)
            emit(at, w, mm(a[...], wcols(col + at, w)))

    def grad(at, b, col):
        n = b.shape[1]

        def body(i):
            r = mm(at[pl.ds(i * 256, 256), :], b[...])
            Gd[i, :, :, :, col : col + n] = r.astype(BF16).reshape(4, 4, 16, n)

        each(4, body)

    def rows(i, n=64):
        return pl.ds(pl.multiple_of(i * n, n), n)

    lanes = lax.broadcasted_iota(jnp.int32, (64, WIDE), 1)
    in0 = lanes < VH
    in1 = (lanes >= VH) & (lanes < REAL)
    real = lanes < REAL

    def log_gamma(hh):
        g0 = float(np.log(1.0 - 2.0 ** (-5.0 - hh)))
        g1 = float(np.log(1.0 - 2.0 ** (-7.0 - hh)))
        return jnp.where(c == 0, jnp.float32(g0), jnp.float32(g1))

    lg = [log_gamma(0), log_gamma(1)]

    def mask_body(i):
        ii = lax.broadcasted_iota(jnp.int32, (64, 256), 0) + i * 64
        jj = lax.broadcasted_iota(jnp.int32, (64, 256), 1)
        d = (ii - jj).astype(F32)
        for hh in range(2):
            MASK[hh, rows(i), :] = jnp.where(d >= 0, jnp.exp(jnp.maximum(d, 0.0) * lg[hh]), 0.0)

    loop(4, mask_body)
    VA[...] = jnp.zeros_like(VA)
    e_x.wait_recv()
    e_g.wait_recv()

    def norm(v):
        mean = jnp.mean(v, axis=-1, keepdims=True)
        center = v - mean
        spread = jnp.mean(center * center, axis=-1, keepdims=True)
        rstd = lax.rsqrt(spread + EPS)
        return center * rstd, rstd, mean

    def ln1_stats(i):
        xh, rstd, mean = norm(X[rows(i), :].astype(F32))
        GM[rows(i), :] = xh
        STAT[0, rows(i), :] = jnp.broadcast_to(mean, (64, 128))
        STAT[1, rows(i), :] = jnp.broadcast_to(rstd, (64, 128))

    loop(4, ln1_stats)
    fetch[10].wait()
    fetch[11].wait()

    def transpose(src, dst):
        dst[...] = src[...].T

    def vector(i):
        return VEC[i : i + 1, :]

    def ln1():
        VEC[...] = wcols(VTILE, 128).astype(F32).T[96:104, :]
        gain1, bias1 = vector(0), vector(1)

        def ln1(i):
            NORM[rows(i), :] = (GM[rows(i), :] * gain1 + bias1).astype(BF16)

        loop(4, ln1)

    def rotated(dst, dst2, offset, sign, scale):
        def emit(at, w, r):
            hh = at // 256
            u, z = r[:, :128], r[:, 128:]
            co, si = COS[...], SIN[...]
            a0 = ((u * co - z * si) * scale).astype(BF16)
            a1 = ((u * si + z * co) * scale).astype(BF16)
            spot = lax.broadcasted_iota(jnp.int32, (256, 128), 0).astype(F32)
            sc = jnp.exp((spot * sign + offset) * lg[hh])
            dst[:, at : at + 128] = a0
            dst[:, at + 128 : at + 256] = a1
            dst2[:, at : at + 128] = (a0.astype(F32) * sc).astype(BF16)
            dst2[:, at + 128 : at + 256] = (a1.astype(F32) * sc).astype(BF16)

        return emit

    def emit_v(at, w, r):
        col = lax.broadcasted_iota(jnp.int32, (256, w), 1) + at
        V[:, at : at + w] = jnp.where(col < REAL, r, 0.0).astype(BF16)

    def kvu():
        fwd(NORM, CK, 512, rotated(K, KW, 255.0, -1.0, 0.0625))
        fwd(NORM, CV, WIDE, emit_v)
        transpose(V, VT)
        for hh in range(2):
            r = mm(VT[VH * hh : VH * (hh + 1), :], KW[:, 256 * hh : 256 * (hh + 1)])
            UT[VH * hh : VH * (hh + 1), :] = r.astype(BF16)

    def states(src, base, back):
        x = me["x"]
        near = dict(me, x=x + 1 - 2 * (x % 2))
        far = dict(me, x=3 - x)
        low = x < 2
        sends = (x != 0) if back else (x != 3)
        gets = (x != 1) if back else (x != 2)
        passes = ~low if back else low
        steps = []
        for i, (at, hh) in enumerate(PIECES):
            t = base + i
            slot = 1 if back else 0
            one = remote(src.at[at], STATES.at[slot, at], st_s.at[base // 4], st_r.at[t], device(near, c))
            pl.when(sends)(one.start)
            steps.append(one)

        def second(i):
            at, hh = PIECES[i]
            t = base + 4 + i
            two = remote(TOT.at[at], STATES.at[2, at], st_s.at[base // 4 + 1], st_r.at[t], device(far, c))

            def total():
                steps[i].wait_recv()
                own = src[at, :].astype(F32)
                got = STATES[slot, at, :].astype(F32)
                g = jnp.exp(256.0 * lg[hh])
                first = (x % 2 == 1) if back else (x % 2 == 0)
                TOT[at, :] = jnp.where(first, own * g + got, own + got * g).astype(BF16)
                two.start()

            pl.when(passes)(total)
            return two

        def finish(dst):
            dst[...] = jnp.zeros_like(dst)
            for i, two in enumerate(twos):
                at, hh = PIECES[i]
                g = jnp.exp(256.0 * lg[hh])

                def single():
                    dst[at, :] = STATES[slot, at, :]

                def double():
                    two.wait_recv()
                    dst[at, :] = STATES[2, at, :]

                def triple():
                    steps[i].wait_recv()
                    two.wait_recv()
                    total = STATES[2, at, :].astype(F32) * g
                    dst[at, :] = (total + STATES[slot, at, :].astype(F32)).astype(BF16)

                one, pair, three = (2, 1, 0) if back else (1, 2, 3)
                pl.when(x == one)(single)
                pl.when(x == pair)(double)
                pl.when(x == three)(triple)

        def sent():
            one = remote(src, src, st_s.at[base // 4], st_r.at[base], sibling)
            two = remote(TOT, TOT, st_s.at[base // 4 + 1], st_r.at[base], sibling)
            pl.when(sends)(one.wait_send)
            pl.when(passes)(two.wait_send)

        twos = []

        def middle(*pieces):
            twos.extend(second(i) for i in pieces)

        return middle, finish, sent

    def join(dst, h0, h1):
        pick = lax.broadcasted_iota(jnp.int32, (256, 128), 1) < VH - 384
        dst[:, 0:384] = h0[:, :384]
        dst[:, 384:512] = jnp.where(pick, h0[:, 384:512], h1[:, :128])
        dst[:, 512:896] = h1[:, 128:512]

    def qi():
        fwd(NORM, CQ, 512, rotated(Q, QS, 1.0, 1.0, 1.0))
        for hh in range(2):
            raw = mm_nt(Q[:, 256 * hh : 256 * (hh + 1)], K[:, 256 * hh : 256 * (hh + 1)])
            WT[hh] = (raw * MASK[hh]).astype(BF16)
        join(MIX, mm(WT[0], V[:, 0:512]), mm(WT[1], V[:, 384:896]))

    def emit_gate(at, w, r):
        GATE[:, at : at + w] = r

    def gate():
        fwd(NORM, CG, WIDE, emit_gate)

    def cross():
        join(GRP, mm_nt(QS[:, 0:256], CT[0:512, :]), mm_nt(QS[:, 256:512], CT[384:896, :]))

    def heads_mean(v):
        m0 = jnp.sum(jnp.where(in0, v, 0.0), axis=-1, keepdims=True) * (1.0 / VH)
        m1 = jnp.sum(jnp.where(in1, v, 0.0), axis=-1, keepdims=True) * (1.0 / VH)
        return jnp.where(in0, m0, m1)

    def group_norm(i):
        m = MIX[rows(i), :] + GRP[rows(i), :]
        center = m - heads_mean(m)
        rstd = lax.rsqrt(heads_mean(center * center) + EPS)
        grouped = jnp.where(real, center * rstd, 0.0)
        GRP[rows(i), :] = grouped
        RSTD[rows(i), :] = rstd
        gate = GATE[rows(i), :]
        GATED[rows(i), :] = (gate * jax.nn.sigmoid(gate) * grouped).astype(BF16)

    def gn():
        loop(4, group_norm)

    def out_body(i):
        r = mm_nt(GATED[...], wrows(i, CO, WIDE))
        s = pl.ds(i * 256, 256)
        MID[:, s] = r
        SB[:, s] = r.astype(BF16)
        remote(SB.at[:, s], RB.at[:, s], ex_s.at[3], ex_r.at[3], sibling).start()

    def out():
        each(4, out_body)

    e_mid = remote(SB, RB, ex_s.at[3], ex_r.at[3], sibling)

    def ln2():
        gain2, bias2 = vector(2), vector(3)

        def ln2_rows(i):
            m = X[rows(i), :].astype(F32) + MID[rows(i), :] + RB[rows(i), :].astype(F32)
            MID[rows(i), :] = m
            xh, rstd, mean = norm(m)
            STAT[2, rows(i), :] = jnp.broadcast_to(mean, (64, 128))
            STAT[3, rows(i), :] = jnp.broadcast_to(rstd, (64, 128))
            SEC[rows(i), :] = (xh * gain2 + bias2).astype(BF16)

        e_mid.wait_recv()
        loop(4, ln2_rows)

    def emit_act(at, w, r):
        ACT[:, at : at + w] = r

    def emit_bct(at, w, r):
        BCT[:, at : at + w] = r

    def gelu_rows(i):
        g = ACT[rows(i), :]
        u = BCT[rows(i), :]
        cdf = 0.5 * (1.0 + lax.erf(g * 0.7071067811865476))
        ge = g * cdf
        HID[rows(i), :] = (ge * u).astype(BF16)
        BCT[rows(i), :] = ge
        ACT[rows(i), :] = (cdf + g * jnp.exp(-0.5 * g * g) * 0.3989422804014327) * u

    def mlp():
        fwd(SEC, CMG, WIDE, emit_act)
        fwd(SEC, CMU, WIDE, emit_bct)

    def gelu():
        loop(4, gelu_rows)

    def place(axes, where):
        return tuple(where.get(a, slice(None)) for a in axes)

    def others(part, phase):
        order = ORDERS[part][::-1]
        return order[phase], [a for a in ZYX if a not in order[: phase + 1]], [a for a in ZYX if a not in order[:phase]]

    def scatter0(parts, late=None):
        s = columns(parts)
        early = stage(6, RA.at[:, :, :, :, s])
        late = late or stage(7, RB1.at[:, :, :, :, s])
        for where in (early, late):
            for part, col, n in parts:
                axis, rest, left = others(part, 0)
                s = (slice(None), pl.ds(col, n))
                for i, k in enumerate((1, 3)):
                    dev = device(shifted(axis, k), c)
                    if where is early:
                        src = Gd.at[place(left, {axis: (me[axis] + 2) % 4, rest[0]: pl.ds(2 * i, 2)}) + s]
                        send(where, src, RA.at[(i, slice(None), slice(None)) + s], dev)
                    else:
                        near = pl.ds(2 - 2 * i, 2)
                        src = Gd.at[place(left, {axis: (me[axis] + k) % 4, rest[0]: near}) + s]
                        send(where, src, RB1.at[(i, near, slice(None)) + s], dev)
        return early, late

    def scatter1(parts, where):
        early, late = where
        arrived(early)
        for part, col, n in parts:
            axis, rest, left = others(part, 0)
            s = (slice(None), pl.ds(col, n))
            for i, k in enumerate((1, 3)):

                def body(j):
                    own = Gd[place(left, {axis: (me[axis] + k) % 4, rest[0]: 2 * i + j}) + s]
                    at = (i, j, slice(None)) + s
                    RA[at] = (own.astype(F32) + RA[at].astype(F32)).astype(BF16)

                loop(2, body)
                src = RA.at[(i, slice(None), slice(None)) + s]
                dst = RB1.at[(i, pl.ds(2 * i, 2), slice(None)) + s]
                send(late, src, dst, device(shifted(axis, k), c))
        return late

    def scatter2(parts, late):
        arrived(late)
        direct = parts is KV
        if direct:
            early = stage(8, R2C.at[:, :, :, columns(parts)])
        else:
            early, late = stage(9, R2A.at[:, :, :, columns(parts)]), stage(10, R2B.at[:, :, :, columns(parts)])
        for part, col, n in parts:
            axis, rest, left = others(part, 0)
            s = (slice(None), pl.ds(col, n))

            def body(j):
                own = Gd[place(left, {axis: me[axis], rest[0]: j}) + s].astype(F32)
                at = (j, slice(None)) + s
                RB1[(0,) + at] = (own + RB1[(0,) + at].astype(F32) + RB1[(1,) + at].astype(F32)).astype(BF16)

            loop(4, body)
            axis, rest, left = others(part, 1)
            if direct:
                for k in (1, 2, 3):
                    to = shifted(axis, k)
                    src = S1.at[place(left, {axis: to[axis]}) + s]
                    send(early, src, R2C.at[(k - 1, slice(None)) + s], device(to, c))
                continue
            for i, k in enumerate((1, 3)):
                dev = device(shifted(axis, k), c)
                src = S1.at[place(left, {axis: (me[axis] + 2) % 4, rest[0]: pl.ds(2 * i, 2)}) + s]
                send(early, src, R2A.at[(i, slice(None)) + s], dev)
                near = pl.ds(2 - 2 * i, 2)
                src = S1.at[place(left, {axis: (me[axis] + k) % 4, rest[0]: near}) + s]
                send(late, src, R2B.at[(i, near) + s], dev)
        return early, late

    def scatter3(parts, where):
        if parts is KV:
            return where[0]
        early, late = where
        arrived(early)
        for part, col, n in parts:
            axis, rest, left = others(part, 1)
            s = (slice(None), pl.ds(col, n))
            for i, k in enumerate((1, 3)):
                half = pl.ds(2 * i, 2)
                own = S1[place(left, {axis: (me[axis] + k) % 4, rest[0]: half}) + s]
                at = (i, slice(None)) + s
                R2A[at] = (own.astype(F32) + R2A[at].astype(F32)).astype(BF16)
                send(late, R2A.at[at], R2B.at[(i, half) + s], device(shifted(axis, k), c))
        return late

    def scatter4(parts, where):
        arrived(where)
        where = stage(11, R3.at[:, :, columns(parts)])
        came = [R2C.at[k] for k in range(3)] if parts is KV else [R2B.at[k] for k in range(2)]
        for part, col, n in parts:
            axis, rest, left = others(part, 1)
            s = (slice(None), pl.ds(col, n))
            t = S1[place(left, {axis: me[axis]}) + s].astype(F32)
            for ref in came:
                t = t + ref[(slice(None),) + s].astype(F32)
            S2[(slice(None),) + s] = t.astype(BF16)
            axis, rest, left = others(part, 2)
            for k in (1, 2, 3):
                to = shifted(axis, k)
                send(where, S2.at[(to[axis],) + s], R3.at[(k - 1,) + s], device(to, c))
        return where

    def scatter5(parts, where, i):
        arrived(where)
        for part, col, n in parts:
            axis, rest, left = others(part, 2)
            s = (slice(None), pl.ds(col, n))
            t = S2[(me[axis],) + s].astype(F32)
            for k in range(3):
                t = t + R3[(k,) + s].astype(F32)
            KEEP[:, s[1]] = t[0:8, :] * c0 + t[8:16, :] * c1
            FSEND[:, s[1]] = t[0:8, :] * c1 + t[8:16, :] * c0
        s = columns(parts)
        copy = remote(FSEND.at[:, s], FRECV.at[:, s], ex_s.at[7], ex_r.at[9 + i], sibling)
        copy.start()
        return copy

    def halves(col, n):
        keep = KEEP[:, col : col + n]
        got = FRECV[:, col : col + n]
        return keep * c0 + got * c1, keep * c1 + got * c0

    def finish(copy, *cols):
        copy.wait_recv()
        puts = []
        for col in cols:
            if col in (CQ, CK):
                i = (CQ, CK).index(col)
                lo, hi = halves(col, 512)
                OUT8[i, :, :512] = lo
                OUT8[i, :, 512:] = hi
                puts.append((OUT8.at[i], (gq_ref, gk_ref)[i], 8))
            elif col == VTILE:
                lo, hi = halves(col, 128)
                OUTVEC[...] = jnp.concatenate([lo + hi, jnp.zeros((120, 128), F32)], axis=0).T[96:104, :]
                puts.append((OUTVEC, vec_ref, 9))
            else:
                i = (CV, CG, CO, CMG, CMU, CMD).index(col)
                lo, hi = halves(col, WIDE)
                moved = pltpu.roll(jnp.concatenate([hi, jnp.zeros((8, 128), F32)], axis=1), 96, 1)
                first96 = lax.broadcasted_iota(jnp.int32, (8, 128), 1) < 96
                OUTW[i, :, 0:768] = lo[:, 0:768]
                OUTW[i, :, 768:896] = jnp.where(first96, lo[:, 768:896], moved[:, 0:128])
                OUTW[i, :, 896:1728] = moved[:, 128:960]
                puts.append((OUTW.at[i], (gv_ref, gg_ref, go_ref, gmg_ref, gmu_ref, gmd_ref)[i], 10))
        for src, dst, at in puts:
            pltpu.make_async_copy(src, dst, loc.at[at]).start()
        return copy

    def emit_hidden(at, w, r):
        GGL[:, at : at + w] = (r * ACT[:, at : at + w]).astype(BF16)
        GUL[:, at : at + w] = (r * BCT[:, at : at + w]).astype(BF16)

    def gmd():
        transpose(G, TT)
        grad(TT, HID, CMD)

    def gh():
        fwd(G, CMD, WIDE, emit_hidden)

    def second_body(i):
        r = mm_nt(GGL[...], wrows(i, CMG, WIDE)) + mm_nt(GUL[...], wrows(i, CMU, WIDE))
        s = pl.ds(i * 256, 256)
        GM[:, s] = r
        SB[:, s] = r.astype(BF16)
        remote(SB.at[:, s], RB2.at[:, s], ex_s.at[5], ex_r.at[5], sibling).start()

    def gs():
        e_mid.wait_send()
        each(4, second_body)

    e_sec = remote(SB, RB2, ex_s.at[5], ex_r.at[5], sibling)

    def gmg():
        transpose(SEC, TT)
        grad(TT, GGL, CMG)

    def gmu():
        transpose(SEC, TT)
        grad(TT, GUL, CMU)

    def norm_back(gs, v, gain, at, which):
        rstd = STAT[which + 1, at, 0:1]
        xh = (v - STAT[which, at, 0:1]) * rstd
        gx = gs * gain
        m0 = jnp.mean(gx, axis=-1, keepdims=True)
        m1 = jnp.mean(gx * xh, axis=-1, keepdims=True)
        return rstd * (gx - m0 - xh * m1), jnp.sum(gs * xh, axis=0, keepdims=True), jnp.sum(gs, axis=0, keepdims=True)

    def ln2b():
        gain2 = vector(2)

        def ln2_back(i):
            gs = GM[rows(i), :] + RB2[rows(i), :].astype(F32)
            part, ggain, gbias = norm_back(gs, MID[rows(i), :], gain2, rows(i), 2)
            gm = G[rows(i), :].astype(F32) + part
            GM[rows(i), :] = gm
            GML[rows(i), :] = gm.astype(BF16)
            mine = (i // 2 == c).astype(F32)
            VA[2:3, :] += ggain * mine
            VA[3:4, :] += gbias * mine

        e_sec.wait_recv()
        loop(4, ln2_back)

    def gout():
        transpose(GML, TT)
        grad(TT, GATED, CO)

    def emit_gated(at, w, r):
        ACT[:, at : at + w] = r

    def gated():
        fwd(GML, CO, WIDE, emit_gated)

    def group_back(i):
        gr = ACT[rows(i), :]
        z = GATE[rows(i), :]
        sg = jax.nn.sigmoid(z)
        grp = GRP[rows(i), :]
        GGP[rows(i), :] = (gr * (sg * (1.0 + z * (1.0 - sg))) * grp).astype(BF16)
        gg = gr * (z * sg)
        gmx = RSTD[rows(i), :] * (gg - heads_mean(gg) - grp * heads_mean(gg * grp))
        GMX[rows(i), :] = jnp.where(real, gmx, 0.0).astype(BF16)

    def groupb():
        loop(4, group_back)

    def gc():
        transpose(GMX, VT)
        u_sent()
        for hh in range(2):
            r = mm(VT[VH * hh : VH * (hh + 1), :], QS[:, 256 * hh : 256 * (hh + 1)])
            UT[VH * hh : VH * (hh + 1), :] = r.astype(BF16)

    def gg():
        grad(NORMT, GGP, CG)

    def gq():
        grad(NORMT, GQ, CQ)

    wide = lax.broadcasted_iota(jnp.int32, (256, 512), 1)
    windows = (slice(0, 512), slice(384, 896))

    def window(ref, hh):
        a = ref[:, windows[hh]]
        keep = wide < VH if hh == 0 else wide >= VH - 384
        return jnp.where(keep, a, jnp.zeros_like(a))

    def spots(hh, offset, sign):
        spot = lax.broadcasted_iota(jnp.int32, (256, 128), 0).astype(F32)
        return jnp.exp((spot * sign + offset) * lg[hh])

    def unrotated(dst, src, hh, cross, offset, sign, scale):
        sc = spots(hh, offset, sign)
        co, si = COS[...], SIN[...]
        a, b = slice(256 * hh, 256 * hh + 128), slice(256 * hh + 128, 256 * hh + 256)
        u = (src[:, a] + cross[:, :128] * sc) * scale
        z = (src[:, b] + cross[:, 128:] * sc) * scale
        dst[:, a] = (u * co + z * si).astype(BF16)
        dst[:, b] = (z * co - u * si).astype(BF16)

    def intra():
        gvi = []
        for hh in range(2):
            h = slice(256 * hh, 256 * (hh + 1))
            gm = window(GMX, hh)
            vw = V[:, windows[hh]]
            graw = (mm_nt(gm, vw) * MASK[hh]).astype(BF16)
            ACT[:, h] = mm(graw, K[:, h])
            BCT[:, h] = mm(graw.T, Q[:, h])
            gvi.append(mm(WT[hh].T, gm))
            unrotated(GQ, ACT, hh, mm(gm, CT[windows[hh], :]), 1.0, 1.0, 1.0)
        join(MIX, gvi[0], gvi[1])

    def down_body(i):
        r = mm_nt(HID[...], wrows(i, CMD, WIDE))
        s = pl.ds(i * 256, 256)
        OWN1[:, s] = r[0:128] * c0 + r[128:256] * c1
        SBO[:, s] = (r[0:128] * c1 + r[128:256] * c0).astype(BF16)

    e_out = remote(SBO, RBO, ex_s.at[4], ex_r.at[4], sibling)
    put_out = pltpu.make_async_copy(OUTV.at[0], out_ref, loc.at[6])
    put_gin = pltpu.make_async_copy(OUTV.at[1], gin_ref, loc.at[7])

    def down():
        each(4, down_body)
        e_out.start()

    def normed_first(i):
        r = mm_nt(GQ[...], wrows(i, CQ, 512)) + mm_nt(GGP[...], wrows(i, CG, WIDE))
        MID[:, pl.ds(i * 256, 256)] = r

    def pn1():
        e_out.wait_recv()
        OUTV[0] = (MID[rows_own, :] + OWN1[...] + RBO[...].astype(F32)).astype(BF16)
        put_out.start()
        each(4, normed_first)

    def kvb():
        gvs = []
        for hh in range(2):
            h = slice(256 * hh, 256 * (hh + 1))
            unrotated(GK, BCT, hh, mm(window(V, hh), GUT[windows[hh], :]), 255.0, -1.0, 0.0625)
            gvs.append(mm_nt(KW[:, h], GUT[windows[hh], :]))
        join(ACT, gvs[0], gvs[1])
        GV[...] = (MIX[...] + ACT[...]).astype(BF16)

    def gk():
        grad(NORMT, GK, CK)

    def gv():
        grad(NORMT, GV, CV)

    def normed_body(i):
        s = pl.ds(i * 256, 256)
        r = MID[:, s] + mm_nt(GK[...], wrows(i, CK, 512)) + mm_nt(GV[...], wrows(i, CV, WIDE))
        OWN2[:, s] = r[0:128] * c0 + r[128:256] * c1
        SBO[:, s] = (r[0:128] * c1 + r[128:256] * c0).astype(BF16)
        remote(SBO.at[:, s], RB3.at[:, s], ex_s.at[6], ex_r.at[6], sibling).start()

    def pn2():
        e_out.wait_send()
        each(4, normed_body)

    e_norm = remote(SBO, RB3, ex_s.at[6], ex_r.at[6], sibling)

    def ln1b():
        gain1 = vector(0)

        def ln1_back(i):
            at = pl.ds(pl.multiple_of(c * 128 + i * 64, 64), 64)
            gs = OWN2[rows(i), :] + RB3[rows(i), :].astype(F32)
            part, ggain, gbias = norm_back(gs, X[at, :].astype(F32), gain1, at, 0)
            OUTV[1, rows(i), :] = (GM[at, :] + part).astype(BF16)
            VA[0:1, :] += ggain
            VA[1:2, :] += gbias

        e_norm.wait_recv()
        loop(2, ln1_back)
        put_gin.start()
        vectors = jnp.concatenate([jnp.zeros((96, 1024), F32), VA[...], jnp.zeros((24, 1024), F32)], axis=0).T
        tile = slice(VTILE, VTILE + 128)
        Gd[:, :, :, :, tile] = (
            Gd[:, :, :, :, tile].astype(F32) + vectors.reshape(4, 4, 4, 16, 128)
        ).astype(BF16)

    w1(0)
    w1(2)
    early_third(0)
    w1(1)
    w1(3)
    early_third(1)
    w3(0)
    early_third(3)
    w2(2)
    w2(1)
    w1(4)
    early_third(2)
    w4(0)
    w2(3)
    w3(1)
    w3(2)
    early_third(4)
    w5(0)
    ln1()
    w2(4)
    kvu()
    u_middle, u_finish, u_sent = states(UT, 0, False)
    w3(3)
    w4(1)
    u_middle(0, 1, 2, 3)
    w4(2)
    w3(4)
    w5(1)
    w4(3)
    gate()
    qi()
    u_finish(CT)
    w5(2)
    cross()
    gn()
    out()
    transpose(NORM, NORMT)
    w4(4)
    ln2()
    w5(3)
    mlp()
    gelu()
    gmd()
    r_down = scatter0(DOWN)
    w5(4)
    gh()
    gs()
    gmg()
    gmu()
    r_mlp = scatter0(MLP)
    ln2b()
    gout()
    gated()
    groupb()
    gc()
    c_middle, c_finish, c_sent = states(UT, 8, True)
    r_out = scatter0(OUT)
    intra()
    gg()
    down()
    gq()
    r_qg = scatter0(QG)
    c_middle(0, 1)
    c_middle(2, 3)
    r_mlp = scatter1(MLP, r_mlp)
    r_down = scatter1(DOWN, r_down)
    r_qg = scatter1(QG, r_qg)
    c_finish(GUT)
    kvb()
    gk()
    gv()
    r_kv = scatter0(KV_EARLY, stage(7, RB1.at[:, :, :, :, columns(KV)]))
    r_mlp = scatter2(MLP, r_mlp)
    pn1()
    pn2()
    r_out = scatter1(OUT, r_out)
    r_down = scatter2(DOWN, r_down)
    ln1b()
    r_vec = scatter0(KV_LATE, r_kv[1])
    r_kv = scatter1(KV_EARLY, r_kv)
    scatter1(KV_LATE, r_vec)
    r_qg = scatter2(QG, r_qg)
    r_down = scatter3(DOWN, r_down)
    r_mlp = scatter3(MLP, r_mlp)
    r_out = scatter2(OUT, r_out)
    r_qg = scatter3(QG, r_qg)
    r_kv = scatter2(KV, r_kv)
    r_out = scatter3(OUT, r_out)
    r_kv = scatter3(KV, r_kv)
    r_down = scatter4(DOWN, r_down)
    r_qg = scatter4(QG, r_qg)
    r_mlp = scatter4(MLP, r_mlp)
    r_kv = scatter4(KV, r_kv)
    r_out = scatter4(OUT, r_out)
    f_qg = scatter5(QG, r_qg, 3)
    f_down = scatter5(DOWN, r_down, 0)
    f_mlp = scatter5(MLP, r_mlp, 1)
    f_kv = scatter5(KV, r_kv, 4)
    f_out = scatter5(OUT, r_out, 2)
    f_qg = finish(f_qg, CQ, CG)
    f_down = finish(f_down, CMD)
    f_mlp = finish(f_mlp, CMG, CMU)
    f_kv = finish(f_kv, CK, CV, VTILE)
    f_out = finish(f_out, CO)
    c_sent()
    put_out.wait()
    put_gin.wait()
    most = pl.ds(CQ, TOTAL - CQ)
    sent = (
        W.at[0, 0, 0:3], W.at[0, 0:3, :, :, 0:CQ], W.at[0, 0:2, :, :, most], W.at[0, 0, :, :, most], W.at[0:2], W.at[0],
        RA, RB1, R2C, R2A.at[:, :, :, most], R2B.at[:, :, :, most], R3,
    )
    for kind, total in enumerate(sent):
        remote(total, total, way_s.at[kind], way_r.at[0], sibling).wait_send()
    for copy in (e_first, e_rest, e_x, e_g, e_sec, e_norm):
        copy.wait_send()
    remote(FSEND, FRECV, ex_s.at[7], ex_r.at[9], sibling).wait_send()
    for ref, at in ((OUT8, 8), (OUTVEC, 9), (OUTW, 10)):
        pltpu.make_async_copy(ref, ref, loc.at[at]).wait()


def hand_over(*refs):
    vec, results, smalls, outs, rows, held = refs[0], refs[1:11], refs[11:15], refs[15:25], refs[25], refs[26:36]
    sems = refs[36]
    fetch = [pltpu.make_async_copy(a, b, sems.at[i]) for i, (a, b) in enumerate(zip(results, held))]
    write = [pltpu.make_async_copy(a, b, sems.at[10 + i]) for i, (a, b) in enumerate(zip(held, outs))]
    last = pltpu.make_async_copy(vec, rows, sems.at[20])
    for copy in fetch:
        copy.start()
    last.start()
    for a, b in zip(fetch, write):
        a.wait()
        b.start()
    last.wait()
    for i, ref in enumerate(smalls):
        ref[...] = rows[i : i + 1, 0:8]
    for copy in write:
        copy.wait()


def scratch():
    def b(*shape):
        return pltpu.VMEM(shape, BF16)

    def f(*shape):
        return pltpu.VMEM(shape, F32)

    def sem(n):
        return pltpu.SemaphoreType.DMA((n,))

    return [
        b(4, 4, 4, 16, TOTAL), b(4, 4, 4, 16, TOTAL), b(2, 2, 4, 16, TOTAL), b(2, 4, 4, 16, TOTAL),
        b(2, 2, 16, TOTAL), b(2, 4, 16, TOTAL), b(3, 4, 16, CQ), b(3, 16, TOTAL),
        b(256, 1024), b(256, 1024), f(8, 1792), b(2, 8, 1024), b(6, 8, 1728), f(8, 128), f(2, 8, 1024), f(6, 8, 1728), f(8, 128),
        b(2, 128, 1024), b(16, TOTAL), b(2, 16, TOTAL), f(8, 1024), f(8, 1024),
        f(256, 128), f(256, 128), f(4, 256, 128),
        b(256, 1024), b(1024, 256), b(1024, 256), b(256, 512), b(256, 512), b(256, 512), b(256, 512),
        b(256, WIDE), b(256, WIDE), f(256, WIDE), b(2, 256, 256), f(2, 256, 256), f(256, WIDE), f(256, WIDE),
        b(REAL, 256), b(REAL, 256), b(3, REAL, 256), b(WIDE, 256), b(WIDE, 256),
        b(256, WIDE), f(256, 1024), b(256, 1024), b(256, 1024), b(128, 1024), b(128, 1024), f(128, 1024),
        b(256, 1024), b(128, 1024), f(128, 1024),
        b(256, 1024), f(256, WIDE), f(256, WIDE), b(256, WIDE), b(256, WIDE), b(256, WIDE),
        f(256, 1024), b(256, WIDE), b(256, 512), b(256, 512), b(256, WIDE),
        f(8, TOTAL), f(8, TOTAL), f(8, TOTAL),
        sem(12), sem(46), sem(4), sem(16), sem(9), sem(14), sem(11),
    ]


def per_device(
    inputs, cotangent, ln1_gain, ln1_bias, w_query, w_key, w_value, w_gate, w_out,
    ln2_gain, ln2_bias, w_mlp_gate, w_mlp_up, w_mlp_down,
):
    cosine, sine = tables()
    anywhere = pl.BlockSpec(memory_space=pl.ANY)
    here = pl.BlockSpec(memory_space=pltpu.VMEM)
    tokens = jax.ShapeDtypeStruct((128, 1024), BF16)
    square = jax.ShapeDtypeStruct((8, 1024), F32)
    wide = jax.ShapeDtypeStruct((8, 1728), F32)
    small = jax.ShapeDtypeStruct((1, 8), F32)
    results = [tokens] * 2 + [square] * 2 + [wide] * 6
    vectors = (ln1_gain, ln1_bias, ln2_gain, ln2_bias)
    out, gin, vec, *grads = pl.pallas_call(
        kernel,
        out_shape=results[:2] + [jax.ShapeDtypeStruct((8, 128), F32)] + results[2:],
        in_specs=[here] * 4 + [anywhere] * 12,
        out_specs=[anywhere] * 11,
        scratch_shapes=scratch(),
        compiler_params=pltpu.CompilerParams(
            collective_id=0, has_side_effects=True, vmem_limit_bytes=64 << 20
        ),
        name="block",
    )(
        *(v.reshape(1, 8) for v in vectors), inputs[0], cotangent[0], w_query, w_key, w_value, w_gate, w_out.T,
        w_mlp_gate, w_mlp_up, w_mlp_down.T, jnp.asarray(cosine), jnp.asarray(sine),
    )
    *smalls, out, gin, gq, gk, gv, gg, go, gmg, gmu, gmd = pl.pallas_call(
        hand_over,
        out_shape=[small] * 4 + results,
        in_specs=[anywhere] * 11,
        out_specs=[here] * 4 + [anywhere] * 10,
        scratch_shapes=[pltpu.VMEM((8, 128), F32)]
        + [pltpu.VMEM(r.shape, r.dtype) for r in results]
        + [pltpu.SemaphoreType.DMA((21,))],
        compiler_params=pltpu.CompilerParams(vmem_limit_bytes=64 << 20),
        name="hand_over",
    )(vec, out, gin, *grads)
    a, b, c, d = (v.reshape(8) for v in smalls)
    return out[None], gin[None], a, b, gq, gk, gv, gg, go.T, c, d, gmg, gmu, gmd.T


def solution(mesh):
    both = ("dp", "seq")
    row, col, vec, tokens = P(both, None), P(None, both), P(both), P("dp", "seq", None)
    return jax.shard_map(
        per_device,
        mesh=mesh,
        in_specs=(tokens, tokens, vec, vec, row, row, row, row, col, vec, vec, row, row, col),
        out_specs=(tokens, tokens, vec, vec, row, row, row, row, col, vec, vec, row, row, col),
        check_vma=False,
    )
```

```python
import functools

import jax
import jax.numpy as jnp
import numpy as np
from jax import lax
from jax.experimental import pallas as pl
from jax.experimental.pallas import tpu as pltpu
from jax.sharding import PartitionSpec as P

MESH = pl.DeviceIdType.MESH
F32 = jnp.float32
BF16 = jnp.bfloat16
EPS = 1e-05
VH = 432

CK, CV, CQ, CG, CO, CMG, CMU, CMD, TOTAL = 0, 512, 1408, 1920, 2816, 3712, 4608, 5504, 6400
WIDE = 896
REAL = 864
VTILE = CV + 768


def cut(start, *tiles):
    parts = []
    for part, n in enumerate(tiles):
        parts.append((part, start, 128 * n))
        start += 128 * n
    return tuple(parts)


GATHERS = (
    cut(CK, 4, 4, 3), cut(CQ, 4, 2, 5), cut(CO, 3, 1, 3), cut(CMG, 5, 4, 5), cut(CMD, 3, 3, 1),
)
KV = cut(CK, 4, 4, 3)
KV_EARLY, KV_LATE = cut(CK, 4, 4, 2), ((2, VTILE, 128),)
QG, OUT, MLP, DOWN = cut(CQ, 4, 1, 6), cut(CO, 3, 2, 2), cut(CMG, 6, 3, 5), cut(CMD, 2, 3, 2)
FORWARD_GATHERS = (1, 2, 3, 4,)
PIECES = ((slice(0, 224), 0), (slice(224, 432), 0), (slice(432, 656), 1), (slice(656, 864), 1))
ORDERS = (("x", "y", "z"), ("y", "z", "x"), ("z", "x", "y"))
ZYX = ("z", "y", "x")


def tables():
    half = 128
    inverse = np.power(10000.0, -np.arange(half, dtype=np.float64) / half)
    angles = np.arange(1024, dtype=np.float64)[:, None] * inverse[None, :]
    return (
        np.cos(angles).astype(np.float32).reshape(4, 256, half),
        np.sin(angles).astype(np.float32).reshape(4, 256, half),
    )


def mm(a, b):
    return lax.dot_general(a, b, (((1,), (0,)), ((), ())), preferred_element_type=F32)


def mm_nt(a, b):
    return lax.dot_general(a, b, (((1,), (1,)), ((), ())), preferred_element_type=F32)


def loop(n, body):
    def step(i, carry):
        body(i)
        return carry

    lax.fori_loop(0, n, step, 0)


def each(n, body):
    for i in range(n):
        body(i)


def kernel(
    gain1_in, bias1_in, gain2_in, bias2_in, x_in, g_in, wq_in, wk_in, wv_in, wg_in, wo_in, wmg_in, wmu_in, wmd_in,
    cos_in, sin_in, out_ref, gin_ref, OUTVEC, gq_ref, gk_ref, gv_ref, gg_ref, go_ref, gmg_ref, gmu_ref, gmd_ref,
    *scratch,
):
    (
        W, Gd, RA, RB1, R2A, R2B, R2C, R3, X, G, WS, IN8, INW, INV, PSEND, PRECV, VEC, VA, COS, SIN, STAT,
        NORM, NORMT, TT, Q, QS, K, KW, V, GGP, GATE, WT, MIX, GRP,
        UT, TOT, STATES, CT, GUT, GATED, MID, SB, RB, SBO, RBO, OWN1, RB2, RB3,
        SEC, ACT, BCT, HID, GGL, GUL, GM, GMX, GQ, GK, GV, FSEND, FRECV, KEEP,
        way_s, way_r, st_s, st_r, ex_s, ex_r, loc,
    ) = scratch
    S1, S2, VT, RSTD, GML = RB1.at[0], R2B.at[0], TT.at[0:WIDE], MIX, SEC
    dp = lax.axis_index("dp")
    sq = lax.axis_index("seq")
    me = {"z": dp // 4, "y": dp % 4, "x": sq // 2}
    c = sq % 2
    c0 = (c == 0).astype(F32)
    c1 = (c == 1).astype(F32)

    def shifted(axis, k):
        p = dict(me)
        p[axis] = (me[axis] + k) % 4
        return p

    def device(p, core):
        return (p["z"] * 4 + p["y"], p["x"] * 2 + core)

    sibling = device(me, 1 - c)

    def remote(src, dst, ss, rs, dev):
        return pltpu.make_async_remote_copy(
            src_ref=src, dst_ref=dst, send_sem=ss, recv_sem=rs, device_id=dev, device_id_type=MESH
        )

    rows_own = pl.ds(pl.multiple_of(c * 128, 128), 128)
    rows_sib = pl.ds(pl.multiple_of((1 - c) * 128, 128), 128)
    fetch = [
        pltpu.make_async_copy(src, dst, loc.at[i])
        for src, dst, i in (
            (wq_in, IN8.at[0], 0), (wk_in, IN8.at[1], 0), (wv_in, INW.at[0], 1), (wg_in, INW.at[1], 1),
            (wo_in, INW.at[2], 1), (wmg_in, INW.at[3], 1), (wmu_in, INW.at[4], 1), (wmd_in, INW.at[5], 1),
            (x_in, X.at[rows_own, :], 2), (g_in, G.at[rows_own, :], 3),
            (cos_in.at[me["x"]], COS, 4), (sin_in.at[me["x"]], SIN, 5),
        )
    ]
    for copy in fetch:
        copy.start()
    barrier = pltpu.get_barrier_semaphore()
    pl.semaphore_signal(barrier, inc=1, device_id=sibling, device_id_type=MESH)
    for axis in ZYX:
        for k in (1, 2, 3):
            pl.semaphore_signal(
                barrier, inc=1, device_id=device(shifted(axis, k), c), device_id_type=MESH
            )

    def put(ref, col, own):
        both = jnp.concatenate([own * c0, own * c1], axis=0)
        ref[:, col : col + own.shape[1]] = both.astype(BF16)

    def pack(col, h0, h1):
        put(PRECV.at[0], col, h0 * c0 + h1 * c1)
        put(PSEND, col, h0 * c1 + h1 * c0)

    def pack_square(i, col):
        w = IN8[i].astype(F32)
        pack(col, w[:, :512], w[:, 512:])

    def pack_wide(i, col):
        lane = lax.broadcasted_iota(jnp.int32, (8, WIDE), 1)
        WS[:, 1664:1792] = jnp.zeros((8, 128), F32)
        WS[:, :1728] = INW[i].astype(F32)
        h0 = jnp.where(lane < REAL, WS[:, :WIDE], 0.0)
        h1 = pltpu.roll(WS[:, 768:1792], 1024 - 96, 1)[:, :WIDE]
        h1 = jnp.where(lane < REAL, h1, 0.0)
        if col == CV:
            v = jnp.concatenate([INV[...], jnp.zeros((120, 128), F32)], axis=0).T
            v = pltpu.roll(v[0:8, :], 96, 1)
            v = jnp.concatenate([jnp.zeros((8, 768), F32), v], axis=1)
            h0 = h0 + v
            h1 = h1 + v
        pack(col, h0, h1)

    def exchange(first, last, i):
        s = pl.ds(first, last - first)
        copy = remote(PSEND.at[:, s], PRECV.at[1, :, s], ex_s.at[i], ex_r.at[i], sibling)
        copy.start()
        return copy

    def assemble(copy, first, last):
        copy.wait_recv()
        for col in range(first, last, 640):
            s = pl.ds(col, min(640, last - col))
            W[me["z"], me["y"], me["x"], :, s] = (
                PRECV[0, :, s].astype(F32) + PRECV[1, :, s].astype(F32)
            ).astype(BF16)

    INV[...] = jnp.zeros_like(INV)
    for i, ref in enumerate((gain1_in, bias1_in, gain2_in, bias2_in)):
        INV[i : i + 1, 0:8] = ref[...].astype(F32)
    pltpu.make_async_copy(IN8, IN8, loc.at[0]).wait()
    pltpu.make_async_copy(INW, INW, loc.at[1]).wait()
    pack_square(1, CK)
    pack_wide(0, CV)
    pl.semaphore_wait(barrier, 10)
    e_first = exchange(0, CQ, 0)
    pack_square(0, CQ)
    for i, col in enumerate((CG, CO, CMG, CMU, CMD)):
        pack_wide(i + 1, col)
    e_rest = exchange(CQ, TOTAL, 8)
    fetch[8].wait()
    e_x = remote(X.at[rows_own, :], X.at[rows_own, :], ex_s.at[1], ex_r.at[1], sibling)
    e_x.start()
    fetch[9].wait()
    e_g = remote(G.at[rows_own, :], G.at[rows_own, :], ex_s.at[2], ex_r.at[2], sibling)
    e_g.start()

    count = [0]

    def stage(kind, total):
        count[0] += 1
        return way_s.at[kind], way_r.at[count[0] - 1], total

    def send(where, src, dst, dev):
        remote(src, dst, where[0], where[1], dev).start()

    def arrived(where):
        ss, rs, total = where
        remote(total, total, ss, rs, sibling).wait_recv()

    def columns(parts):
        return pl.ds(parts[0][1], sum(n for _, _, n in parts))

    def gather(group, phase, forward=False):
        s = columns(GATHERS[group])
        halves = phase == 2 or (phase == 1 and group in FORWARD_GATHERS)
        if phase == 1:
            where = stage(3 if forward else 2 if halves else 1, W.at[0, 0 : 1 if forward else 2 if halves else 3, :, :, s])
        else:
            where = stage(5, W.at[0, :, :, :, s]) if forward else stage(4, W.at[0:2, :, :, :, s])
        gather_parts(where, GATHERS[group], phase, halves, forward)
        return where

    def gather_parts(where, parts, phase, halves, forward):
        for part, col, n in parts:
            order = ORDERS[part]
            axis = order[phase]
            for i, k in enumerate((1, 3) if halves else (1, 2, 3)):
                idx = {a: me[a] for a in ZYX}
                for a in order[:phase]:
                    idx[a] = slice(None)
                if forward:
                    idx[axis] = (me[axis] - k) % 4
                    idx[[a for a in ZYX if a in order[:phase]][0]] = pl.ds(2 * i, 2)
                src = W.at[tuple(idx[a] for a in ZYX) + (slice(None), pl.ds(col, n))]
                send(where, src, src, device(shifted(axis, k), c))

    def early_third(g):
        p4[g] = stage(4, W.at[0:2, :, :, :, columns(GATHERS[g])])
        for part, col, n in GATHERS[g]:
            a, b, axis = ORDERS[part]
            idx = {a: slice(None), b: me[b], axis: me[axis]}
            src = W.at[tuple(idx[q] for q in ZYX) + (slice(None), pl.ds(col, n))]
            for k in (1, 3):
                send(p4[g], src, src, device(shifted(axis, k), c))

    def late_third(g):
        for part, col, n in GATHERS[g]:
            a, b, axis = ORDERS[part]
            for j in (1, 2, 3):
                idx = {a: slice(None), b: (me[b] + j) % 4, axis: me[axis]}
                src = W.at[tuple(idx[q] for q in ZYX) + (slice(None), pl.ds(col, n))]
                for k in (1, 3):
                    send(p4[g], src, src, device(shifted(axis, k), c))

    def first_phase(groups, first, last):
        where = stage(0, W.at[0, 0, 0:3, :, first:last])
        for g in groups:
            gather_parts(where, GATHERS[g], 0, False, False)
        return where

    assemble(e_first, 0, CQ)
    p1 = {0: first_phase((0,), 0, CQ)}
    assemble(e_rest, CQ, TOTAL)
    p1[1] = first_phase((1, 2, 3, 4), CQ, TOTAL)
    p2, p3, p4, p5 = {}, {}, {}, {}
    waited = []

    def w1(g):
        at = min(g, 1)
        if at not in waited:
            waited.append(at)
            arrived(p1[at])
        p2[g] = gather(g, 1)

    def w2(g):
        if g in FORWARD_GATHERS:
            arrived(p2[g])
            p3[g] = gather(g, 1, True)

    def w3(g):
        arrived(p3[g] if g in FORWARD_GATHERS else p2[g])
        late_third(g)

    def w4(g):
        arrived(p4[g])
        p5[g] = gather(g, 2, True)

    def w5(g):
        arrived(p5[g])

    def wcols(col, n):
        return W[:, :, :, :, col : col + n].reshape(1024, n)

    def wrows(i, col, n):
        return W[i, :, :, :, col : col + n].reshape(256, n)

    def fwd(a, col, n, emit):
        for at in range(0, n, 256):
            w = min(256, n - at)
            emit(at, w, mm(a[...], wcols(col + at, w)))

    def grad(at, b, col):
        n = b.shape[1]

        def body(i):
            r = mm(at[pl.ds(i * 256, 256), :], b[...])
            Gd[i, :, :, :, col : col + n] = r.astype(BF16).reshape(4, 4, 16, n)

        each(4, body)

    def rows(i, n=64):
        return pl.ds(pl.multiple_of(i * n, n), n)

    lanes = lax.broadcasted_iota(jnp.int32, (64, WIDE), 1)
    in0 = lanes < VH
    in1 = (lanes >= VH) & (lanes < REAL)
    real = lanes < REAL

    def log_gamma(hh):
        g0 = float(np.log(1.0 - 2.0 ** (-5.0 - hh)))
        g1 = float(np.log(1.0 - 2.0 ** (-7.0 - hh)))
        return jnp.where(c == 0, jnp.float32(g0), jnp.float32(g1))

    lg = [log_gamma(0), log_gamma(1)]

    def mask(hh):
        d = (
            lax.broadcasted_iota(jnp.int32, (256, 256), 0) - lax.broadcasted_iota(jnp.int32, (256, 256), 1)
        ).astype(F32)
        return jnp.where(d >= 0, jnp.exp(jnp.maximum(d, 0.0) * lg[hh]), 0.0)

    VA[...] = jnp.zeros_like(VA)
    e_x.wait_recv()
    e_g.wait_recv()

    def norm(v):
        mean = jnp.mean(v, axis=-1, keepdims=True)
        center = v - mean
        spread = jnp.mean(center * center, axis=-1, keepdims=True)
        rstd = lax.rsqrt(spread + EPS)
        return center * rstd, rstd, mean

    def ln1_stats(i):
        xh, rstd, mean = norm(X[rows(i), :].astype(F32))
        GM[rows(i), :] = xh
        STAT[0, rows(i), :] = jnp.broadcast_to(mean, (64, 128))
        STAT[1, rows(i), :] = jnp.broadcast_to(rstd, (64, 128))

    loop(4, ln1_stats)
    fetch[10].wait()
    fetch[11].wait()

    def transpose(src, dst):
        dst[...] = src[...].T

    def vector(i):
        return VEC[i : i + 1, :]

    def ln1():
        VEC[...] = wcols(VTILE, 128).astype(F32).T[96:104, :]
        gain1, bias1 = vector(0), vector(1)

        def ln1(i):
            NORM[rows(i), :] = (GM[rows(i), :] * gain1 + bias1).astype(BF16)

        loop(4, ln1)

    def rotated(dst, dst2, offset, sign, scale):
        def emit(at, w, r):
            hh = at // 256
            u, z = r[:, :128], r[:, 128:]
            co, si = COS[...], SIN[...]
            a0 = ((u * co - z * si) * scale).astype(BF16)
            a1 = ((u * si + z * co) * scale).astype(BF16)
            spot = lax.broadcasted_iota(jnp.int32, (256, 128), 0).astype(F32)
            sc = jnp.exp((spot * sign + offset) * lg[hh])
            dst[:, at : at + 128] = a0
            dst[:, at + 128 : at + 256] = a1
            dst2[:, at : at + 128] = (a0.astype(F32) * sc).astype(BF16)
            dst2[:, at + 128 : at + 256] = (a1.astype(F32) * sc).astype(BF16)

        return emit

    def emit_v(at, w, r):
        col = lax.broadcasted_iota(jnp.int32, (256, w), 1) + at
        V[:, at : at + w] = jnp.where(col < REAL, r, 0.0).astype(BF16)

    def kvu():
        fwd(NORM, CK, 512, rotated(K, KW, 255.0, -1.0, 0.0625))
        fwd(NORM, CV, WIDE, emit_v)
        transpose(V, VT)
        for hh in range(2):
            r = mm(VT[VH * hh : VH * (hh + 1), :], KW[:, 256 * hh : 256 * (hh + 1)])
            UT[VH * hh : VH * (hh + 1), :] = r.astype(BF16)

    def states(src, base, back):
        x = me["x"]
        near = dict(me, x=x + 1 - 2 * (x % 2))
        far = dict(me, x=3 - x)
        low = x < 2
        sends = (x != 0) if back else (x != 3)
        gets = (x != 1) if back else (x != 2)
        passes = ~low if back else low
        steps = []
        for i, (at, hh) in enumerate(PIECES):
            t = base + i
            slot = 1 if back else 0
            one = remote(src.at[at], STATES.at[slot, at], st_s.at[base // 4], st_r.at[t], device(near, c))
            pl.when(sends)(one.start)
            steps.append(one)

        def second(i):
            at, hh = PIECES[i]
            t = base + 4 + i
            two = remote(TOT.at[at], STATES.at[2, at], st_s.at[base // 4 + 1], st_r.at[t], device(far, c))

            def total():
                steps[i].wait_recv()
                own = src[at, :].astype(F32)
                got = STATES[slot, at, :].astype(F32)
                g = jnp.exp(256.0 * lg[hh])
                first = (x % 2 == 1) if back else (x % 2 == 0)
                TOT[at, :] = jnp.where(first, own * g + got, own + got * g).astype(BF16)
                two.start()

            pl.when(passes)(total)
            return two

        def finish(dst):
            dst[...] = jnp.zeros_like(dst)
            for i, two in enumerate(twos):
                at, hh = PIECES[i]
                g = jnp.exp(256.0 * lg[hh])

                def single():
                    dst[at, :] = STATES[slot, at, :]

                def double():
                    two.wait_recv()
                    dst[at, :] = STATES[2, at, :]

                def triple():
                    steps[i].wait_recv()
                    two.wait_recv()
                    total = STATES[2, at, :].astype(F32) * g
                    dst[at, :] = (total + STATES[slot, at, :].astype(F32)).astype(BF16)

                one, pair, three = (2, 1, 0) if back else (1, 2, 3)
                pl.when(x == one)(single)
                pl.when(x == pair)(double)
                pl.when(x == three)(triple)

        def sent():
            one = remote(src, src, st_s.at[base // 4], st_r.at[base], sibling)
            two = remote(TOT, TOT, st_s.at[base // 4 + 1], st_r.at[base], sibling)
            pl.when(sends)(one.wait_send)
            pl.when(passes)(two.wait_send)

        twos = []

        def middle(*pieces):
            twos.extend(second(i) for i in pieces)

        return middle, finish, sent

    def join(dst, h0, h1):
        pick = lax.broadcasted_iota(jnp.int32, (256, 128), 1) < VH - 384
        dst[:, 0:384] = h0[:, :384]
        dst[:, 384:512] = jnp.where(pick, h0[:, 384:512], h1[:, :128])
        dst[:, 512:896] = h1[:, 128:512]

    def qi():
        fwd(NORM, CQ, 512, rotated(Q, QS, 1.0, 1.0, 1.0))
        for hh in range(2):
            raw = mm_nt(Q[:, 256 * hh : 256 * (hh + 1)], K[:, 256 * hh : 256 * (hh + 1)])
            WT[hh] = (raw * mask(hh)).astype(BF16)
        join(MIX, mm(WT[0], V[:, 0:512]), mm(WT[1], V[:, 384:896]))

    def emit_gate(at, w, r):
        GATE[:, at : at + w] = r

    def gate():
        fwd(NORM, CG, WIDE, emit_gate)

    def cross():
        join(GRP, mm_nt(QS[:, 0:256], CT[0:512, :]), mm_nt(QS[:, 256:512], CT[384:896, :]))

    def heads_mean(v):
        m0 = jnp.sum(jnp.where(in0, v, 0.0), axis=-1, keepdims=True) * (1.0 / VH)
        m1 = jnp.sum(jnp.where(in1, v, 0.0), axis=-1, keepdims=True) * (1.0 / VH)
        return jnp.where(in0, m0, m1)

    def group_norm(i):
        m = MIX[rows(i), :] + GRP[rows(i), :]
        center = m - heads_mean(m)
        rstd = lax.rsqrt(heads_mean(center * center) + EPS)
        grouped = jnp.where(real, center * rstd, 0.0)
        GRP[rows(i), :] = grouped
        RSTD[rows(i), :] = rstd
        gate = GATE[rows(i), :]
        GATED[rows(i), :] = (gate * jax.nn.sigmoid(gate) * grouped).astype(BF16)

    def gn():
        loop(4, group_norm)

    def out_body(i):
        r = mm_nt(GATED[...], wrows(i, CO, WIDE))
        s = pl.ds(i * 256, 256)
        MID[:, s] = r
        SB[:, s] = r.astype(BF16)
        remote(SB.at[:, s], RB.at[:, s], ex_s.at[3], ex_r.at[3], sibling).start()

    def out():
        each(4, out_body)

    e_mid = remote(SB, RB, ex_s.at[3], ex_r.at[3], sibling)

    def ln2():
        gain2, bias2 = vector(2), vector(3)

        def ln2_rows(i):
            m = X[rows(i), :].astype(F32) + MID[rows(i), :] + RB[rows(i), :].astype(F32)
            MID[rows(i), :] = m
            xh, rstd, mean = norm(m)
            STAT[2, rows(i), :] = jnp.broadcast_to(mean, (64, 128))
            STAT[3, rows(i), :] = jnp.broadcast_to(rstd, (64, 128))
            SEC[rows(i), :] = (xh * gain2 + bias2).astype(BF16)

        e_mid.wait_recv()
        loop(4, ln2_rows)

    def emit_act(at, w, r):
        ACT[:, at : at + w] = r

    def emit_bct(at, w, r):
        BCT[:, at : at + w] = r

    def gelu_rows(i):
        g = ACT[rows(i), :]
        u = BCT[rows(i), :]
        cdf = 0.5 * (1.0 + lax.erf(g * 0.7071067811865476))
        ge = g * cdf
        HID[rows(i), :] = (ge * u).astype(BF16)
        BCT[rows(i), :] = ge
        ACT[rows(i), :] = (cdf + g * jnp.exp(-0.5 * g * g) * 0.3989422804014327) * u

    def mlp():
        fwd(SEC, CMG, WIDE, emit_act)
        fwd(SEC, CMU, WIDE, emit_bct)

    def gelu():
        loop(4, gelu_rows)

    def place(axes, where):
        return tuple(where.get(a, slice(None)) for a in axes)

    def others(part, phase):
        order = ORDERS[part][::-1]
        return order[phase], [a for a in ZYX if a not in order[: phase + 1]], [a for a in ZYX if a not in order[:phase]]

    def scatter0(parts, late=None):
        s = columns(parts)
        early = stage(6, RA.at[:, :, :, :, s])
        late = late or stage(7, RB1.at[:, :, :, :, s])
        for where in (early, late):
            for part, col, n in parts:
                axis, rest, left = others(part, 0)
                s = (slice(None), pl.ds(col, n))
                for i, k in enumerate((1, 3)):
                    dev = device(shifted(axis, k), c)
                    if where is early:
                        src = Gd.at[place(left, {axis: (me[axis] + 2) % 4, rest[0]: pl.ds(2 * i, 2)}) + s]
                        send(where, src, RA.at[(i, slice(None), slice(None)) + s], dev)
                    else:
                        near = pl.ds(2 - 2 * i, 2)
                        src = Gd.at[place(left, {axis: (me[axis] + k) % 4, rest[0]: near}) + s]
                        send(where, src, RB1.at[(i, near, slice(None)) + s], dev)
        return early, late

    def scatter1(parts, where):
        early, late = where
        arrived(early)
        for part, col, n in parts:
            axis, rest, left = others(part, 0)
            s = (slice(None), pl.ds(col, n))
            for i, k in enumerate((1, 3)):

                def body(j):
                    own = Gd[place(left, {axis: (me[axis] + k) % 4, rest[0]: 2 * i + j}) + s]
                    at = (i, j, slice(None)) + s
                    RA[at] = (own.astype(F32) + RA[at].astype(F32)).astype(BF16)

                loop(2, body)
                src = RA.at[(i, slice(None), slice(None)) + s]
                dst = RB1.at[(i, pl.ds(2 * i, 2), slice(None)) + s]
                send(late, src, dst, device(shifted(axis, k), c))
        return late

    def scatter2(parts, late):
        arrived(late)
        direct = parts is KV
        if direct:
            early = stage(8, R2C.at[:, :, :, columns(parts)])
        else:
            early, late = stage(9, R2A.at[:, :, :, columns(parts)]), stage(10, R2B.at[:, :, :, columns(parts)])
        for part, col, n in parts:
            axis, rest, left = others(part, 0)
            s = (slice(None), pl.ds(col, n))

            def body(j):
                own = Gd[place(left, {axis: me[axis], rest[0]: j}) + s].astype(F32)
                at = (j, slice(None)) + s
                RB1[(0,) + at] = (own + RB1[(0,) + at].astype(F32) + RB1[(1,) + at].astype(F32)).astype(BF16)

            loop(4, body)
            axis, rest, left = others(part, 1)
            if direct:
                for k in (1, 2, 3):
                    to = shifted(axis, k)
                    src = S1.at[place(left, {axis: to[axis]}) + s]
                    send(early, src, R2C.at[(k - 1, slice(None)) + s], device(to, c))
                continue
            for i, k in enumerate((1, 3)):
                dev = device(shifted(axis, k), c)
                src = S1.at[place(left, {axis: (me[axis] + 2) % 4, rest[0]: pl.ds(2 * i, 2)}) + s]
                send(early, src, R2A.at[(i, slice(None)) + s], dev)
                near = pl.ds(2 - 2 * i, 2)
                src = S1.at[place(left, {axis: (me[axis] + k) % 4, rest[0]: near}) + s]
                send(late, src, R2B.at[(i, near) + s], dev)
        return early, late

    def scatter3(parts, where):
        if parts is KV:
            return where[0]
        early, late = where
        arrived(early)
        for part, col, n in parts:
            axis, rest, left = others(part, 1)
            s = (slice(None), pl.ds(col, n))
            for i, k in enumerate((1, 3)):
                half = pl.ds(2 * i, 2)
                own = S1[place(left, {axis: (me[axis] + k) % 4, rest[0]: half}) + s]
                at = (i, slice(None)) + s
                R2A[at] = (own.astype(F32) + R2A[at].astype(F32)).astype(BF16)
                send(late, R2A.at[at], R2B.at[(i, half) + s], device(shifted(axis, k), c))
        return late

    def scatter4(parts, where):
        arrived(where)
        where = stage(11, R3.at[:, :, columns(parts)])
        came = [R2C.at[k] for k in range(3)] if parts is KV else [R2B.at[k] for k in range(2)]
        for part, col, n in parts:
            axis, rest, left = others(part, 1)
            s = (slice(None), pl.ds(col, n))
            t = S1[place(left, {axis: me[axis]}) + s].astype(F32)
            for ref in came:
                t = t + ref[(slice(None),) + s].astype(F32)
            S2[(slice(None),) + s] = t.astype(BF16)
            axis, rest, left = others(part, 2)
            for k in (1, 2, 3):
                to = shifted(axis, k)
                send(where, S2.at[(to[axis],) + s], R3.at[(k - 1,) + s], device(to, c))
        return where

    def scatter5(parts, where, i):
        arrived(where)
        for part, col, n in parts:
            axis, rest, left = others(part, 2)
            s = (slice(None), pl.ds(col, n))
            t = S2[(me[axis],) + s].astype(F32)
            for k in range(3):
                t = t + R3[(k,) + s].astype(F32)
            KEEP[:, s[1]] = t[0:8, :] * c0 + t[8:16, :] * c1
            FSEND[:, s[1]] = t[0:8, :] * c1 + t[8:16, :] * c0
        s = columns(parts)
        copy = remote(FSEND.at[:, s], FRECV.at[:, s], ex_s.at[7], ex_r.at[9 + i], sibling)
        copy.start()
        return copy

    def halves(col, n):
        keep = KEEP[:, col : col + n]
        got = FRECV[:, col : col + n]
        return keep * c0 + got * c1, keep * c1 + got * c0

    def finish(copy, *cols):
        copy.wait_recv()
        for col in cols:
            if col in (CQ, CK):
                ref = (gq_ref, gk_ref)[(CQ, CK).index(col)]
                lo, hi = halves(col, 512)
                ref[:, :512] = lo
                ref[:, 512:] = hi
            elif col == VTILE:
                lo, hi = halves(col, 128)
                OUTVEC[...] = jnp.concatenate([lo + hi, jnp.zeros((120, 128), F32)], axis=0).T[96:104, :]
            else:
                ref = (gv_ref, gg_ref, go_ref, gmg_ref, gmu_ref, gmd_ref)[(CV, CG, CO, CMG, CMU, CMD).index(col)]
                lo, hi = halves(col, WIDE)
                moved = pltpu.roll(jnp.concatenate([hi, jnp.zeros((8, 128), F32)], axis=1), 96, 1)
                first96 = lax.broadcasted_iota(jnp.int32, (8, 128), 1) < 96
                ref[:, 0:768] = lo[:, 0:768]
                ref[:, 768:896] = jnp.where(first96, lo[:, 768:896], moved[:, 0:128])
                ref[:, 896:1728] = moved[:, 128:960]
        return copy

    def emit_hidden(at, w, r):
        GGL[:, at : at + w] = (r * ACT[:, at : at + w]).astype(BF16)
        GUL[:, at : at + w] = (r * BCT[:, at : at + w]).astype(BF16)

    def gmd():
        transpose(G, TT)
        grad(TT, HID, CMD)

    def gh():
        fwd(G, CMD, WIDE, emit_hidden)

    def second_body(i):
        r = mm_nt(GGL[...], wrows(i, CMG, WIDE)) + mm_nt(GUL[...], wrows(i, CMU, WIDE))
        s = pl.ds(i * 256, 256)
        GM[:, s] = r
        SB[:, s] = r.astype(BF16)
        remote(SB.at[:, s], RB2.at[:, s], ex_s.at[5], ex_r.at[5], sibling).start()

    def gs():
        e_mid.wait_send()
        each(4, second_body)

    e_sec = remote(SB, RB2, ex_s.at[5], ex_r.at[5], sibling)

    def gmg():
        transpose(SEC, TT)
        grad(TT, GGL, CMG)

    def gmu():
        transpose(SEC, TT)
        grad(TT, GUL, CMU)

    def norm_back(gs, v, gain, at, which):
        rstd = STAT[which + 1, at, 0:1]
        xh = (v - STAT[which, at, 0:1]) * rstd
        gx = gs * gain
        m0 = jnp.mean(gx, axis=-1, keepdims=True)
        m1 = jnp.mean(gx * xh, axis=-1, keepdims=True)
        return rstd * (gx - m0 - xh * m1), jnp.sum(gs * xh, axis=0, keepdims=True), jnp.sum(gs, axis=0, keepdims=True)

    def ln2b():
        gain2 = vector(2)

        def ln2_back(i):
            gs = GM[rows(i), :] + RB2[rows(i), :].astype(F32)
            part, ggain, gbias = norm_back(gs, MID[rows(i), :], gain2, rows(i), 2)
            gm = G[rows(i), :].astype(F32) + part
            GM[rows(i), :] = gm
            GML[rows(i), :] = gm.astype(BF16)
            mine = (i // 2 == c).astype(F32)
            VA[2:3, :] += ggain * mine
            VA[3:4, :] += gbias * mine

        e_sec.wait_recv()
        loop(4, ln2_back)

    def gout():
        transpose(GML, TT)
        grad(TT, GATED, CO)

    def emit_gated(at, w, r):
        ACT[:, at : at + w] = r

    def gated():
        fwd(GML, CO, WIDE, emit_gated)

    def group_back(i):
        gr = ACT[rows(i), :]
        z = GATE[rows(i), :]
        sg = jax.nn.sigmoid(z)
        grp = GRP[rows(i), :]
        GGP[rows(i), :] = (gr * (sg * (1.0 + z * (1.0 - sg))) * grp).astype(BF16)
        gg = gr * (z * sg)
        gmx = RSTD[rows(i), :] * (gg - heads_mean(gg) - grp * heads_mean(gg * grp))
        GMX[rows(i), :] = jnp.where(real, gmx, 0.0).astype(BF16)

    def groupb():
        loop(4, group_back)

    def gc():
        transpose(GMX, VT)
        u_sent()
        for hh in range(2):
            r = mm(VT[VH * hh : VH * (hh + 1), :], QS[:, 256 * hh : 256 * (hh + 1)])
            UT[VH * hh : VH * (hh + 1), :] = r.astype(BF16)

    def gg():
        grad(NORMT, GGP, CG)

    def gq():
        grad(NORMT, GQ, CQ)

    wide = lax.broadcasted_iota(jnp.int32, (256, 512), 1)
    windows = (slice(0, 512), slice(384, 896))

    def window(ref, hh):
        a = ref[:, windows[hh]]
        keep = wide < VH if hh == 0 else wide >= VH - 384
        return jnp.where(keep, a, jnp.zeros_like(a))

    def spots(hh, offset, sign):
        spot = lax.broadcasted_iota(jnp.int32, (256, 128), 0).astype(F32)
        return jnp.exp((spot * sign + offset) * lg[hh])

    def unrotated(dst, src, hh, cross, offset, sign, scale):
        sc = spots(hh, offset, sign)
        co, si = COS[...], SIN[...]
        a, b = slice(256 * hh, 256 * hh + 128), slice(256 * hh + 128, 256 * hh + 256)
        u = (src[:, a] + cross[:, :128] * sc) * scale
        z = (src[:, b] + cross[:, 128:] * sc) * scale
        dst[:, a] = (u * co + z * si).astype(BF16)
        dst[:, b] = (z * co - u * si).astype(BF16)

    def intra():
        gvi = []
        for hh in range(2):
            h = slice(256 * hh, 256 * (hh + 1))
            gm = window(GMX, hh)
            vw = V[:, windows[hh]]
            graw = (mm_nt(gm, vw) * mask(hh)).astype(BF16)
            ACT[:, h] = mm(graw, K[:, h])
            BCT[:, h] = mm(graw.T, Q[:, h])
            gvi.append(mm(WT[hh].T, gm))
            unrotated(GQ, ACT, hh, mm(gm, CT[windows[hh], :]), 1.0, 1.0, 1.0)
        join(MIX, gvi[0], gvi[1])

    def down_body(i):
        r = mm_nt(HID[...], wrows(i, CMD, WIDE))
        s = pl.ds(i * 256, 256)
        OWN1[:, s] = r[0:128] * c0 + r[128:256] * c1
        SBO[:, s] = (r[0:128] * c1 + r[128:256] * c0).astype(BF16)

    e_out = remote(SBO, RBO, ex_s.at[4], ex_r.at[4], sibling)
    def down():
        each(4, down_body)
        e_out.start()

    def normed_first(i):
        r = mm_nt(GQ[...], wrows(i, CQ, 512)) + mm_nt(GGP[...], wrows(i, CG, WIDE))
        MID[:, pl.ds(i * 256, 256)] = r

    def pn1():
        e_out.wait_recv()
        out_ref[...] = (MID[rows_own, :] + OWN1[...] + RBO[...].astype(F32)).astype(BF16)
        each(4, normed_first)

    def kvb():
        gvs = []
        for hh in range(2):
            h = slice(256 * hh, 256 * (hh + 1))
            unrotated(GK, BCT, hh, mm(window(V, hh), GUT[windows[hh], :]), 255.0, -1.0, 0.0625)
            gvs.append(mm_nt(KW[:, h], GUT[windows[hh], :]))
        join(ACT, gvs[0], gvs[1])
        GV[...] = (MIX[...] + ACT[...]).astype(BF16)

    def gk():
        grad(NORMT, GK, CK)

    def gv():
        grad(NORMT, GV, CV)

    def normed_body(i):
        s = pl.ds(i * 256, 256)
        r = MID[:, s] + mm_nt(GK[...], wrows(i, CK, 512)) + mm_nt(GV[...], wrows(i, CV, WIDE))
        OWN1[:, s] = r[0:128] * c0 + r[128:256] * c1
        SBO[:, s] = (r[0:128] * c1 + r[128:256] * c0).astype(BF16)
        remote(SBO.at[:, s], RB3.at[:, s], ex_s.at[6], ex_r.at[6], sibling).start()

    def pn2():
        e_out.wait_send()
        each(4, normed_body)

    e_norm = remote(SBO, RB3, ex_s.at[6], ex_r.at[6], sibling)

    def ln1b():
        gain1 = vector(0)

        def ln1_back(i):
            at = pl.ds(pl.multiple_of(c * 128 + i * 64, 64), 64)
            gs = OWN1[rows(i), :] + RB3[rows(i), :].astype(F32)
            part, ggain, gbias = norm_back(gs, X[at, :].astype(F32), gain1, at, 0)
            gin_ref[rows(i), :] = (GM[at, :] + part).astype(BF16)
            VA[0:1, :] += ggain
            VA[1:2, :] += gbias

        e_norm.wait_recv()
        loop(2, ln1_back)
        vectors = jnp.concatenate([jnp.zeros((96, 1024), F32), VA[...], jnp.zeros((24, 1024), F32)], axis=0).T
        tile = slice(VTILE, VTILE + 128)
        Gd[:, :, :, :, tile] = (
            Gd[:, :, :, :, tile].astype(F32) + vectors.reshape(4, 4, 4, 16, 128)
        ).astype(BF16)

    w1(0)
    w1(1)
    w1(3)
    w1(2)
    early_third(0)
    w3(0)
    w2(1)
    w2(2)
    w1(4)
    early_third(3)
    w2(3)
    w4(0)
    early_third(1)
    early_third(4)
    w3(1)
    w5(0)
    ln1()
    w2(4)
    early_third(2)
    w3(2)
    kvu()
    u_middle, u_finish, u_sent = states(UT, 0, False)
    w3(3)
    w4(1)
    u_middle(0, 1, 2, 3)
    w4(2)
    w3(4)
    transpose(NORM, NORMT)
    w4(3)
    u_finish(CT)
    w5(1)
    gate()
    qi()
    w5(2)
    cross()
    gn()
    out()
    w4(4)
    ln2()
    w5(3)
    mlp()
    gelu()
    gmd()
    r_down = scatter0(DOWN)
    w5(4)
    gh()
    gmu()
    gmg()
    r_mlp = scatter0(MLP)
    gs()
    down()
    ln2b()
    gated()
    groupb()
    gc()
    gout()
    c_middle, c_finish, c_sent = states(UT, 8, True)
    r_out = scatter0(OUT)
    gg()
    r_down = scatter1(DOWN, r_down)
    intra()
    gq()
    pn1()
    r_qg = scatter0(QG)
    c_middle(0, 1)
    c_middle(2, 3)
    r_mlp = scatter1(MLP, r_mlp)
    r_out = scatter1(OUT, r_out)
    r_qg = scatter1(QG, r_qg)
    c_finish(GUT)
    kvb()
    gv()
    gk()
    r_kv = scatter0(KV_EARLY, stage(7, RB1.at[:, :, :, :, columns(KV)]))
    pn2()
    r_mlp = scatter2(MLP, r_mlp)
    ln1b()
    r_vec = scatter0(KV_LATE, r_kv[1])
    r_kv = scatter1(KV_EARLY, r_kv)
    scatter1(KV_LATE, r_vec)
    r_qg = scatter2(QG, r_qg)
    r_out = scatter2(OUT, r_out)
    r_down = scatter2(DOWN, r_down)
    r_mlp = scatter3(MLP, r_mlp)
    r_qg = scatter3(QG, r_qg)
    r_kv = scatter2(KV, r_kv)
    r_kv = scatter3(KV, r_kv)
    r_down = scatter3(DOWN, r_down)
    r_out = scatter3(OUT, r_out)
    r_qg = scatter4(QG, r_qg)
    r_mlp = scatter4(MLP, r_mlp)
    r_kv = scatter4(KV, r_kv)
    r_down = scatter4(DOWN, r_down)
    r_out = scatter4(OUT, r_out)
    f_qg = scatter5(QG, r_qg, 3)
    f_kv = scatter5(KV, r_kv, 4)
    f_down = scatter5(DOWN, r_down, 0)
    f_mlp = scatter5(MLP, r_mlp, 1)
    f_out = scatter5(OUT, r_out, 2)
    f_qg = finish(f_qg, CQ, CG)
    f_kv = finish(f_kv, CK, CV, VTILE)
    f_down = finish(f_down, CMD)
    f_mlp = finish(f_mlp, CMG, CMU)
    f_out = finish(f_out, CO)
    c_sent()
    most = pl.ds(CQ, TOTAL - CQ)
    sent = (
        W.at[0, 0, 0:3], W.at[0, 0:3, :, :, 0:CQ], W.at[0, 0:2, :, :, most], W.at[0, 0, :, :, most], W.at[0:2], W.at[0],
        RA, RB1, R2C, R2A.at[:, :, :, most], R2B.at[:, :, :, most], R3,
    )
    for kind, total in enumerate(sent):
        remote(total, total, way_s.at[kind], way_r.at[0], sibling).wait_send()
    for copy in (e_first, e_rest, e_x, e_g, e_sec, e_norm):
        copy.wait_send()
    remote(FSEND, FRECV, ex_s.at[7], ex_r.at[9], sibling).wait_send()


def hand_over(*refs):
    vec, results, smalls, outs, sems = refs[0], refs[1:11], refs[11:15], refs[15:25], refs[25]
    copies = [pltpu.make_async_copy(a, b, sems.at[i]) for i, (a, b) in enumerate(zip(results, outs))]
    for copy in copies:
        copy.start()
    for i, ref in enumerate(smalls):
        ref[...] = vec[i : i + 1, 0:8]
    for copy in copies:
        copy.wait()


def scratch():
    def b(*shape):
        return pltpu.VMEM(shape, BF16)

    def f(*shape):
        return pltpu.VMEM(shape, F32)

    def sem(n):
        return pltpu.SemaphoreType.DMA((n,))

    return [
        b(4, 4, 4, 16, TOTAL), b(4, 4, 4, 16, TOTAL), b(2, 2, 4, 16, TOTAL), b(2, 4, 4, 16, TOTAL),
        b(2, 2, 16, TOTAL), b(2, 4, 16, TOTAL), b(3, 4, 16, CQ), b(3, 16, TOTAL),
        b(256, 1024), b(256, 1024), f(8, 1792), b(2, 8, 1024), b(6, 8, 1728), f(8, 128),
        b(16, TOTAL), b(2, 16, TOTAL), f(8, 1024), f(8, 1024),
        f(256, 128), f(256, 128), f(4, 256, 128),
        b(256, 1024), b(1024, 256), b(1024, 256), b(256, 512), b(256, 512), b(256, 512), b(256, 512),
        b(256, WIDE), b(256, WIDE), f(256, WIDE), b(2, 256, 256), f(256, WIDE), f(256, WIDE),
        b(REAL, 256), b(REAL, 256), b(3, REAL, 256), b(WIDE, 256), b(WIDE, 256),
        b(256, WIDE), f(256, 1024), b(256, 1024), b(256, 1024), b(128, 1024), b(128, 1024), f(128, 1024),
        b(256, 1024), b(128, 1024),
        b(256, 1024), f(256, WIDE), f(256, WIDE), b(256, WIDE), b(256, WIDE), b(256, WIDE),
        f(256, 1024), b(256, WIDE), b(256, 512), b(256, 512), b(256, WIDE),
        f(8, TOTAL), f(8, TOTAL), f(8, TOTAL),
        sem(12), sem(46), sem(4), sem(16), sem(9), sem(14), sem(11),
    ]


def per_device(
    inputs, cotangent, ln1_gain, ln1_bias, w_query, w_key, w_value, w_gate, w_out,
    ln2_gain, ln2_bias, w_mlp_gate, w_mlp_up, w_mlp_down,
):
    cosine, sine = tables()
    anywhere = pl.BlockSpec(memory_space=pl.ANY)
    here = pl.BlockSpec(memory_space=pltpu.VMEM)
    tokens = jax.ShapeDtypeStruct((128, 1024), BF16)
    square = jax.ShapeDtypeStruct((8, 1024), F32)
    wide = jax.ShapeDtypeStruct((8, 1728), F32)
    small = jax.ShapeDtypeStruct((1, 8), F32)
    results = [tokens] * 2 + [square] * 2 + [wide] * 6
    vectors = (ln1_gain, ln1_bias, ln2_gain, ln2_bias)
    out, gin, vec, *grads = pl.pallas_call(
        kernel,
        out_shape=[pltpu.VMEM(r.shape, r.dtype) for r in results[:2] + [jax.ShapeDtypeStruct((8, 128), F32)] + results[2:]],
        in_specs=[here] * 4 + [anywhere] * 12,
        out_specs=[here] * 11,
        scratch_shapes=scratch(),
        compiler_params=pltpu.CompilerParams(
            collective_id=0, has_side_effects=True, vmem_limit_bytes=63 << 20
        ),
        name="block",
    )(
        *(v.reshape(1, 8) for v in vectors), inputs[0], cotangent[0], w_query, w_key, w_value, w_gate, w_out.T,
        w_mlp_gate, w_mlp_up, w_mlp_down.T, jnp.asarray(cosine), jnp.asarray(sine),
    )
    *smalls, out, gin, gq, gk, gv, gg, go, gmg, gmu, gmd = pl.pallas_call(
        hand_over,
        out_shape=[small] * 4 + results,
        in_specs=[here] * 11,
        out_specs=[here] * 4 + [anywhere] * 10,
        scratch_shapes=[pltpu.SemaphoreType.DMA((10,))],
        compiler_params=pltpu.CompilerParams(vmem_limit_bytes=32 << 20),
        name="hand_over",
    )(vec, out, gin, *grads)
    a, b, c, d = (v.reshape(8) for v in smalls)
    return out[None], gin[None], a, b, gq, gk, gv, gg, go.T, c, d, gmg, gmu, gmd.T


def solution(mesh):
    both = ("dp", "seq")
    row, col, vec, tokens = P(both, None), P(None, both), P(both), P("dp", "seq", None)
    return jax.shard_map(
        per_device,
        mesh=mesh,
        in_specs=(tokens, tokens, vec, vec, row, row, row, row, col, vec, vec, row, row, col),
        out_specs=(tokens, tokens, vec, vec, row, row, row, row, col, vec, vec, row, row, col),
        check_vma=False,
    )
```

```python
import functools

import jax
import jax.numpy as jnp
import numpy as np
from jax import lax
from jax.experimental import pallas as pl
from jax.experimental.pallas import tpu as pltpu
from jax.sharding import PartitionSpec as P

MESH = pl.DeviceIdType.MESH
F32 = jnp.float32
BF16 = jnp.bfloat16
EPS = 1e-05
VH = 432

CK, CV, CQ, CG, CO, CMG, CMU, CMD, TOTAL = 0, 512, 1408, 1920, 2816, 3712, 4608, 5504, 6400
WIDE = 896
REAL = 864
VTILE = CV + 768


def cut(start, *tiles):
    parts = []
    for part, n in enumerate(tiles):
        parts.append((part, start, 128 * n))
        start += 128 * n
    return tuple(parts)


GATHERS = (
    cut(CK, 4, 4, 3), cut(CQ, 4, 2, 5), cut(CO, 3, 1, 3), cut(CMG, 5, 4, 5), cut(CMD, 3, 3, 1),
)
KV = cut(CK, 4, 4, 3)
KV_EARLY, KV_LATE = cut(CK, 4, 4, 2), ((2, VTILE, 128),)
QG, OUT, MLP, DOWN = cut(CQ, 4, 1, 6), cut(CO, 3, 2, 2), cut(CMG, 6, 3, 5), cut(CMD, 2, 3, 2)
FORWARD_GATHERS = (1, 2, 3, 4,)
PIECES = ((slice(0, 224), 0), (slice(224, 432), 0), (slice(432, 656), 1), (slice(656, 864), 1))
ORDERS = (("x", "y", "z"), ("y", "z", "x"), ("z", "x", "y"))
ZYX = ("z", "y", "x")


def tables():
    half = 128
    inverse = np.power(10000.0, -np.arange(half, dtype=np.float64) / half)
    angles = np.arange(1024, dtype=np.float64)[:, None] * inverse[None, :]
    return (
        np.cos(angles).astype(np.float32).reshape(4, 256, half),
        np.sin(angles).astype(np.float32).reshape(4, 256, half),
    )


def mm(a, b):
    return lax.dot_general(a, b, (((1,), (0,)), ((), ())), preferred_element_type=F32)


def mm_nt(a, b):
    return lax.dot_general(a, b, (((1,), (1,)), ((), ())), preferred_element_type=F32)


def loop(n, body):
    def step(i, carry):
        body(i)
        return carry

    lax.fori_loop(0, n, step, 0)


def each(n, body):
    for i in range(n):
        body(i)


def kernel(
    gain1_in, bias1_in, gain2_in, bias2_in, x_in, g_in, wq_in, wk_in, wv_in, wg_in, wo_in, wmg_in, wmu_in, wmd_in,
    cos_in, sin_in, out_ref, gin_ref, OUTVEC, gq_ref, gk_ref, gv_ref, gg_ref, go_ref, gmg_ref, gmu_ref, gmd_ref,
    *scratch,
):
    (
        W, Gd, RA, RB1, R2A, R2B, R2C, R3, X, G, WS, IN8, INW, INV, PSEND, PRECV, VEC, VA, COS, SIN, STAT,
        NORM, NORMT, TT, Q, QS, K, KW, V, GGP, GATE, WT, MIX, GRP,
        UT, TOT, STATES, CT, GUT, GATED, MID, SB, RB, SBO, RBO, OWN1, RB2, RB3,
        SEC, ACT, BCT, HID, GGL, GUL, GM, GMX, GQ, GK, GV, FSEND, FRECV, KEEP,
        way_s, way_r, st_s, st_r, ex_s, ex_r, loc,
    ) = scratch
    S1, S2, VT, RSTD, GML = RB1.at[0], R2B.at[0], TT.at[0:WIDE], MIX, SEC
    dp = lax.axis_index("dp")
    sq = lax.axis_index("seq")
    me = {"z": dp // 4, "y": dp % 4, "x": sq // 2}
    c = sq % 2
    c0 = (c == 0).astype(F32)
    c1 = (c == 1).astype(F32)

    def shifted(axis, k):
        p = dict(me)
        p[axis] = (me[axis] + k) % 4
        return p

    def device(p, core):
        return (p["z"] * 4 + p["y"], p["x"] * 2 + core)

    sibling = device(me, 1 - c)

    def remote(src, dst, ss, rs, dev):
        return pltpu.make_async_remote_copy(
            src_ref=src, dst_ref=dst, send_sem=ss, recv_sem=rs, device_id=dev, device_id_type=MESH
        )

    rows_own = pl.ds(pl.multiple_of(c * 128, 128), 128)
    rows_sib = pl.ds(pl.multiple_of((1 - c) * 128, 128), 128)
    fetch = [
        pltpu.make_async_copy(src, dst, loc.at[i])
        for src, dst, i in (
            (wq_in, IN8.at[0], 0), (wk_in, IN8.at[1], 0), (wv_in, INW.at[0], 1), (wg_in, INW.at[1], 1),
            (wo_in, INW.at[2], 1), (wmg_in, INW.at[3], 1), (wmu_in, INW.at[4], 1), (wmd_in, INW.at[5], 1),
            (x_in, X.at[rows_own, :], 2), (g_in, G.at[rows_own, :], 3),
            (cos_in.at[me["x"]], COS, 4), (sin_in.at[me["x"]], SIN, 5),
        )
    ]
    for copy in fetch:
        copy.start()
    barrier = pltpu.get_barrier_semaphore()
    pl.semaphore_signal(barrier, inc=1, device_id=sibling, device_id_type=MESH)
    for axis in ZYX:
        for k in (1, 2, 3):
            pl.semaphore_signal(
                barrier, inc=1, device_id=device(shifted(axis, k), c), device_id_type=MESH
            )

    def put(ref, col, own):
        both = jnp.concatenate([own * c0, own * c1], axis=0)
        ref[:, col : col + own.shape[1]] = both.astype(BF16)

    def pack(col, h0, h1):
        put(PRECV.at[0], col, h0 * c0 + h1 * c1)
        put(PSEND, col, h0 * c1 + h1 * c0)

    def pack_square(i, col):
        w = IN8[i].astype(F32)
        pack(col, w[:, :512], w[:, 512:])

    def pack_wide(i, col):
        lane = lax.broadcasted_iota(jnp.int32, (8, WIDE), 1)
        WS[:, 1664:1792] = jnp.zeros((8, 128), F32)
        WS[:, :1728] = INW[i].astype(F32)
        h0 = jnp.where(lane < REAL, WS[:, :WIDE], 0.0)
        h1 = pltpu.roll(WS[:, 768:1792], 1024 - 96, 1)[:, :WIDE]
        h1 = jnp.where(lane < REAL, h1, 0.0)
        if col == CV:
            v = jnp.concatenate([INV[...], jnp.zeros((120, 128), F32)], axis=0).T
            v = pltpu.roll(v[0:8, :], 96, 1)
            v = jnp.concatenate([jnp.zeros((8, 768), F32), v], axis=1)
            h0 = h0 + v
            h1 = h1 + v
        pack(col, h0, h1)

    def exchange(first, last, i):
        s = pl.ds(first, last - first)
        copy = remote(PSEND.at[:, s], PRECV.at[1, :, s], ex_s.at[i], ex_r.at[i], sibling)
        copy.start()
        return copy

    def assemble(copy, first, last):
        copy.wait_recv()
        for col in range(first, last, 640):
            s = pl.ds(col, min(640, last - col))
            W[me["z"], me["y"], me["x"], :, s] = (
                PRECV[0, :, s].astype(F32) + PRECV[1, :, s].astype(F32)
            ).astype(BF16)

    INV[...] = jnp.zeros_like(INV)
    for i, ref in enumerate((gain1_in, bias1_in, gain2_in, bias2_in)):
        INV[i : i + 1, 0:8] = ref[...].astype(F32)
    pltpu.make_async_copy(IN8, IN8, loc.at[0]).wait()
    pltpu.make_async_copy(INW, INW, loc.at[1]).wait()
    pack_square(1, CK)
    pack_wide(0, CV)
    pl.semaphore_wait(barrier, 10)
    e_first = exchange(0, CQ, 0)
    pack_square(0, CQ)
    for i, col in enumerate((CG, CO, CMG, CMU, CMD)):
        pack_wide(i + 1, col)
    e_rest = exchange(CQ, TOTAL, 8)
    fetch[8].wait()
    e_x = remote(X.at[rows_own, :], X.at[rows_own, :], ex_s.at[1], ex_r.at[1], sibling)
    e_x.start()
    fetch[9].wait()
    e_g = remote(G.at[rows_own, :], G.at[rows_own, :], ex_s.at[2], ex_r.at[2], sibling)
    e_g.start()

    count = [0]

    def stage(kind, total):
        count[0] += 1
        return way_s.at[kind], way_r.at[count[0] - 1], total

    def send(where, src, dst, dev):
        remote(src, dst, where[0], where[1], dev).start()

    def arrived(where):
        ss, rs, total = where
        remote(total, total, ss, rs, sibling).wait_recv()

    def columns(parts):
        return pl.ds(parts[0][1], sum(n for _, _, n in parts))

    def gather(group, phase, forward=False):
        s = columns(GATHERS[group])
        halves = phase == 2 or (phase == 1 and group in FORWARD_GATHERS)
        if phase == 1:
            where = stage(3 if forward else 2 if halves else 1, W.at[0, 0 : 1 if forward else 2 if halves else 3, :, :, s])
        else:
            where = stage(5, W.at[0, :, :, :, s]) if forward else stage(4, W.at[0:2, :, :, :, s])
        gather_parts(where, GATHERS[group], phase, halves, forward)
        return where

    def gather_parts(where, parts, phase, halves, forward):
        for part, col, n in parts:
            order = ORDERS[part]
            axis = order[phase]
            for i, k in enumerate((1, 3) if halves else (1, 2, 3)):
                idx = {a: me[a] for a in ZYX}
                for a in order[:phase]:
                    idx[a] = slice(None)
                if forward:
                    idx[axis] = (me[axis] - k) % 4
                    idx[[a for a in ZYX if a in order[:phase]][0]] = pl.ds(2 * i, 2)
                src = W.at[tuple(idx[a] for a in ZYX) + (slice(None), pl.ds(col, n))]
                send(where, src, src, device(shifted(axis, k), c))

    def early_third(g):
        p4[g] = stage(4, W.at[0:2, :, :, :, columns(GATHERS[g])])
        for part, col, n in GATHERS[g]:
            a, b, axis = ORDERS[part]
            idx = {a: slice(None), b: me[b], axis: me[axis]}
            src = W.at[tuple(idx[q] for q in ZYX) + (slice(None), pl.ds(col, n))]
            for k in (1, 3):
                send(p4[g], src, src, device(shifted(axis, k), c))

    def late_third(g):
        for part, col, n in GATHERS[g]:
            a, b, axis = ORDERS[part]
            for j in (1, 2, 3):
                idx = {a: slice(None), b: (me[b] + j) % 4, axis: me[axis]}
                src = W.at[tuple(idx[q] for q in ZYX) + (slice(None), pl.ds(col, n))]
                for k in (1, 3):
                    send(p4[g], src, src, device(shifted(axis, k), c))

    def first_phase(groups, first, last):
        where = stage(0, W.at[0, 0, 0:3, :, first:last])
        for g in groups:
            gather_parts(where, GATHERS[g], 0, False, False)
        return where

    assemble(e_first, 0, CQ)
    p1 = {0: first_phase((0,), 0, CQ)}
    assemble(e_rest, CQ, TOTAL)
    p1[1] = first_phase((1, 2, 3, 4), CQ, TOTAL)
    p2, p3, p4, p5 = {}, {}, {}, {}
    waited = []

    def w1(g):
        at = min(g, 1)
        if at not in waited:
            waited.append(at)
            arrived(p1[at])
        p2[g] = gather(g, 1)

    def w2(g):
        if g in FORWARD_GATHERS:
            arrived(p2[g])
            p3[g] = gather(g, 1, True)

    def w3(g):
        arrived(p3[g] if g in FORWARD_GATHERS else p2[g])
        late_third(g)

    def w4(g):
        arrived(p4[g])
        p5[g] = gather(g, 2, True)

    def w5(g):
        arrived(p5[g])

    def wcols(col, n):
        return W[:, :, :, :, col : col + n].reshape(1024, n)

    def wrows(i, col, n):
        return W[2 * i : 2 * i + 2, :, :, :, col : col + n].reshape(512, n)

    def fwd(a, col, n, emit):
        for at in range(0, n, 256):
            w = min(256, n - at)
            emit(at, w, mm(a[...], wcols(col + at, w)))

    def grad(at, b, col):
        n = b.shape[1]

        def body(i):
            r = mm(at[pl.ds(i * 256, 256), :], b[...])
            Gd[i, :, :, :, col : col + n] = r.astype(BF16).reshape(4, 4, 16, n)

        each(4, body)

    def rows(i, n=64):
        return pl.ds(pl.multiple_of(i * n, n), n)

    lanes = lax.broadcasted_iota(jnp.int32, (64, WIDE), 1)
    in0 = lanes < VH
    in1 = (lanes >= VH) & (lanes < REAL)
    real = lanes < REAL

    def log_gamma(hh):
        g0 = float(np.log(1.0 - 2.0 ** (-5.0 - hh)))
        g1 = float(np.log(1.0 - 2.0 ** (-7.0 - hh)))
        return jnp.where(c == 0, jnp.float32(g0), jnp.float32(g1))

    lg = [log_gamma(0), log_gamma(1)]

    def mask(hh):
        d = (
            lax.broadcasted_iota(jnp.int32, (256, 256), 0) - lax.broadcasted_iota(jnp.int32, (256, 256), 1)
        ).astype(F32)
        return jnp.where(d >= 0, jnp.exp(jnp.maximum(d, 0.0) * lg[hh]), 0.0)

    VA[...] = jnp.zeros_like(VA)
    e_x.wait_recv()
    e_g.wait_recv()

    def norm(v):
        mean = jnp.mean(v, axis=-1, keepdims=True)
        center = v - mean
        spread = jnp.mean(center * center, axis=-1, keepdims=True)
        rstd = lax.rsqrt(spread + EPS)
        return center * rstd, rstd, mean

    def ln1_stats(i):
        xh, rstd, mean = norm(X[rows(i), :].astype(F32))
        GM[rows(i), :] = xh
        STAT[0, rows(i), :] = jnp.broadcast_to(mean, (64, 128))
        STAT[1, rows(i), :] = jnp.broadcast_to(rstd, (64, 128))

    loop(4, ln1_stats)
    fetch[10].wait()
    fetch[11].wait()

    def transpose(src, dst):
        dst[...] = src[...].T

    def vector(i):
        return VEC[i : i + 1, :]

    def ln1():
        VEC[...] = wcols(VTILE, 128).astype(F32).T[96:104, :]
        gain1, bias1 = vector(0), vector(1)

        def ln1(i):
            NORM[rows(i), :] = (GM[rows(i), :] * gain1 + bias1).astype(BF16)

        loop(4, ln1)

    def rotated(dst, dst2, offset, sign, scale):
        def emit(at, w, r):
            hh = at // 256
            u, z = r[:, :128], r[:, 128:]
            co, si = COS[...], SIN[...]
            a0 = ((u * co - z * si) * scale).astype(BF16)
            a1 = ((u * si + z * co) * scale).astype(BF16)
            spot = lax.broadcasted_iota(jnp.int32, (256, 128), 0).astype(F32)
            sc = jnp.exp((spot * sign + offset) * lg[hh])
            dst[:, at : at + 128] = a0
            dst[:, at + 128 : at + 256] = a1
            dst2[:, at : at + 128] = (a0.astype(F32) * sc).astype(BF16)
            dst2[:, at + 128 : at + 256] = (a1.astype(F32) * sc).astype(BF16)

        return emit

    def emit_v(at, w, r):
        col = lax.broadcasted_iota(jnp.int32, (256, w), 1) + at
        V[:, at : at + w] = jnp.where(col < REAL, r, 0.0).astype(BF16)

    def kvu():
        fwd(NORM, CK, 512, rotated(K, KW, 255.0, -1.0, 0.0625))
        fwd(NORM, CV, WIDE, emit_v)
        transpose(V, VT)
        for hh in range(2):
            r = mm(VT[VH * hh : VH * (hh + 1), :], KW[:, 256 * hh : 256 * (hh + 1)])
            UT[VH * hh : VH * (hh + 1), :] = r.astype(BF16)

    def states(src, base, back):
        x = me["x"]
        near = dict(me, x=x + 1 - 2 * (x % 2))
        far = dict(me, x=3 - x)
        low = x < 2
        sends = (x != 0) if back else (x != 3)
        gets = (x != 1) if back else (x != 2)
        passes = ~low if back else low
        steps = []
        for i, (at, hh) in enumerate(PIECES):
            t = base + i
            slot = 1 if back else 0
            one = remote(src.at[at], STATES.at[slot, at], st_s.at[base // 4], st_r.at[t], device(near, c))
            pl.when(sends)(one.start)
            steps.append(one)

        def second(i):
            at, hh = PIECES[i]
            t = base + 4 + i
            two = remote(TOT.at[at], STATES.at[2, at], st_s.at[base // 4 + 1], st_r.at[t], device(far, c))

            def total():
                steps[i].wait_recv()
                own = src[at, :].astype(F32)
                got = STATES[slot, at, :].astype(F32)
                g = jnp.exp(256.0 * lg[hh])
                first = (x % 2 == 1) if back else (x % 2 == 0)
                TOT[at, :] = jnp.where(first, own * g + got, own + got * g).astype(BF16)
                two.start()

            pl.when(passes)(total)
            return two

        def finish(dst):
            dst[...] = jnp.zeros_like(dst)
            for i, two in enumerate(twos):
                at, hh = PIECES[i]
                g = jnp.exp(256.0 * lg[hh])

                def single():
                    dst[at, :] = STATES[slot, at, :]

                def double():
                    two.wait_recv()
                    dst[at, :] = STATES[2, at, :]

                def triple():
                    steps[i].wait_recv()
                    two.wait_recv()
                    total = STATES[2, at, :].astype(F32) * g
                    dst[at, :] = (total + STATES[slot, at, :].astype(F32)).astype(BF16)

                one, pair, three = (2, 1, 0) if back else (1, 2, 3)
                pl.when(x == one)(single)
                pl.when(x == pair)(double)
                pl.when(x == three)(triple)

        def sent():
            one = remote(src, src, st_s.at[base // 4], st_r.at[base], sibling)
            two = remote(TOT, TOT, st_s.at[base // 4 + 1], st_r.at[base], sibling)
            pl.when(sends)(one.wait_send)
            pl.when(passes)(two.wait_send)

        twos = []

        def middle(*pieces):
            twos.extend(second(i) for i in pieces)

        return middle, finish, sent

    def join(dst, h0, h1):
        pick = lax.broadcasted_iota(jnp.int32, (256, 128), 1) < VH - 384
        dst[:, 0:384] = h0[:, :384]
        dst[:, 384:512] = jnp.where(pick, h0[:, 384:512], h1[:, :128])
        dst[:, 512:896] = h1[:, 128:512]

    def qi():
        fwd(NORM, CQ, 512, rotated(Q, QS, 1.0, 1.0, 1.0))
        for hh in range(2):
            raw = mm_nt(Q[:, 256 * hh : 256 * (hh + 1)], K[:, 256 * hh : 256 * (hh + 1)])
            WT[hh] = (raw * mask(hh)).astype(BF16)
        join(MIX, mm(WT[0], V[:, 0:512]), mm(WT[1], V[:, 384:896]))

    def emit_gate(at, w, r):
        GATE[:, at : at + w] = r

    def gate():
        fwd(NORM, CG, WIDE, emit_gate)

    def cross():
        join(GRP, mm_nt(QS[:, 0:256], CT[0:512, :]), mm_nt(QS[:, 256:512], CT[384:896, :]))

    def heads_mean(v):
        m0 = jnp.sum(jnp.where(in0, v, 0.0), axis=-1, keepdims=True) * (1.0 / VH)
        m1 = jnp.sum(jnp.where(in1, v, 0.0), axis=-1, keepdims=True) * (1.0 / VH)
        return jnp.where(in0, m0, m1)

    def group_norm(i):
        m = MIX[rows(i), :] + GRP[rows(i), :]
        center = m - heads_mean(m)
        rstd = lax.rsqrt(heads_mean(center * center) + EPS)
        grouped = jnp.where(real, center * rstd, 0.0)
        GRP[rows(i), :] = grouped
        RSTD[rows(i), :] = rstd
        gate = GATE[rows(i), :]
        GATED[rows(i), :] = (gate * jax.nn.sigmoid(gate) * grouped).astype(BF16)

    def gn():
        loop(4, group_norm)

    def out_body(i):
        r = mm_nt(GATED[...], wrows(i, CO, WIDE))
        s = pl.ds(i * 512, 512)
        MID[:, s] = r
        SB[:, s] = r.astype(BF16)
        remote(SB.at[:, s], RB.at[:, s], ex_s.at[3], ex_r.at[3], sibling).start()

    def out():
        each(2, out_body)

    e_mid = remote(SB, RB, ex_s.at[3], ex_r.at[3], sibling)

    def ln2():
        gain2, bias2 = vector(2), vector(3)

        def ln2_rows(i):
            m = X[rows(i), :].astype(F32) + MID[rows(i), :] + RB[rows(i), :].astype(F32)
            MID[rows(i), :] = m
            xh, rstd, mean = norm(m)
            STAT[2, rows(i), :] = jnp.broadcast_to(mean, (64, 128))
            STAT[3, rows(i), :] = jnp.broadcast_to(rstd, (64, 128))
            SEC[rows(i), :] = (xh * gain2 + bias2).astype(BF16)

        e_mid.wait_recv()
        loop(4, ln2_rows)

    def emit_act(at, w, r):
        ACT[:, at : at + w] = r

    def emit_bct(at, w, r):
        BCT[:, at : at + w] = r

    def gelu_rows(i):
        g = ACT[rows(i), :]
        u = BCT[rows(i), :]
        cdf = 0.5 * (1.0 + lax.erf(g * 0.7071067811865476))
        ge = g * cdf
        HID[rows(i), :] = (ge * u).astype(BF16)
        BCT[rows(i), :] = ge
        ACT[rows(i), :] = (cdf + g * jnp.exp(-0.5 * g * g) * 0.3989422804014327) * u

    def mlp():
        fwd(SEC, CMG, WIDE, emit_act)
        fwd(SEC, CMU, WIDE, emit_bct)

    def gelu():
        loop(4, gelu_rows)

    def place(axes, where):
        return tuple(where.get(a, slice(None)) for a in axes)

    def others(part, phase):
        order = ORDERS[part][::-1]
        return order[phase], [a for a in ZYX if a not in order[: phase + 1]], [a for a in ZYX if a not in order[:phase]]

    def scatter0(parts, late=None):
        s = columns(parts)
        early = stage(6, RA.at[:, :, :, :, s])
        late = late or stage(7, RB1.at[:, :, :, :, s])
        for where in (early, late):
            for part, col, n in parts:
                axis, rest, left = others(part, 0)
                s = (slice(None), pl.ds(col, n))
                for i, k in enumerate((1, 3)):
                    dev = device(shifted(axis, k), c)
                    if where is early:
                        src = Gd.at[place(left, {axis: (me[axis] + 2) % 4, rest[0]: pl.ds(2 * i, 2)}) + s]
                        send(where, src, RA.at[(i, slice(None), slice(None)) + s], dev)
                    else:
                        near = pl.ds(2 - 2 * i, 2)
                        src = Gd.at[place(left, {axis: (me[axis] + k) % 4, rest[0]: near}) + s]
                        send(where, src, RB1.at[(i, near, slice(None)) + s], dev)
        return early, late

    def scatter1(parts, where):
        early, late = where
        arrived(early)
        for part, col, n in parts:
            axis, rest, left = others(part, 0)
            s = (slice(None), pl.ds(col, n))
            for i, k in enumerate((1, 3)):

                def body(j):
                    own = Gd[place(left, {axis: (me[axis] + k) % 4, rest[0]: 2 * i + j}) + s]
                    at = (i, j, slice(None)) + s
                    RA[at] = (own.astype(F32) + RA[at].astype(F32)).astype(BF16)

                loop(2, body)
                src = RA.at[(i, slice(None), slice(None)) + s]
                dst = RB1.at[(i, pl.ds(2 * i, 2), slice(None)) + s]
                send(late, src, dst, device(shifted(axis, k), c))
        return late

    def scatter2(parts, late):
        arrived(late)
        direct = parts is KV
        if direct:
            early = stage(8, R2C.at[:, :, :, columns(parts)])
        else:
            early, late = stage(9, R2A.at[:, :, :, columns(parts)]), stage(10, R2B.at[:, :, :, columns(parts)])
        for part, col, n in parts:
            axis, rest, left = others(part, 0)
            s = (slice(None), pl.ds(col, n))

            def body(j):
                own = Gd[place(left, {axis: me[axis], rest[0]: j}) + s].astype(F32)
                at = (j, slice(None)) + s
                RB1[(0,) + at] = (own + RB1[(0,) + at].astype(F32) + RB1[(1,) + at].astype(F32)).astype(BF16)

            loop(4, body)
            axis, rest, left = others(part, 1)
            if direct:
                for k in (1, 2, 3):
                    to = shifted(axis, k)
                    src = S1.at[place(left, {axis: to[axis]}) + s]
                    send(early, src, R2C.at[(k - 1, slice(None)) + s], device(to, c))
                continue
            for i, k in enumerate((1, 3)):
                dev = device(shifted(axis, k), c)
                src = S1.at[place(left, {axis: (me[axis] + 2) % 4, rest[0]: pl.ds(2 * i, 2)}) + s]
                send(early, src, R2A.at[(i, slice(None)) + s], dev)
                near = pl.ds(2 - 2 * i, 2)
                src = S1.at[place(left, {axis: (me[axis] + k) % 4, rest[0]: near}) + s]
                send(late, src, R2B.at[(i, near) + s], dev)
        return early, late

    def scatter3(parts, where):
        if parts is KV:
            return where[0]
        early, late = where
        arrived(early)
        for part, col, n in parts:
            axis, rest, left = others(part, 1)
            s = (slice(None), pl.ds(col, n))
            for i, k in enumerate((1, 3)):
                half = pl.ds(2 * i, 2)
                own = S1[place(left, {axis: (me[axis] + k) % 4, rest[0]: half}) + s]
                at = (i, slice(None)) + s
                R2A[at] = (own.astype(F32) + R2A[at].astype(F32)).astype(BF16)
                send(late, R2A.at[at], R2B.at[(i, half) + s], device(shifted(axis, k), c))
        return late

    def scatter4(parts, where):
        arrived(where)
        where = stage(11, R3.at[:, :, columns(parts)])
        came = [R2C.at[k] for k in range(3)] if parts is KV else [R2B.at[k] for k in range(2)]
        for part, col, n in parts:
            axis, rest, left = others(part, 1)
            s = (slice(None), pl.ds(col, n))
            t = S1[place(left, {axis: me[axis]}) + s].astype(F32)
            for ref in came:
                t = t + ref[(slice(None),) + s].astype(F32)
            S2[(slice(None),) + s] = t.astype(BF16)
            axis, rest, left = others(part, 2)
            for k in (1, 2, 3):
                to = shifted(axis, k)
                send(where, S2.at[(to[axis],) + s], R3.at[(k - 1,) + s], device(to, c))
        return where

    def scatter5(parts, where, i):
        arrived(where)
        for part, col, n in parts:
            axis, rest, left = others(part, 2)
            s = (slice(None), pl.ds(col, n))
            t = S2[(me[axis],) + s].astype(F32)
            for k in range(3):
                t = t + R3[(k,) + s].astype(F32)
            KEEP[:, s[1]] = t[0:8, :] * c0 + t[8:16, :] * c1
            FSEND[:, s[1]] = t[0:8, :] * c1 + t[8:16, :] * c0
        s = columns(parts)
        copy = remote(FSEND.at[:, s], FRECV.at[:, s], ex_s.at[7], ex_r.at[9 + i], sibling)
        copy.start()
        return copy

    def halves(col, n):
        keep = KEEP[:, col : col + n]
        got = FRECV[:, col : col + n]
        return keep * c0 + got * c1, keep * c1 + got * c0

    def finish(copy, *cols):
        copy.wait_recv()
        for col in cols:
            if col in (CQ, CK):
                ref = (gq_ref, gk_ref)[(CQ, CK).index(col)]
                lo, hi = halves(col, 512)
                ref[:, :512] = lo
                ref[:, 512:] = hi
            elif col == VTILE:
                lo, hi = halves(col, 128)
                OUTVEC[...] = jnp.concatenate([lo + hi, jnp.zeros((120, 128), F32)], axis=0).T[96:104, :]
            else:
                ref = (gv_ref, gg_ref, go_ref, gmg_ref, gmu_ref, gmd_ref)[(CV, CG, CO, CMG, CMU, CMD).index(col)]
                lo, hi = halves(col, WIDE)
                moved = pltpu.roll(jnp.concatenate([hi, jnp.zeros((8, 128), F32)], axis=1), 96, 1)
                first96 = lax.broadcasted_iota(jnp.int32, (8, 128), 1) < 96
                ref[:, 0:768] = lo[:, 0:768]
                ref[:, 768:896] = jnp.where(first96, lo[:, 768:896], moved[:, 0:128])
                ref[:, 896:1728] = moved[:, 128:960]
        return copy

    def emit_hidden(at, w, r):
        GGL[:, at : at + w] = (r * ACT[:, at : at + w]).astype(BF16)
        GUL[:, at : at + w] = (r * BCT[:, at : at + w]).astype(BF16)

    def gmd():
        transpose(G, TT)
        grad(TT, HID, CMD)

    def gh():
        fwd(G, CMD, WIDE, emit_hidden)

    def second_body(i):
        r = mm_nt(GGL[...], wrows(i, CMG, WIDE)) + mm_nt(GUL[...], wrows(i, CMU, WIDE))
        s = pl.ds(i * 512, 512)
        GM[:, s] = r
        SB[:, s] = r.astype(BF16)
        remote(SB.at[:, s], RB2.at[:, s], ex_s.at[5], ex_r.at[5], sibling).start()

    def gs():
        e_mid.wait_send()
        each(2, second_body)

    e_sec = remote(SB, RB2, ex_s.at[5], ex_r.at[5], sibling)

    def gmg():
        transpose(SEC, TT)
        grad(TT, GGL, CMG)

    def gmu():
        transpose(SEC, TT)
        grad(TT, GUL, CMU)

    def norm_back(gs, v, gain, at, which):
        rstd = STAT[which + 1, at, 0:1]
        xh = (v - STAT[which, at, 0:1]) * rstd
        gx = gs * gain
        m0 = jnp.mean(gx, axis=-1, keepdims=True)
        m1 = jnp.mean(gx * xh, axis=-1, keepdims=True)
        return rstd * (gx - m0 - xh * m1), jnp.sum(gs * xh, axis=0, keepdims=True), jnp.sum(gs, axis=0, keepdims=True)

    def ln2b():
        gain2 = vector(2)

        def ln2_back(i):
            gs = GM[rows(i), :] + RB2[rows(i), :].astype(F32)
            part, ggain, gbias = norm_back(gs, MID[rows(i), :], gain2, rows(i), 2)
            gm = G[rows(i), :].astype(F32) + part
            GM[rows(i), :] = gm
            GML[rows(i), :] = gm.astype(BF16)
            mine = (i // 2 == c).astype(F32)
            VA[2:3, :] += ggain * mine
            VA[3:4, :] += gbias * mine

        e_sec.wait_recv()
        loop(4, ln2_back)

    def gout():
        transpose(GML, TT)
        grad(TT, GATED, CO)

    def emit_gated(at, w, r):
        ACT[:, at : at + w] = r

    def gated():
        fwd(GML, CO, WIDE, emit_gated)

    def group_back(i):
        gr = ACT[rows(i), :]
        z = GATE[rows(i), :]
        sg = jax.nn.sigmoid(z)
        grp = GRP[rows(i), :]
        GGP[rows(i), :] = (gr * (sg * (1.0 + z * (1.0 - sg))) * grp).astype(BF16)
        gg = gr * (z * sg)
        gmx = RSTD[rows(i), :] * (gg - heads_mean(gg) - grp * heads_mean(gg * grp))
        GMX[rows(i), :] = jnp.where(real, gmx, 0.0).astype(BF16)

    def groupb():
        loop(4, group_back)

    def gc():
        transpose(GMX, VT)
        u_sent()
        for hh in range(2):
            r = mm(VT[VH * hh : VH * (hh + 1), :], QS[:, 256 * hh : 256 * (hh + 1)])
            UT[VH * hh : VH * (hh + 1), :] = r.astype(BF16)

    def gg():
        grad(NORMT, GGP, CG)

    def gq():
        grad(NORMT, GQ, CQ)

    wide = lax.broadcasted_iota(jnp.int32, (256, 512), 1)
    windows = (slice(0, 512), slice(384, 896))

    def window(ref, hh):
        a = ref[:, windows[hh]]
        keep = wide < VH if hh == 0 else wide >= VH - 384
        return jnp.where(keep, a, jnp.zeros_like(a))

    def spots(hh, offset, sign):
        spot = lax.broadcasted_iota(jnp.int32, (256, 128), 0).astype(F32)
        return jnp.exp((spot * sign + offset) * lg[hh])

    def unrotated(dst, src, hh, cross, offset, sign, scale):
        sc = spots(hh, offset, sign)
        co, si = COS[...], SIN[...]
        a, b = slice(256 * hh, 256 * hh + 128), slice(256 * hh + 128, 256 * hh + 256)
        u = (src[:, a] + cross[:, :128] * sc) * scale
        z = (src[:, b] + cross[:, 128:] * sc) * scale
        dst[:, a] = (u * co + z * si).astype(BF16)
        dst[:, b] = (z * co - u * si).astype(BF16)

    def intra():
        gvi = []
        for hh in range(2):
            h = slice(256 * hh, 256 * (hh + 1))
            gm = window(GMX, hh)
            vw = V[:, windows[hh]]
            graw = (mm_nt(gm, vw) * mask(hh)).astype(BF16)
            ACT[:, h] = mm(graw, K[:, h])
            BCT[:, h] = mm(graw.T, Q[:, h])
            gvi.append(mm(WT[hh].T, gm))
            unrotated(GQ, ACT, hh, mm(gm, CT[windows[hh], :]), 1.0, 1.0, 1.0)
        join(MIX, gvi[0], gvi[1])

    def down_body(i):
        r = mm_nt(HID[...], wrows(i, CMD, WIDE))
        s = pl.ds(i * 512, 512)
        OWN1[:, s] = r[0:128] * c0 + r[128:256] * c1
        SBO[:, s] = (r[0:128] * c1 + r[128:256] * c0).astype(BF16)

    e_out = remote(SBO, RBO, ex_s.at[4], ex_r.at[4], sibling)
    def down():
        each(2, down_body)
        e_out.start()

    def normed_first(i):
        r = mm_nt(GQ[...], wrows(i, CQ, 512)) + mm_nt(GGP[...], wrows(i, CG, WIDE))
        MID[:, pl.ds(i * 512, 512)] = r

    def pn1():
        e_out.wait_recv()
        out_ref[...] = (MID[rows_own, :] + OWN1[...] + RBO[...].astype(F32)).astype(BF16)
        each(2, normed_first)

    def kvb():
        gvs = []
        for hh in range(2):
            h = slice(256 * hh, 256 * (hh + 1))
            unrotated(GK, BCT, hh, mm(window(V, hh), GUT[windows[hh], :]), 255.0, -1.0, 0.0625)
            gvs.append(mm_nt(KW[:, h], GUT[windows[hh], :]))
        join(ACT, gvs[0], gvs[1])
        GV[...] = (MIX[...] + ACT[...]).astype(BF16)

    def gk():
        grad(NORMT, GK, CK)

    def gv():
        grad(NORMT, GV, CV)

    def normed_body(i):
        s = pl.ds(i * 512, 512)
        r = MID[:, s] + mm_nt(GK[...], wrows(i, CK, 512)) + mm_nt(GV[...], wrows(i, CV, WIDE))
        OWN1[:, s] = r[0:128] * c0 + r[128:256] * c1
        SBO[:, s] = (r[0:128] * c1 + r[128:256] * c0).astype(BF16)
        remote(SBO.at[:, s], RB3.at[:, s], ex_s.at[6], ex_r.at[6], sibling).start()

    def pn2():
        e_out.wait_send()
        each(2, normed_body)

    e_norm = remote(SBO, RB3, ex_s.at[6], ex_r.at[6], sibling)

    def ln1b():
        gain1 = vector(0)

        def ln1_back(i):
            at = pl.ds(pl.multiple_of(c * 128 + i * 64, 64), 64)
            gs = OWN1[rows(i), :] + RB3[rows(i), :].astype(F32)
            part, ggain, gbias = norm_back(gs, X[at, :].astype(F32), gain1, at, 0)
            gin_ref[rows(i), :] = (GM[at, :] + part).astype(BF16)
            VA[0:1, :] += ggain
            VA[1:2, :] += gbias

        e_norm.wait_recv()
        loop(2, ln1_back)
        vectors = jnp.concatenate([jnp.zeros((96, 1024), F32), VA[...], jnp.zeros((24, 1024), F32)], axis=0).T
        tile = slice(VTILE, VTILE + 128)
        Gd[:, :, :, :, tile] = (
            Gd[:, :, :, :, tile].astype(F32) + vectors.reshape(4, 4, 4, 16, 128)
        ).astype(BF16)

    w1(0)
    w1(1)
    w1(3)
    w1(2)
    early_third(0)
    w3(0)
    w2(1)
    w2(2)
    w1(4)
    early_third(3)
    w2(3)
    w4(0)
    early_third(1)
    early_third(4)
    w3(1)
    w5(0)
    ln1()
    w2(4)
    early_third(2)
    w3(2)
    kvu()
    u_middle, u_finish, u_sent = states(UT, 0, False)
    w3(3)
    w4(1)
    u_middle(0, 1, 2, 3)
    w4(2)
    w3(4)
    transpose(NORM, NORMT)
    w4(3)
    u_finish(CT)
    w5(1)
    gate()
    qi()
    w5(2)
    cross()
    gn()
    out()
    w4(4)
    ln2()
    w5(3)
    mlp()
    gelu()
    gmd()
    r_down = scatter0(DOWN)
    w5(4)
    gh()
    gmu()
    gmg()
    r_mlp = scatter0(MLP)
    gs()
    down()
    ln2b()
    gated()
    groupb()
    gc()
    gout()
    c_middle, c_finish, c_sent = states(UT, 8, True)
    r_out = scatter0(OUT)
    gg()
    r_down = scatter1(DOWN, r_down)
    intra()
    gq()
    pn1()
    r_qg = scatter0(QG)
    c_middle(0, 1)
    c_middle(2, 3)
    r_mlp = scatter1(MLP, r_mlp)
    r_out = scatter1(OUT, r_out)
    r_qg = scatter1(QG, r_qg)
    c_finish(GUT)
    kvb()
    gv()
    gk()
    r_kv = scatter0(KV_EARLY, stage(7, RB1.at[:, :, :, :, columns(KV)]))
    pn2()
    r_mlp = scatter2(MLP, r_mlp)
    ln1b()
    r_vec = scatter0(KV_LATE, r_kv[1])
    r_kv = scatter1(KV_EARLY, r_kv)
    scatter1(KV_LATE, r_vec)
    r_qg = scatter2(QG, r_qg)
    r_out = scatter2(OUT, r_out)
    r_down = scatter2(DOWN, r_down)
    r_mlp = scatter3(MLP, r_mlp)
    r_qg = scatter3(QG, r_qg)
    r_kv = scatter2(KV, r_kv)
    r_kv = scatter3(KV, r_kv)
    r_down = scatter3(DOWN, r_down)
    r_out = scatter3(OUT, r_out)
    r_qg = scatter4(QG, r_qg)
    r_mlp = scatter4(MLP, r_mlp)
    r_kv = scatter4(KV, r_kv)
    r_down = scatter4(DOWN, r_down)
    r_out = scatter4(OUT, r_out)
    f_qg = scatter5(QG, r_qg, 3)
    f_kv = scatter5(KV, r_kv, 4)
    f_down = scatter5(DOWN, r_down, 0)
    f_mlp = scatter5(MLP, r_mlp, 1)
    f_out = scatter5(OUT, r_out, 2)
    f_qg = finish(f_qg, CQ, CG)
    f_kv = finish(f_kv, CK, CV, VTILE)
    f_down = finish(f_down, CMD)
    f_mlp = finish(f_mlp, CMG, CMU)
    f_out = finish(f_out, CO)
    c_sent()
    most = pl.ds(CQ, TOTAL - CQ)
    sent = (
        W.at[0, 0, 0:3], W.at[0, 0:3, :, :, 0:CQ], W.at[0, 0:2, :, :, most], W.at[0, 0, :, :, most], W.at[0:2], W.at[0],
        RA, RB1, R2C, R2A.at[:, :, :, most], R2B.at[:, :, :, most], R3,
    )
    for kind, total in enumerate(sent):
        remote(total, total, way_s.at[kind], way_r.at[0], sibling).wait_send()
    for copy in (e_first, e_rest, e_x, e_g, e_sec, e_norm):
        copy.wait_send()
    remote(FSEND, FRECV, ex_s.at[7], ex_r.at[9], sibling).wait_send()


def hand_over(*refs):
    vec, results, smalls, outs, sems = refs[0], refs[1:11], refs[11:15], refs[15:25], refs[25]
    copies = [pltpu.make_async_copy(a, b, sems.at[i]) for i, (a, b) in enumerate(zip(results, outs))]
    for copy in copies:
        copy.start()
    for i, ref in enumerate(smalls):
        ref[...] = vec[i : i + 1, 0:8]
    for copy in copies:
        copy.wait()


def scratch():
    def b(*shape):
        return pltpu.VMEM(shape, BF16)

    def f(*shape):
        return pltpu.VMEM(shape, F32)

    def sem(n):
        return pltpu.SemaphoreType.DMA((n,))

    return [
        b(4, 4, 4, 16, TOTAL), b(4, 4, 4, 16, TOTAL), b(2, 2, 4, 16, TOTAL), b(2, 4, 4, 16, TOTAL),
        b(2, 2, 16, TOTAL), b(2, 4, 16, TOTAL), b(3, 4, 16, CQ), b(3, 16, TOTAL),
        b(256, 1024), b(256, 1024), f(8, 1792), b(2, 8, 1024), b(6, 8, 1728), f(8, 128),
        b(16, TOTAL), b(2, 16, TOTAL), f(8, 1024), f(8, 1024),
        f(256, 128), f(256, 128), f(4, 256, 128),
        b(256, 1024), b(1024, 256), b(1024, 256), b(256, 512), b(256, 512), b(256, 512), b(256, 512),
        b(256, WIDE), b(256, WIDE), f(256, WIDE), b(2, 256, 256), f(256, WIDE), f(256, WIDE),
        b(REAL, 256), b(REAL, 256), b(3, REAL, 256), b(WIDE, 256), b(WIDE, 256),
        b(256, WIDE), f(256, 1024), b(256, 1024), b(256, 1024), b(128, 1024), b(128, 1024), f(128, 1024),
        b(256, 1024), b(128, 1024),
        b(256, 1024), f(256, WIDE), f(256, WIDE), b(256, WIDE), b(256, WIDE), b(256, WIDE),
        f(256, 1024), b(256, WIDE), b(256, 512), b(256, 512), b(256, WIDE),
        f(8, TOTAL), f(8, TOTAL), f(8, TOTAL),
        sem(12), sem(46), sem(4), sem(16), sem(9), sem(14), sem(11),
    ]


def per_device(
    inputs, cotangent, ln1_gain, ln1_bias, w_query, w_key, w_value, w_gate, w_out,
    ln2_gain, ln2_bias, w_mlp_gate, w_mlp_up, w_mlp_down,
):
    cosine, sine = tables()
    anywhere = pl.BlockSpec(memory_space=pl.ANY)
    here = pl.BlockSpec(memory_space=pltpu.VMEM)
    tokens = jax.ShapeDtypeStruct((128, 1024), BF16)
    square = jax.ShapeDtypeStruct((8, 1024), F32)
    wide = jax.ShapeDtypeStruct((8, 1728), F32)
    small = jax.ShapeDtypeStruct((1, 8), F32)
    results = [tokens] * 2 + [square] * 2 + [wide] * 6
    vectors = (ln1_gain, ln1_bias, ln2_gain, ln2_bias)
    out, gin, vec, *grads = pl.pallas_call(
        kernel,
        out_shape=[pltpu.VMEM(r.shape, r.dtype) for r in results[:2] + [jax.ShapeDtypeStruct((8, 128), F32)] + results[2:]],
        in_specs=[here] * 4 + [anywhere] * 12,
        out_specs=[here] * 11,
        scratch_shapes=scratch(),
        compiler_params=pltpu.CompilerParams(
            collective_id=0, has_side_effects=True, vmem_limit_bytes=63 << 20
        ),
        name="block",
    )(
        *(v.reshape(1, 8) for v in vectors), inputs[0], cotangent[0], w_query, w_key, w_value, w_gate, w_out.T,
        w_mlp_gate, w_mlp_up, w_mlp_down.T, jnp.asarray(cosine), jnp.asarray(sine),
    )
    *smalls, out, gin, gq, gk, gv, gg, go, gmg, gmu, gmd = pl.pallas_call(
        hand_over,
        out_shape=[small] * 4 + results,
        in_specs=[here] * 11,
        out_specs=[here] * 4 + [anywhere] * 10,
        scratch_shapes=[pltpu.SemaphoreType.DMA((10,))],
        compiler_params=pltpu.CompilerParams(vmem_limit_bytes=32 << 20),
        name="hand_over",
    )(vec, out, gin, *grads)
    a, b, c, d = (v.reshape(8) for v in smalls)
    return out[None], gin[None], a, b, gq, gk, gv, gg, go.T, c, d, gmg, gmu, gmd.T


def solution(mesh):
    both = ("dp", "seq")
    row, col, vec, tokens = P(both, None), P(None, both), P(both), P("dp", "seq", None)
    return jax.shard_map(
        per_device,
        mesh=mesh,
        in_specs=(tokens, tokens, vec, vec, row, row, row, row, col, vec, vec, row, row, col),
        out_specs=(tokens, tokens, vec, vec, row, row, row, row, col, vec, vec, row, row, col),
        check_vma=False,
    )
```
